32 devices in a mesh: rows: 8 (over z, core), imgs: 4 (over y, x).
Axes of the slice: x: 2, y: 2, z: 4, core: 2. Of those that a mesh axis runs over, the one named last changes fastest.
Arguments:
- features: bfloat16 [32, 32, 32, 512], P('rows', 'imgs'), may hold values from -20 to 20
- cotangent: bfloat16 [32, 32, 32, 512], P('rows', 'imgs'), may hold values from -20 to 20
- norm1_gain: float32 [512], replicated, may hold values from 0.5 to 1.5
- norm1_shift: float32 [512], replicated, may hold values from -1.5 to 1.5
- conv1_kernel: bfloat16 [3, 3, 512, 512], replicated, may hold values from -0.09375 to 0.09375
- conv1_shift: float32 [512], replicated, may hold values from -1.5 to 1.5
- norm2_gain: float32 [512], replicated, may hold values from 0.5 to 1.5
- norm2_shift: float32 [512], replicated, may hold values from -1.5 to 1.5
- conv2_kernel: bfloat16 [3, 3, 512, 512], replicated, may hold values from -0.09375 to 0.09375
- conv2_shift: float32 [512], replicated, may hold values from -1.5 to 1.5
- norm3_gain: float32 [512], replicated, may hold values from 0.5 to 1.5
- norm3_shift: float32 [512], replicated, may hold values from -1.5 to 1.5
- query_weight: bfloat16 [512, 512], replicated, may hold values from -0.25 to 0.25
- query_shift: float32 [512], replicated, may hold values from -2 to 2
- key_weight: bfloat16 [512, 512], replicated, may hold values from -0.25 to 0.25
- value_weight: bfloat16 [512, 512], replicated, may hold values from -0.25 to 0.25
- value_shift: float32 [512], replicated, may hold values from -1.5 to 1.5
- out_weight: bfloat16 [512, 512], replicated, may hold values from -1.5 to 1.5
- out_shift: float32 [512], replicated, may hold values from -1.5 to 1.5
Outputs:
- output: float32 [32, 32, 32, 512], P('rows', 'imgs')
- features_grad: float32 [32, 32, 32, 512], P('rows', 'imgs')
- norm1_gain_grad: float32 [512], replicated
- norm1_shift_grad: float32 [512], replicated
- conv1_kernel_grad: float32 [3, 3, 512, 512], replicated
- conv1_shift_grad: float32 [512], replicated
- norm2_gain_grad: float32 [512], replicated
- norm2_shift_grad: float32 [512], replicated
- conv2_kernel_grad: float32 [3, 3, 512, 512], replicated
- conv2_shift_grad: float32 [512], replicated
- norm3_gain_grad: float32 [512], replicated
- norm3_shift_grad: float32 [512], replicated
- query_weight_grad: float32 [512, 512], replicated
- query_shift_grad: float32 [512], replicated
- key_weight_grad: float32 [512, 512], replicated
- value_weight_grad: float32 [512, 512], replicated
- value_shift_grad: float32 [512], replicated
- out_weight_grad: float32 [512, 512], replicated
- out_shift_grad: float32 [512], replicated
The draws below stay inside these ranges and needn't reach their ends.
All inputs are finite; a program needn't handle non-finite values.
Results may differ from the reference program's by a relative error of at most 0.0154.
The reference program's roundings to bfloat16 on the way count: a program that leaves them out, or rounds other values in their place, can miss the bound.
Values may be sent and summed in bfloat16 or wider, within the bound.
No kernel may reach another device: no remote copies, remote signals or barrier semaphores. Data moves between devices by JAX's collectives and lax.ppermute only.
A program may use at most 256 MiB of HBM per device.

```python
import math
import jax
import jax.numpy as jnp
from jax import lax

C = 512
GROUPS = 32
H = 32
W = 32
IMAGES = 32


def scaled_field(first, second, rising):
    shape = (H, IMAGES, W, C)
    column = jnp.exp(jax.random.uniform(second, (C,), jnp.float32, -0.9, 0.9))
    position = jnp.arange(H, dtype=jnp.float32) / (H - 1)
    base = jnp.clip(jax.random.normal(first, shape, jnp.float32), -4.0, 4.0)
    row_factor = 0.6 * rising ** position
    return base * row_factor[:, None, None, None] * column


def draw_features(key, part):
    key = jax.random.fold_in(key, 11)
    first, second = jax.random.split(key)
    return scaled_field(first, second, 3.0).astype(jnp.bfloat16)


def draw_cotangent(key, part):
    key = jax.random.fold_in(key, 12)
    first, second = jax.random.split(key)
    return scaled_field(first, second, 3.0).astype(jnp.bfloat16)


def scatter_about(rng, extent, width, bound, held_as=jnp.bfloat16):
    return jnp.clip(width * jax.random.normal(rng, extent, jnp.float32), -bound, bound).astype(held_as)


def setup_inputs(seed: int = 0) -> dict:
    key_of = jax.random.split(jax.random.key(seed), 20)
    features = draw_features(jax.random.fold_in(key_of[19], 71), 0)
    cotangent = draw_cotangent(jax.random.fold_in(key_of[19], 71), 0)
    norm1_gain = jnp.clip(1.0 + 0.1 * jax.random.normal(key_of[2], (C,), jnp.float32), 0.5, 1.5)
    norm1_shift = scatter_about(key_of[3], (C,), 0.3, 1.5, jnp.float32)
    conv1_kernel = scatter_about(key_of[4], (3, 3, C, C), (9 * C) ** -0.5, 0.09375)
    conv1_shift = scatter_about(key_of[5], (C,), 0.3, 1.5, jnp.float32)
    norm2_gain = jnp.clip(1.0 + 0.1 * jax.random.normal(key_of[6], (C,), jnp.float32), 0.5, 1.5)
    norm2_shift = scatter_about(key_of[7], (C,), 0.3, 1.5, jnp.float32)
    conv2_kernel = scatter_about(key_of[8], (3, 3, C, C), (9 * C) ** -0.5, 0.09375)
    conv2_shift = scatter_about(key_of[9], (C,), 0.3, 1.5, jnp.float32)
    norm3_gain = jnp.clip(1.0 + 0.1 * jax.random.normal(key_of[10], (C,), jnp.float32), 0.5, 1.5)
    norm3_shift = scatter_about(key_of[11], (C,), 0.3, 1.5, jnp.float32)
    query_weight = scatter_about(key_of[12], (C, C), C ** -0.5, 0.25)
    query_shift = scatter_about(key_of[13], (C,), 0.5, 2.0, jnp.float32)
    key_weight = scatter_about(key_of[14], (C, C), C ** -0.5, 0.25)
    value_weight = scatter_about(key_of[15], (C, C), C ** -0.5, 0.25)
    value_shift = scatter_about(key_of[16], (C,), 0.3, 1.5, jnp.float32)
    out_weight = scatter_about(key_of[17], (C, C), (C // 32) ** -0.5, 1.5)
    out_shift = scatter_about(key_of[18], (C,), 0.3, 1.5, jnp.float32)
    return {"features": features, "cotangent": cotangent, "norm1_gain": norm1_gain, "norm1_shift": norm1_shift, "conv1_kernel": conv1_kernel, "conv1_shift": conv1_shift, "norm2_gain": norm2_gain, "norm2_shift": norm2_shift, "conv2_kernel": conv2_kernel, "conv2_shift": conv2_shift, "norm3_gain": norm3_gain, "norm3_shift": norm3_shift, "query_weight": query_weight, "query_shift": query_shift, "key_weight": key_weight, "value_weight": value_weight, "value_shift": value_shift, "out_weight": out_weight, "out_shift": out_shift}


@jax.custom_vjp
def reduced_precision(v):
    return lax.optimization_barrier(v.astype(jnp.bfloat16)).astype(jnp.float32)

@jax.custom_vjp
def reduced_precision_backward(v):
    return v

def low_keep(v):
    return (reduced_precision(v), None)

def low_pass(kept, grad):
    return (grad,)

def back_keep(v):
    return (v, None)

def back_low(kept, grad):
    return (reduced_precision(grad),)
reduced_precision.defvjp(low_keep, low_pass)
reduced_precision_backward.defvjp(back_keep, back_low)
EPSILON = 1e-06
PRECISION_TOP = lax.Precision.HIGHEST

def silu_apply(tensor):
    return tensor * jax.nn.sigmoid(tensor)

def group_norm(tensor, norm_gain, norm_offset):
    height, images, across, channels = tensor.shape
    grouped = tensor.reshape(height, images, across, GROUPS, channels // GROUPS)
    centre = lax.optimization_barrier(jnp.mean(grouped, axis=(0, 2, 4), keepdims=True))
    spread = lax.optimization_barrier(jnp.mean(jnp.square(grouped - centre), axis=(0, 2, 4), keepdims=True))
    normed = (grouped - centre) * lax.rsqrt(spread + EPSILON)
    return normed.reshape(tensor.shape) * norm_gain + norm_offset

def convolve(tensor, kernel, offset):
    height, images, across, channels = tensor.shape
    padded = jnp.pad(tensor, ((1, 1), (0, 0), (1, 1), (0, 0)))
    summed = jnp.zeros((height, images, across, kernel.shape[3]), jnp.float32)
    for row_off in range(3):
        for col_off in range(3):
            window = padded[row_off:row_off + height, :, col_off:col_off + across, :]
            summed = summed + jnp.einsum('rbwc,cd->rbwd', window, kernel[row_off, col_off], precision=PRECISION_TOP)
    return summed + offset

def project(tensor, weight):
    return jnp.einsum('rbwc,cd->rbwd', tensor, weight, precision=PRECISION_TOP)

def image_to_sequence(tensor):
    height, images, across, channels = tensor.shape
    return tensor.transpose(1, 0, 2, 3).reshape(images, height * across, channels)

def decoder_layer(features, norm1_gain, norm1_shift, conv1_kernel, conv1_shift, norm2_gain, norm2_shift, conv2_kernel, conv2_shift, norm3_gain, norm3_shift, query_weight, query_shift, key_weight, value_weight, value_shift, out_weight, out_shift):
    height, images, across, channels = features.shape
    activated = reduced_precision(silu_apply(group_norm(features, norm1_gain, norm1_shift)))
    conv_out = reduced_precision_backward(convolve(activated, conv1_kernel, conv1_shift))
    second = reduced_precision(silu_apply(group_norm(conv_out, norm2_gain, norm2_shift)))
    branch = reduced_precision_backward(convolve(second, conv2_kernel, conv2_shift))
    residual = features + branch
    normed = reduced_precision(group_norm(residual, norm3_gain, norm3_shift))
    query_rows = reduced_precision(reduced_precision_backward(project(normed, query_weight) + query_shift))
    key_state_rows = reduced_precision(reduced_precision_backward(project(normed, key_weight)))
    value_state_rows = reduced_precision(reduced_precision_backward(project(normed, value_weight) + value_shift))
    attention_score_scale = 1.0 / math.sqrt(channels)
    attention_scores = reduced_precision_backward(jnp.einsum('xao,xno->xan', image_to_sequence(query_rows), image_to_sequence(key_state_rows), precision=PRECISION_TOP) * attention_score_scale)
    weight_tensors = reduced_precision(jax.nn.softmax(attention_scores, axis=-1))
    attention_output = reduced_precision(reduced_precision_backward(jnp.einsum('afj,ajy->afy', weight_tensors, image_to_sequence(value_state_rows), precision=PRECISION_TOP)))
    attention_output = attention_output.reshape(images, height, across, channels).transpose(1, 0, 2, 3)
    return residual + project(attention_output, out_weight) + out_shift

def reference(features, cotangent, norm1_gain, norm1_shift, conv1_kernel, conv1_shift, norm2_gain, norm2_shift, conv2_kernel, conv2_shift, norm3_gain, norm3_shift, query_weight, query_shift, key_weight, value_weight, value_shift, out_weight, out_shift):
    params = (norm1_gain, norm1_shift, conv1_kernel.astype(jnp.float32), conv1_shift, norm2_gain, norm2_shift, conv2_kernel.astype(jnp.float32), conv2_shift, norm3_gain, norm3_shift, query_weight.astype(jnp.float32), query_shift, key_weight.astype(jnp.float32), value_weight.astype(jnp.float32), value_shift, out_weight.astype(jnp.float32), out_shift)
    images = features.shape[1]
    group_size = max((candidate for candidate in range(1, 5) if images % candidate == 0))
    num_steps = images // group_size

    def accumulate(totals, position):
        start_at = (position * group_size).astype(jnp.int32)
        block_in = lax.dynamic_slice_in_dim(features, start_at, group_size, 1).astype(jnp.float32)
        block_back = lax.dynamic_slice_in_dim(cotangent, start_at, group_size, 1).astype(jnp.float32)
        result, pullback = jax.vjp(decoder_layer, block_in, *params)
        gradients = pullback(block_back)
        updated = tuple((total + gradient for total, gradient in zip(totals, gradients[1:])))
        return (updated, (result, gradients[0]))
    initial = tuple((jnp.zeros(param.shape, jnp.float32) for param in params))
    totals, (results, input_grads) = lax.scan(accumulate, initial, jnp.arange(num_steps, dtype=jnp.int32))

    def unstack(stacked):
        return stacked.transpose(1, 0, 2, 3, 4).reshape(features.shape)
    return (unstack(results), unstack(input_grads), totals[0], totals[1], totals[2], totals[3], totals[4], totals[5], totals[6], totals[7], totals[8], totals[9], totals[10], totals[11], totals[12], totals[13], totals[14], totals[15], totals[16])
```

```python
import math

import jax
import jax.numpy as jnp
from jax import lax
from jax.experimental import pallas as pl
from jax.experimental.pallas import tpu as pltpu
from jax.sharding import PartitionSpec as P

GROUPS = 32
H = 32


EPSILON = 1e-06


def padded_2(block, sides, width):
    for axis, dim in sides:
        count = lax.axis_size(axis)
        forward = [(i, i + 1) for i in range(count - 1)]
        backward = [(target, source) for source, target in forward]
        low = lax.ppermute(
            lax.slice_in_dim(block, block.shape[dim] - width, None, axis=dim), axis, forward
        )
        high = lax.ppermute(lax.slice_in_dim(block, 0, width, axis=dim), axis, backward)
        block = jnp.concatenate([low, block, high], axis=dim)
    return block


def sigmoid_pair(tensor):
    logistic = jax.nn.sigmoid(tensor)
    return (tensor * logistic, logistic * (1.0 + tensor * (1.0 - logistic)))


def group_view(tensor):
    height, images, across, channels = tensor.shape
    return tensor.reshape(height, images, across, GROUPS, channels // GROUPS)


def spread_back(statistic):
    return statistic[None, :, None, :, None]


def norm_forward(tensor, norm_gain, norm_offset):
    grouped = group_view(tensor)
    members = H * tensor.shape[2] * (tensor.shape[3] // GROUPS)
    centre = lax.psum(jnp.sum(grouped, axis=(0, 2, 4)), "rows") / members
    centered = grouped - spread_back(centre)
    spread = lax.psum(jnp.sum(jnp.square(centered), axis=(0, 2, 4)), "rows") / members
    factor = lax.rsqrt(spread + EPSILON)
    normed = (centered * spread_back(factor)).reshape(tensor.shape)
    return (normed * norm_gain + norm_offset, normed, factor)


def norm_backward(gradient, normed, factor, norm_gain):
    gain_grad = jnp.sum(gradient * normed, axis=(0, 1, 2))
    offset_grad = jnp.sum(gradient, axis=(0, 1, 2))
    scaled = group_view(gradient * norm_gain)
    flat_normed = group_view(normed)
    members = H * gradient.shape[2] * (gradient.shape[3] // GROUPS)
    mean_grad, cross_grad = lax.psum(
        (jnp.sum(scaled, axis=(0, 2, 4)), jnp.sum(scaled * flat_normed, axis=(0, 2, 4))), "rows"
    )
    input_grad = (
        scaled - spread_back(mean_grad / members) - flat_normed * spread_back(cross_grad / members)
    ) * spread_back(factor)
    return (input_grad.reshape(gradient.shape), gain_grad, offset_grad)


def widen(tensor):
    return jnp.pad(tensor, ((0, 0), (0, 0), (1, 1), (0, 0)))


def conv_forward(tensor, kernel, offset):
    height, across = (tensor.shape[0], tensor.shape[2])
    padded = widen(padded_2(tensor, (("rows", 0),), 1))
    summed = jnp.zeros(tensor.shape[:3] + (kernel.shape[3],), jnp.float32)
    for row_off in range(3):
        for col_off in range(3):
            window = padded[row_off : row_off + height, :, col_off : col_off + across, :]
            summed = summed + jnp.einsum(
                "rbwc,cd->rbwd",
                window,
                kernel[row_off, col_off],
                preferred_element_type=jnp.float32,
            )
    return (summed + offset, padded)


def conv_backward(gradient, padded, kernel):
    height, across = (gradient.shape[0], gradient.shape[2])
    beside_all = widen(padded_2(gradient, (("rows", 0),), 1))
    input_grad = jnp.zeros(gradient.shape[:3] + (kernel.shape[2],), jnp.float32)
    tap_grads = []
    for row_off in range(3):
        for col_off in range(3):
            window = beside_all[
                2 - row_off : 2 - row_off + height, :, 2 - col_off : 2 - col_off + across, :
            ]
            input_grad = input_grad + jnp.einsum(
                "rbwd,cd->rbwc",
                window,
                kernel[row_off, col_off],
                preferred_element_type=jnp.float32,
            )
            source = padded[row_off : row_off + height, :, col_off : col_off + across, :]
            tap_grads.append(
                jnp.einsum("rbwc,rbwd->cd", source, gradient, preferred_element_type=jnp.float32)
            )
    kernel_grad = jnp.stack(tap_grads).reshape(kernel.shape)
    offset_grad = jnp.sum(gradient.astype(jnp.float32), axis=(0, 1, 2))
    return (input_grad, kernel_grad, offset_grad)


def linear(tensor, weight):
    return jnp.einsum("rbwc,cd->rbwd", tensor, weight, preferred_element_type=jnp.float32)


def back_linear(gradient, weight):
    return jnp.einsum("rbwd,cd->rbwc", gradient, weight, preferred_element_type=jnp.float32)


def weight_product(tensor, gradient):
    return jnp.einsum("rbwc,rbwd->cd", tensor, gradient, preferred_element_type=jnp.float32)


def image_to_sequence(tensor):
    height, images, across, channels = tensor.shape
    return tensor.transpose(1, 0, 2, 3).reshape(images, height * across, channels)


def from_sequence(sequence, height, across):
    images, length, channels = sequence.shape
    return sequence.reshape(images, height, across, channels).transpose(1, 0, 2, 3)


def reduce_all(gradients):
    flattened = jnp.concatenate([gradient.reshape(-1) for gradient in gradients])
    length = flattened.shape[0]
    devices = lax.axis_size("rows") * lax.axis_size("imgs")
    per_share = -(-length // (devices * 128)) * 128
    padded_len = per_share * devices
    strided = jnp.pad(flattened, (0, padded_len - length)).reshape(per_share, devices).T
    packed = strided.reshape(padded_len // 128, 128)
    my_share = lax.psum_scatter(packed, ("rows", "imgs"), scatter_dimension=0, tiled=True)
    summed_all = lax.all_gather(
        my_share.astype(jnp.bfloat16), ("rows", "imgs"), axis=0, tiled=True
    ).astype(my_share.dtype)
    summed_all = summed_all.reshape(devices, per_share).T.reshape(-1)
    results = []
    offset_at = 0
    for gradient in gradients:
        results.append(summed_all[offset_at : offset_at + gradient.size].reshape(gradient.shape))
        offset_at = offset_at + gradient.size
    return results


def per_device_by_rows(
    features,
    cotangent,
    norm1_gain,
    norm1_shift,
    conv1_kernel,
    conv1_shift,
    norm2_gain,
    norm2_shift,
    conv2_kernel,
    conv2_shift,
    norm3_gain,
    norm3_shift,
    query_weight,
    query_shift,
    key_weight,
    value_weight,
    value_shift,
    out_weight,
    out_shift,
):
    height, images, across, channels = features.shape
    attention_score_scale = 1.0 / math.sqrt(channels)
    inputs = features.astype(jnp.float32)
    norm_one, normed_one, factor_one = norm_forward(inputs, norm1_gain, norm1_shift)
    act_one, slope_one = sigmoid_pair(norm_one)
    conv_one, padded_one = conv_forward(act_one.astype(jnp.bfloat16), conv1_kernel, conv1_shift)
    norm_two, normed_two, factor_two = norm_forward(conv_one, norm2_gain, norm2_shift)
    act_two, slope_two = sigmoid_pair(norm_two)
    conv_two, padded_two = conv_forward(act_two.astype(jnp.bfloat16), conv2_kernel, conv2_shift)
    residual = inputs + conv_two
    norm_three, normed_three, factor_three = norm_forward(residual, norm3_gain, norm3_shift)
    attend_input = norm_three.astype(jnp.bfloat16)
    query_rows = (linear(attend_input, query_weight) + query_shift).astype(jnp.bfloat16)
    key_state_rows = linear(attend_input, key_weight).astype(jnp.bfloat16)
    value_state_rows = (linear(attend_input, value_weight) + value_shift).astype(jnp.bfloat16)
    all_keys, all_values = (
        lax.all_gather(key_state_rows, "rows", axis=0, tiled=True),
        lax.all_gather(value_state_rows, "rows", axis=0, tiled=True),
    )
    query_sequence = image_to_sequence(query_rows)
    key_sequence = image_to_sequence(all_keys)
    value_sequence = image_to_sequence(all_values)
    attention_scores = (
        jnp.einsum("xao,xno->xan", query_sequence, key_sequence, preferred_element_type=jnp.float32)
        * attention_score_scale
    )
    row_peak = jnp.max(attention_scores, axis=-1, keepdims=True)
    log_total = row_peak + jnp.log(
        jnp.sum(jnp.exp(attention_scores - row_peak), axis=-1, keepdims=True)
    )
    weight_tensors = jnp.exp(attention_scores - log_total).astype(jnp.bfloat16)
    attended_seq = jnp.einsum(
        "afj,ajy->afy", weight_tensors, value_sequence, preferred_element_type=jnp.float32
    )
    attention_output = from_sequence(attended_seq.astype(jnp.bfloat16), height, across)
    output = residual + linear(attention_output, out_weight) + out_shift
    out_shift_grad = jnp.sum(cotangent.astype(jnp.float32), axis=(0, 1, 2))
    out_weight_grad = weight_product(attention_output, cotangent)
    mixed_grad = back_linear(cotangent, out_weight).astype(jnp.bfloat16)
    mixed_sequence = image_to_sequence(mixed_grad)
    scores_again = (
        jnp.einsum("xao,xno->xan", query_sequence, key_sequence, preferred_element_type=jnp.float32)
        * attention_score_scale
    )
    probabilities = jnp.exp(scores_again - log_total)
    probability_gradient = jnp.einsum(
        "xao,xno->xan", mixed_sequence, value_sequence, preferred_element_type=jnp.float32
    )
    delta = jnp.sum(probabilities * probability_gradient, axis=-1, keepdims=True)
    score_gradient = (probabilities * (probability_gradient - delta)).astype(jnp.bfloat16)
    query_local = (
        jnp.einsum("afj,ajy->afy", score_gradient, key_sequence, preferred_element_type=jnp.float32)
        * attention_score_scale
    )
    query_grad = from_sequence(query_local, height, across).astype(jnp.bfloat16)
    key_full = (
        jnp.einsum(
            "svt,svz->stz", score_gradient, query_sequence, preferred_element_type=jnp.float32
        )
        * attention_score_scale
    )
    value_full = jnp.einsum(
        "svt,svz->stz",
        probabilities.astype(jnp.bfloat16),
        mixed_sequence,
        preferred_element_type=jnp.float32,
    )
    stacked = from_sequence(jnp.concatenate([key_full, value_full], axis=-1), H, across)
    own_grads = lax.psum_scatter(
        stacked.astype(jnp.bfloat16), "rows", scatter_dimension=0, tiled=True
    ).astype(jnp.float32)
    key_grad = own_grads[..., :channels].astype(jnp.bfloat16)
    value_grad = own_grads[..., channels:].astype(jnp.bfloat16)
    query_weight_grad = weight_product(attend_input, query_grad)
    query_shift_grad = jnp.sum(query_grad.astype(jnp.float32), axis=(0, 1, 2))
    key_weight_grad = weight_product(attend_input, key_grad)
    value_weight_grad = weight_product(attend_input, value_grad)
    value_shift_grad = jnp.sum(value_grad.astype(jnp.float32), axis=(0, 1, 2))
    attend_grad = (
        back_linear(query_grad, query_weight)
        + back_linear(key_grad, key_weight)
        + back_linear(value_grad, value_weight)
    )
    resid_part, norm3_gain_grad, norm3_shift_grad = norm_backward(
        attend_grad, normed_three, factor_three, norm3_gain
    )
    resid_grad = cotangent.astype(jnp.float32) + resid_part
    conv_two_in, conv2_kernel_grad, conv2_shift_grad = conv_backward(
        resid_grad.astype(jnp.bfloat16), padded_two, conv2_kernel
    )
    conv_one_out, norm2_gain_grad, norm2_shift_grad = norm_backward(
        conv_two_in * slope_two, normed_two, factor_two, norm2_gain
    )
    conv_one_in, conv1_kernel_grad, conv1_shift_grad = conv_backward(
        conv_one_out.astype(jnp.bfloat16), padded_one, conv1_kernel
    )
    inputs_part, norm1_gain_grad, norm1_shift_grad = norm_backward(
        conv_one_in * slope_one, normed_one, factor_one, norm1_gain
    )
    features_grad = resid_grad + inputs_part
    reduced = reduce_all(
        [
            norm1_gain_grad,
            norm1_shift_grad,
            conv1_kernel_grad,
            conv1_shift_grad,
            norm2_gain_grad,
            norm2_shift_grad,
            conv2_kernel_grad,
            conv2_shift_grad,
            norm3_gain_grad,
            norm3_shift_grad,
            query_weight_grad,
            query_shift_grad,
            key_weight_grad,
            value_weight_grad,
            value_shift_grad,
            out_weight_grad,
            out_shift_grad,
        ]
    )
    return (output, features_grad) + tuple(reduced)


F32 = jnp.float32
BF16 = jnp.bfloat16
AXES = ("rows", "imgs")
LIMIT = 48 * 1024 * 1024
TILE = 64
MM_TILE = 256


def kernel_call(body, out_shape, scratch=(), smem_args=1, n_args=0):
    vmem = pl.BlockSpec(memory_space=pltpu.VMEM)
    smem = pl.BlockSpec(memory_space=pltpu.SMEM)
    return pl.pallas_call(
        body,
        out_shape=out_shape,
        in_specs=[smem] * smem_args + [vmem] * n_args,
        out_specs=jax.tree.map(lambda _: vmem, out_shape),
        scratch_shapes=list(scratch),
        compiler_params=pltpu.CompilerParams(vmem_limit_bytes=LIMIT),
    )


def shape_of(shape, dtype):
    return jax.ShapeDtypeStruct(shape, dtype)


def tiles(total, size, body, start=0):
    def step(index, carry):
        body(pl.multiple_of(index * size, size))
        return carry

    lax.fori_loop(start, total // size, step, 0)


def fold_tiles(total, size, body, carry):
    def step(index, held):
        return body(pl.multiple_of(index * size, size), held)

    return lax.fori_loop(0, total // size, step, carry)


def fold_rows(tensor):
    return jnp.sum(tensor.reshape(tensor.shape[0] // 8, 8, tensor.shape[1]), axis=0)


def column(partial):
    return jnp.sum(partial, axis=0, keepdims=True)


def group_mean(column_sum, members):
    channels = column_sum.shape[1]
    size = channels // GROUPS
    one = lax.broadcasted_iota(jnp.int32, (channels, channels), 0) // size
    two = lax.broadcasted_iota(jnp.int32, (channels, channels), 1) // size
    same = jnp.where(one == two, 1.0, 0.0).astype(F32)
    summed = jnp.dot(
        jnp.broadcast_to(column_sum, (8, channels)),
        same,
        precision=lax.Precision.HIGHEST,
        preferred_element_type=F32,
    )
    return summed[:1] * (1.0 / members)


def norm_stats(read, total, channels):
    members = total * (channels // GROUPS)
    zero = jnp.zeros((8, channels), F32)
    sums = fold_tiles(total, TILE, lambda at, held: held + fold_rows(read(at)), zero)
    centre = group_mean(column(sums), members)
    squares = fold_tiles(
        total, TILE, lambda at, held: held + fold_rows(jnp.square(read(at) - centre)), zero
    )
    return centre, lax.rsqrt(group_mean(column(squares), members) + EPSILON)


def fill_shifted(cat_ref, at, tile, across):
    size, channels = tile.shape
    place = lax.broadcasted_iota(jnp.int32, tile.shape, 0) % across
    before = jnp.where(place == 0, 0.0, pltpu.roll(tile, 1, 0))
    after = jnp.where(place == across - 1, 0.0, pltpu.roll(tile, size - 1, 0))
    rows = pl.ds(pl.multiple_of(across + at, across), size)
    cat_ref[rows, 0:channels] = before.astype(BF16)
    cat_ref[rows, channels : 2 * channels] = tile.astype(BF16)
    cat_ref[rows, 2 * channels : 3 * channels] = after.astype(BF16)


def clear_border(cat_ref, across):
    width = cat_ref.shape[1]
    total = cat_ref.shape[0]
    cat_ref[0:across, :] = jnp.zeros((across, width), BF16)
    cat_ref[total - across : total, :] = jnp.zeros((across, width), BF16)


def window_product(cat_ref, weight_ref, at, size, across):
    total = None
    for row_off in range(3):
        rows = pl.ds(pl.multiple_of(at + row_off * across, across), size)
        part = jnp.dot(cat_ref[rows, :], weight_ref[row_off], preferred_element_type=F32)
        total = part if total is None else total + part
    return total


def dot_t(left, right):
    return lax.dot_general(left, right, (((1,), (1,)), ((), ())), preferred_element_type=F32)


def t_dot(left, right):
    return lax.dot_general(left, right, (((0,), (0,)), ((), ())), preferred_element_type=F32)


def first_conv_body(
    me_ref, *refs
):
    pieces, (gain_ref, shift_ref, weight_ref, bias_ref) = refs[:8], refs[8:12]
    image_ref, act_ref, conv_ref, stats_ref, cat_ref = refs[12:]
    total, channels = image_ref.shape
    share = total // 8
    across = 32
    me = me_ref[0]
    for index in range(8):
        at = pl.multiple_of((me ^ index) * share, share)
        image_ref[pl.ds(at, share), :] = pieces[index][...]

    def read(at):
        return image_ref[pl.ds(at, TILE), :].astype(F32)

    centre, factor = norm_stats(read, total, channels)
    stats_ref[0:1, :] = centre
    stats_ref[1:2, :] = factor
    gain, shift = gain_ref[...], shift_ref[...]
    clear_border(cat_ref, across)

    def activate(at):
        held = (read(at) - centre) * factor * gain + shift
        act = held * jax.nn.sigmoid(held)
        act_ref[pl.ds(at, TILE), :] = act.astype(BF16)
        fill_shifted(cat_ref, at, act, across)

    tiles(total, TILE, activate)
    bias = bias_ref[...]

    def convolve(at):
        conv_ref[pl.ds(at, MM_TILE), :] = (
            window_product(cat_ref, weight_ref, at, MM_TILE, across) + bias
        )

    tiles(total, MM_TILE, convolve)


def second_conv_body(
    gain2_ref, shift2_ref, weight_ref, bias_ref, gain3_ref, shift3_ref,
    q_weight_ref, q_shift_ref, k_weight_ref, v_weight_ref, v_shift_ref, image_ref, conv_ref,
    act_ref, resid_ref, stats_ref, norm_ref, q_ref, k_ref, v_ref, cat_ref,
):
    total, channels = conv_ref.shape
    across = 32

    def read(at):
        return conv_ref[pl.ds(at, TILE), :]

    centre, factor = norm_stats(read, total, channels)
    stats_ref[0:1, :] = centre
    stats_ref[1:2, :] = factor
    gain, shift = gain2_ref[...], shift2_ref[...]
    clear_border(cat_ref, across)

    def activate(at):
        held = (read(at) - centre) * factor * gain + shift
        act = held * jax.nn.sigmoid(held)
        act_ref[pl.ds(at, TILE), :] = act.astype(BF16)
        fill_shifted(cat_ref, at, act, across)

    tiles(total, TILE, activate)
    bias = bias_ref[...]

    def convolve(at):
        rows = pl.ds(at, MM_TILE)
        resid_ref[rows, :] = (
            window_product(cat_ref, weight_ref, at, MM_TILE, across)
            + bias
            + image_ref[rows, :].astype(F32)
        )

    tiles(total, MM_TILE, convolve)
    centre3, factor3 = norm_stats(lambda at: resid_ref[pl.ds(at, TILE), :], total, channels)
    stats_ref[2:3, :] = centre3
    stats_ref[3:4, :] = factor3
    gain3, shift3 = gain3_ref[...], shift3_ref[...]
    q_shift, v_shift = q_shift_ref[...], v_shift_ref[...]

    def project(at):
        rows = pl.ds(at, MM_TILE)
        held = ((resid_ref[rows, :] - centre3) * factor3 * gain3 + shift3).astype(BF16)
        norm_ref[rows, :] = held
        q_ref[rows, :] = (
            jnp.dot(held, q_weight_ref[...], preferred_element_type=F32) + q_shift
        ).astype(BF16)
        k_ref[rows, :] = jnp.dot(held, k_weight_ref[...], preferred_element_type=F32).astype(BF16)
        v_ref[rows, :] = (
            jnp.dot(held, v_weight_ref[...], preferred_element_type=F32) + v_shift
        ).astype(BF16)

    tiles(total, MM_TILE, project)


def attention_body(me_ref, *refs):
    cot_pieces = refs[:8]
    (q_ref, k_ref, v_ref, norm_ref, resid_ref, stats_ref, gain3_ref,
     q_weight_ref, k_weight_ref, v_weight_ref, o_weight_ref, o_shift_ref) = refs[8:20]
    out_pieces = refs[20:28]
    (weights_grad_ref, small_ref, d_resid_ref, d_conv_ref,
     cot_ref, out_ref, mixed_ref, d_q_ref, d_k_acc, d_v_acc, d_k_ref, d_v_ref) = refs[28:]
    total, channels = q_ref.shape
    share = total // 8
    scale = 1.0 / math.sqrt(channels)
    me = me_ref[0]
    for index in range(8):
        at = pl.multiple_of((me ^ index) * share, share)
        cot_ref[pl.ds(at, share), :] = cot_pieces[index][...]
    o_shift = o_shift_ref[...]
    d_k_acc[...] = jnp.zeros(d_k_acc.shape, F32)
    d_v_acc[...] = jnp.zeros(d_v_acc.shape, F32)

    def attend(at):
        rows = pl.ds(at, MM_TILE)
        query = q_ref[rows, :]
        scores = dot_t(query, k_ref[...]) * scale
        exps = jnp.exp(scores - jnp.max(scores, axis=-1, keepdims=True))
        probs = exps * (1.0 / jnp.sum(exps, axis=-1, keepdims=True))
        weights = probs.astype(BF16)
        mixed = jnp.dot(weights, v_ref[...], preferred_element_type=F32).astype(BF16)
        mixed_ref[rows, :] = mixed
        out_ref[rows, :] = (
            resid_ref[rows, :]
            + jnp.dot(mixed, o_weight_ref[...], preferred_element_type=F32)
            + o_shift
        ).astype(BF16)
        d_mixed = dot_t(cot_ref[rows, :], o_weight_ref[...]).astype(BF16)
        d_prob = dot_t(d_mixed, v_ref[...])
        delta = jnp.sum(probs * d_prob, axis=-1, keepdims=True)
        d_scores = (probs * (d_prob - delta)).astype(BF16)
        d_q_ref[rows, :] = (
            jnp.dot(d_scores, k_ref[...], preferred_element_type=F32) * scale
        ).astype(BF16)
        d_k_acc[...] += t_dot(d_scores, query)
        d_v_acc[...] += t_dot(weights, d_mixed)

    tiles(total, MM_TILE, attend)
    for index in range(8):
        at = pl.multiple_of((me ^ index) * share, share)
        out_pieces[index][...] = out_ref[pl.ds(at, share), :]
    d_k_ref[...] = (d_k_acc[...] * scale).astype(BF16)
    d_v_ref[...] = d_v_acc[...].astype(BF16)
    weights_grad_ref[0] = t_dot(norm_ref[...], d_q_ref[...]).astype(BF16)
    weights_grad_ref[1] = t_dot(norm_ref[...], d_k_ref[...]).astype(BF16)
    weights_grad_ref[2] = t_dot(norm_ref[...], d_v_ref[...]).astype(BF16)
    weights_grad_ref[3] = t_dot(mixed_ref[...], cot_ref[...]).astype(BF16)

    centre, factor = stats_ref[2:3, :], stats_ref[3:4, :]
    gain = gain3_ref[...]
    zero = jnp.zeros((8, channels), F32)

    tiles(total, MM_TILE, lambda at: back_tile(
        at, d_q_ref, d_k_ref, d_v_ref, q_weight_ref, k_weight_ref, v_weight_ref, d_resid_ref))

    def gather(at, held):
        rows = pl.ds(at, TILE)
        grad = d_resid_ref[rows, :]
        normed = (resid_ref[rows, :] - centre) * factor
        return (
            held[0] + fold_rows(grad),
            held[1] + fold_rows(grad * normed),
            held[2] + fold_rows(cot_ref[rows, :].astype(F32)),
            held[3] + fold_rows(d_q_ref[rows, :].astype(F32)),
            held[4] + fold_rows(d_v_ref[rows, :].astype(F32)),
        )

    sums = fold_tiles(total, TILE, gather, (zero,) * 5)
    shift_grad, gain_grad, o_shift_grad, q_shift_grad, v_shift_grad = [column(s) for s in sums]
    members = total * (channels // GROUPS)
    mean_grad = group_mean(shift_grad * gain, members)
    cross_grad = group_mean(gain_grad * gain, members)

    def finish(at, held):
        rows = pl.ds(at, TILE)
        normed = (resid_ref[rows, :] - centre) * factor
        grad = cot_ref[rows, :].astype(F32) + factor * (
            d_resid_ref[rows, :] * gain - mean_grad - normed * cross_grad
        )
        d_resid_ref[rows, :] = grad
        rounded = grad.astype(BF16)
        d_conv_ref[rows, :] = rounded
        return held + fold_rows(rounded.astype(F32))

    conv_shift_grad = column(fold_tiles(total, TILE, finish, zero))
    small_ref[0:1, :] = gain_grad
    small_ref[1:2, :] = shift_grad
    small_ref[2:3, :] = q_shift_grad
    small_ref[3:4, :] = v_shift_grad
    small_ref[4:5, :] = o_shift_grad
    small_ref[5:6, :] = conv_shift_grad
    small_ref[6:8, :] = jnp.zeros((2, channels), F32)


def back_tile(at, d_q_ref, d_k_ref, d_v_ref, q_weight_ref, k_weight_ref, v_weight_ref, out_ref):
    rows = pl.ds(at, MM_TILE)
    out_ref[rows, :] = (
        dot_t(d_q_ref[rows, :], q_weight_ref[...])
        + dot_t(d_k_ref[rows, :], k_weight_ref[...])
        + dot_t(d_v_ref[rows, :], v_weight_ref[...])
    )


def kernel_grad_body(act_ref, grad_ref, out_ref, cat_ref, turned_ref):
    total, channels = act_ref.shape
    across = 32
    clear_border(cat_ref, across)

    def fill(at):
        fill_shifted(cat_ref, at, grad_ref[pl.ds(at, TILE), :].astype(F32), across)

    tiles(total, TILE, fill)
    turned_ref[...] = act_ref[...].T
    for row_off in range(3):
        first = (2 - row_off) * across

        def product(at, row_off=row_off, first=first):
            rows = pl.ds(at, MM_TILE)
            part = jnp.dot(
                turned_ref[rows, :], cat_ref[first : first + total, :], preferred_element_type=F32
            ).astype(BF16)
            for col_off in range(3):
                low = (2 - col_off) * channels
                out_ref[row_off * 3 + col_off, rows, :] = part[:, low : low + channels]

        tiles(channels, MM_TILE, product)


def input_grad_body(with_rest, me_ref, *refs):
    grad_ref, weight_ref, source_ref, stats_ref, gain_ref, shift_ref = refs[:6]
    rest_ref = refs[6] if with_rest else None
    refs = refs[7:] if with_rest else refs[6:]
    if with_rest:
        out_pieces, (small_ref, cat_ref, held_ref, out_ref) = refs[:8], refs[8:]
    else:
        out_ref, small_ref, cat_ref, held_ref = refs
    total, channels = grad_ref.shape
    across = 32
    centre, factor = stats_ref[0:1, :], stats_ref[1:2, :]
    gain, shift = gain_ref[...], shift_ref[...]
    clear_border(cat_ref, across)

    def fill(at):
        fill_shifted(cat_ref, at, grad_ref[pl.ds(at, TILE), :].astype(F32), across)

    tiles(total, TILE, fill)

    def product(at):
        held_ref[pl.ds(at, MM_TILE), :] = window_product(cat_ref, weight_ref, at, MM_TILE, across)

    tiles(total, MM_TILE, product)
    zero = jnp.zeros((8, channels), F32)

    def slope(at, held):
        rows = pl.ds(at, TILE)
        normed = (source_ref[rows, :].astype(F32) - centre) * factor
        pre = normed * gain + shift
        logistic = jax.nn.sigmoid(pre)
        grad = held_ref[rows, :] * (logistic * (1.0 + pre * (1.0 - logistic)))
        held_ref[rows, :] = grad
        return held[0] + fold_rows(grad), held[1] + fold_rows(grad * normed)

    shift_sum, gain_sum = fold_tiles(total, TILE, slope, (zero, zero))
    shift_grad, gain_grad = column(shift_sum), column(gain_sum)
    members = total * (channels // GROUPS)
    mean_grad = group_mean(shift_grad * gain, members)
    cross_grad = group_mean(gain_grad * gain, members)

    def finish(at, held):
        rows = pl.ds(at, TILE)
        normed = (source_ref[rows, :].astype(F32) - centre) * factor
        grad = factor * (held_ref[rows, :] * gain - mean_grad - normed * cross_grad)
        if with_rest:
            grad = grad + rest_ref[rows, :]
        rounded = grad.astype(BF16)
        out_ref[rows, :] = rounded
        return held + fold_rows(rounded.astype(F32))

    out_sum = column(fold_tiles(total, TILE, finish, zero))
    small_ref[0:1, :] = gain_grad
    small_ref[1:2, :] = shift_grad
    small_ref[2:3, :] = out_sum
    small_ref[3:8, :] = jnp.zeros((5, channels), F32)
    if with_rest:
        share = total // 8
        me = me_ref[0]
        for index in range(8):
            at = pl.multiple_of((me ^ index) * share, share)
            out_pieces[index][...] = out_ref[pl.ds(at, share), :]


def pack_body(me_ref, block_ref, *piece_refs):
    me = me_ref[0]
    for index in range(8):
        for row in range(block_ref.shape[0]):
            piece_refs[index][pl.ds(row * 32, 32), :] = block_ref[row, me ^ index]


def unpack_body(me_ref, *refs):
    pieces, block_ref = refs[:8], refs[8]
    me = me_ref[0]
    for index in range(8):
        for row in range(block_ref.shape[0]):
            block_ref[row, me ^ index] = pieces[index][pl.ds(row * 32, 32), :].astype(F32)


def pack(me, block):
    rows, _, across, channels = block.shape
    piece = shape_of((rows * across, channels), BF16)
    return kernel_call(pack_body, [piece] * 8, n_args=1)(me, block)


def unpack(me, pieces, block_shape):
    return kernel_call(unpack_body, shape_of(block_shape, F32), n_args=8)(me, *pieces)


def swap_pieces(pieces):
    count = len(pieces)
    return [pieces[0]] + [
        lax.ppermute(pieces[k], "rows", [(r, r ^ k) for r in range(count)]) for k in range(1, count)
    ]


def partner_table(kind):
    table = []
    for row in range(8):
        for img in range(4):
            core = row & 1
            if kind == "core":
                other = (row ^ 1, img)
            elif kind == "near":
                other = (row ^ 2, img)
            elif kind == "far":
                other = (row ^ 4, img)
            elif kind == "plane_a":
                other = (row, img ^ (2 if core else 1))
            else:
                other = (row, img ^ (1 if core else 2))
            table.append((row * 4 + img, other[0] * 4 + other[1]))
    return table


ORDER = ("core", "plane_a", "plane_b", "near", "far")


def exchange(tensor, kind):
    return lax.ppermute(tensor, AXES, partner_table(kind))


def own_bits():
    row, img = lax.axis_index("rows"), lax.axis_index("imgs")
    core, near, far = row & 1, (row >> 1) & 1, (row >> 2) & 1
    low, high = img & 1, (img >> 1) & 1
    return {
        "core": core,
        "plane_a": jnp.where(core == 1, high, low),
        "plane_b": jnp.where(core == 1, low, high),
        "near": near,
        "far": far,
    }


def halve(tensor, bit, kind):
    half = tensor.shape[0] // 2
    sent = lax.dynamic_slice_in_dim(tensor, (1 - bit) * half, half, 0)
    kept = lax.dynamic_slice_in_dim(tensor, bit * half, half, 0)
    got = exchange(sent, kind)
    return (kept.astype(F32) + got.astype(F32)).astype(BF16)


def double(tensor, bit, kind, dtype=BF16):
    half = tensor.shape[0]
    got = exchange(tensor, kind)
    both = jnp.zeros((2 * half,) + tensor.shape[1:], dtype)
    both = lax.dynamic_update_slice_in_dim(both, tensor.astype(dtype), bit * half, 0)
    return lax.dynamic_update_slice_in_dim(both, got.astype(dtype), (1 - bit) * half, 0)


def reduce_chunk(chunk, bits):
    for kind in ORDER:
        chunk = halve(chunk, bits[kind], kind)
    for kind in ORDER[:0:-1]:
        chunk = double(chunk, bits[kind], kind)
    return double(chunk, bits["core"], "core", F32)


def reduce_small(rows):
    for kind in ORDER:
        rows = rows + exchange(rows, kind)
    return rows


def turned_kernel(kernel):
    return kernel[::-1, ::-1].transpose(0, 1, 3, 2).reshape(3, -1, kernel.shape[2])


def per_device_by_images(
    features,
    cotangent,
    norm1_gain,
    norm1_shift,
    conv1_kernel,
    conv1_shift,
    norm2_gain,
    norm2_shift,
    conv2_kernel,
    conv2_shift,
    norm3_gain,
    norm3_shift,
    query_weight,
    query_shift,
    key_weight,
    value_weight,
    value_shift,
    out_weight,
    out_shift,
):
    rows, images, across, channels = features.shape
    total = rows * images * across
    bits = own_bits()
    me = lax.axis_index("rows").astype(jnp.int32).reshape(1)

    def line(vector):
        return vector.reshape(1, channels)

    image = shape_of((total, channels), BF16)
    image_f32 = shape_of((total, channels), F32)
    piece = shape_of((total // 8, channels), BF16)
    stats_shape = shape_of((8, channels), F32)
    cat = pltpu.VMEM((total + 2 * across, 3 * channels), BF16)

    feature_pieces = swap_pieces(pack(me, features))
    cot_sent = pack(me, cotangent)
    turned1 = turned_kernel(conv1_kernel)
    turned2 = turned_kernel(conv2_kernel)

    image_in, act_one, conv_one, stats_one = kernel_call(
        first_conv_body, [image, image, image_f32, stats_shape], [cat], n_args=12
    )(
        me, *feature_pieces, line(norm1_gain), line(norm1_shift),
        conv1_kernel.reshape(3, 3 * channels, channels), line(conv1_shift),
    )
    cot_pieces = swap_pieces(cot_sent)
    act_two, residual, stats_two, normed, query, key, value = kernel_call(
        second_conv_body, [image, image_f32, stats_shape, image, image, image, image], [cat],
        smem_args=0, n_args=13,
    )(
        line(norm2_gain), line(norm2_shift), conv2_kernel.reshape(3, 3 * channels, channels),
        line(conv2_shift), line(norm3_gain), line(norm3_shift), query_weight, line(query_shift),
        key_weight, value_weight, line(value_shift), image_in, conv_one,
    )
    attended = kernel_call(
        attention_body,
        [piece] * 8
        + [shape_of((4, channels, channels), BF16), stats_shape, image_f32, image],
        [
            pltpu.VMEM((total, channels), BF16),
            pltpu.VMEM((total, channels), BF16),
            pltpu.VMEM((total, channels), BF16),
            pltpu.VMEM((total, channels), BF16),
            pltpu.VMEM((total, channels), F32),
            pltpu.VMEM((total, channels), F32),
            pltpu.VMEM((total, channels), BF16),
            pltpu.VMEM((total, channels), BF16),
        ],
        n_args=20,
    )(
        me, *cot_pieces, query, key, value, normed, residual, stats_two, line(norm3_gain),
        query_weight, key_weight, value_weight, out_weight, line(out_shift),
    )
    out_pieces = swap_pieces(attended[:8])
    linear_grads, small_three, d_resid, d_conv_two = attended[8:]

    def kernel_grad(act, grad):
        return kernel_call(
            kernel_grad_body, shape_of((9, channels, channels), BF16),
            [cat, pltpu.VMEM((channels, total), BF16)], smem_args=0, n_args=2,
        )(act, grad)

    conv2_grad = kernel_grad(act_two, d_conv_two)
    d_conv_one, small_two = kernel_call(
        lambda *refs: input_grad_body(False, *refs), [image, stats_shape],
        [cat, pltpu.VMEM((total, channels), F32)], n_args=6,
    )(me, d_conv_two, turned2, conv_one, stats_two, line(norm2_gain), line(norm2_shift))
    conv1_grad = kernel_grad(act_one, d_conv_one)
    finals = kernel_call(
        lambda *refs: input_grad_body(True, *refs), [piece] * 8 + [stats_shape],
        [cat, pltpu.VMEM((total, channels), F32), pltpu.VMEM((total, channels), BF16)], n_args=7,
    )(
        me, d_conv_one, turned1, image_in, stats_one, line(norm1_gain), line(norm1_shift), d_resid
    )
    grad_pieces = swap_pieces(finals[:8])
    small_one = finals[8]

    output = unpack(me, out_pieces, features.shape)
    features_grad = unpack(me, grad_pieces, features.shape)
    linear_sum = reduce_chunk(linear_grads.reshape(-1, channels), bits)
    conv2_sum = reduce_chunk(conv2_grad.reshape(-1, channels), bits)
    conv1_sum = reduce_chunk(conv1_grad.reshape(-1, channels), bits)
    small = reduce_small(jnp.concatenate([small_one, small_two, small_three]))
    linear_sum = linear_sum.reshape(4, channels, channels)
    return (
        output,
        features_grad,
        small[0],
        small[1],
        conv1_sum.reshape(conv1_kernel.shape),
        small[10],
        small[8],
        small[9],
        conv2_sum.reshape(conv2_kernel.shape),
        small[21],
        small[16],
        small[17],
        linear_sum[0],
        small[18],
        linear_sum[1],
        linear_sum[2],
        small[19],
        linear_sum[3],
        small[20],
    )


def per_device(features, *rest):
    rows, imgs = lax.axis_size("rows"), lax.axis_size("imgs")
    if (rows, imgs) == (8, 4) and features.shape[1] == rows and features.shape[2] == 32:
        return per_device_by_images(features, *rest)
    return per_device_by_rows(features, *rest)


def solution(mesh):
    placed = (
        P("rows", "imgs", None, None),
        P("rows", "imgs", None, None),
        P(),
        P(),
        P(),
        P(),
        P(),
        P(),
        P(),
        P(),
        P(),
        P(),
        P(),
        P(),
        P(),
        P(),
        P(),
        P(),
        P(),
    )
    return jax.shard_map(
        per_device,
        mesh=mesh,
        in_specs=placed,
        out_specs=(
            P("rows", "imgs", None, None),
            P("rows", "imgs", None, None),
            P(),
            P(),
            P(),
            P(),
            P(),
            P(),
            P(),
            P(),
            P(),
            P(),
            P(),
            P(),
            P(),
            P(),
            P(),
            P(),
            P(),
        ),
        check_vma=False,
    )
```

```python
import math

import jax
import jax.numpy as jnp
from jax import lax
from jax.experimental import pallas as pl
from jax.experimental.pallas import tpu as pltpu
from jax.sharding import PartitionSpec as P

GROUPS = 32
H = 32


EPSILON = 1e-06


def padded_2(block, sides, width):
    for axis, dim in sides:
        count = lax.axis_size(axis)
        forward = [(i, i + 1) for i in range(count - 1)]
        backward = [(target, source) for source, target in forward]
        low = lax.ppermute(
            lax.slice_in_dim(block, block.shape[dim] - width, None, axis=dim), axis, forward
        )
        high = lax.ppermute(lax.slice_in_dim(block, 0, width, axis=dim), axis, backward)
        block = jnp.concatenate([low, block, high], axis=dim)
    return block


def sigmoid_pair(tensor):
    logistic = jax.nn.sigmoid(tensor)
    return (tensor * logistic, logistic * (1.0 + tensor * (1.0 - logistic)))


def group_view(tensor):
    height, images, across, channels = tensor.shape
    return tensor.reshape(height, images, across, GROUPS, channels // GROUPS)


def spread_back(statistic):
    return statistic[None, :, None, :, None]


def norm_forward(tensor, norm_gain, norm_offset):
    grouped = group_view(tensor)
    members = H * tensor.shape[2] * (tensor.shape[3] // GROUPS)
    centre = lax.psum(jnp.sum(grouped, axis=(0, 2, 4)), "rows") / members
    centered = grouped - spread_back(centre)
    spread = lax.psum(jnp.sum(jnp.square(centered), axis=(0, 2, 4)), "rows") / members
    factor = lax.rsqrt(spread + EPSILON)
    normed = (centered * spread_back(factor)).reshape(tensor.shape)
    return (normed * norm_gain + norm_offset, normed, factor)


def norm_backward(gradient, normed, factor, norm_gain):
    gain_grad = jnp.sum(gradient * normed, axis=(0, 1, 2))
    offset_grad = jnp.sum(gradient, axis=(0, 1, 2))
    scaled = group_view(gradient * norm_gain)
    flat_normed = group_view(normed)
    members = H * gradient.shape[2] * (gradient.shape[3] // GROUPS)
    mean_grad, cross_grad = lax.psum(
        (jnp.sum(scaled, axis=(0, 2, 4)), jnp.sum(scaled * flat_normed, axis=(0, 2, 4))), "rows"
    )
    input_grad = (
        scaled - spread_back(mean_grad / members) - flat_normed * spread_back(cross_grad / members)
    ) * spread_back(factor)
    return (input_grad.reshape(gradient.shape), gain_grad, offset_grad)


def widen(tensor):
    return jnp.pad(tensor, ((0, 0), (0, 0), (1, 1), (0, 0)))


def conv_forward(tensor, kernel, offset):
    height, across = (tensor.shape[0], tensor.shape[2])
    padded = widen(padded_2(tensor, (("rows", 0),), 1))
    summed = jnp.zeros(tensor.shape[:3] + (kernel.shape[3],), jnp.float32)
    for row_off in range(3):
        for col_off in range(3):
            window = padded[row_off : row_off + height, :, col_off : col_off + across, :]
            summed = summed + jnp.einsum(
                "rbwc,cd->rbwd",
                window,
                kernel[row_off, col_off],
                preferred_element_type=jnp.float32,
            )
    return (summed + offset, padded)


def conv_backward(gradient, padded, kernel):
    height, across = (gradient.shape[0], gradient.shape[2])
    beside_all = widen(padded_2(gradient, (("rows", 0),), 1))
    input_grad = jnp.zeros(gradient.shape[:3] + (kernel.shape[2],), jnp.float32)
    tap_grads = []
    for row_off in range(3):
        for col_off in range(3):
            window = beside_all[
                2 - row_off : 2 - row_off + height, :, 2 - col_off : 2 - col_off + across, :
            ]
            input_grad = input_grad + jnp.einsum(
                "rbwd,cd->rbwc",
                window,
                kernel[row_off, col_off],
                preferred_element_type=jnp.float32,
            )
            source = padded[row_off : row_off + height, :, col_off : col_off + across, :]
            tap_grads.append(
                jnp.einsum("rbwc,rbwd->cd", source, gradient, preferred_element_type=jnp.float32)
            )
    kernel_grad = jnp.stack(tap_grads).reshape(kernel.shape)
    offset_grad = jnp.sum(gradient.astype(jnp.float32), axis=(0, 1, 2))
    return (input_grad, kernel_grad, offset_grad)


def linear(tensor, weight):
    return jnp.einsum("rbwc,cd->rbwd", tensor, weight, preferred_element_type=jnp.float32)


def back_linear(gradient, weight):
    return jnp.einsum("rbwd,cd->rbwc", gradient, weight, preferred_element_type=jnp.float32)


def weight_product(tensor, gradient):
    return jnp.einsum("rbwc,rbwd->cd", tensor, gradient, preferred_element_type=jnp.float32)


def image_to_sequence(tensor):
    height, images, across, channels = tensor.shape
    return tensor.transpose(1, 0, 2, 3).reshape(images, height * across, channels)


def from_sequence(sequence, height, across):
    images, length, channels = sequence.shape
    return sequence.reshape(images, height, across, channels).transpose(1, 0, 2, 3)


def reduce_all(gradients):
    flattened = jnp.concatenate([gradient.reshape(-1) for gradient in gradients])
    length = flattened.shape[0]
    devices = lax.axis_size("rows") * lax.axis_size("imgs")
    per_share = -(-length // (devices * 128)) * 128
    padded_len = per_share * devices
    strided = jnp.pad(flattened, (0, padded_len - length)).reshape(per_share, devices).T
    packed = strided.reshape(padded_len // 128, 128)
    my_share = lax.psum_scatter(packed, ("rows", "imgs"), scatter_dimension=0, tiled=True)
    summed_all = lax.all_gather(
        my_share.astype(jnp.bfloat16), ("rows", "imgs"), axis=0, tiled=True
    ).astype(my_share.dtype)
    summed_all = summed_all.reshape(devices, per_share).T.reshape(-1)
    results = []
    offset_at = 0
    for gradient in gradients:
        results.append(summed_all[offset_at : offset_at + gradient.size].reshape(gradient.shape))
        offset_at = offset_at + gradient.size
    return results


def per_device_by_rows(
    features,
    cotangent,
    norm1_gain,
    norm1_shift,
    conv1_kernel,
    conv1_shift,
    norm2_gain,
    norm2_shift,
    conv2_kernel,
    conv2_shift,
    norm3_gain,
    norm3_shift,
    query_weight,
    query_shift,
    key_weight,
    value_weight,
    value_shift,
    out_weight,
    out_shift,
):
    height, images, across, channels = features.shape
    attention_score_scale = 1.0 / math.sqrt(channels)
    inputs = features.astype(jnp.float32)
    norm_one, normed_one, factor_one = norm_forward(inputs, norm1_gain, norm1_shift)
    act_one, slope_one = sigmoid_pair(norm_one)
    conv_one, padded_one = conv_forward(act_one.astype(jnp.bfloat16), conv1_kernel, conv1_shift)
    norm_two, normed_two, factor_two = norm_forward(conv_one, norm2_gain, norm2_shift)
    act_two, slope_two = sigmoid_pair(norm_two)
    conv_two, padded_two = conv_forward(act_two.astype(jnp.bfloat16), conv2_kernel, conv2_shift)
    residual = inputs + conv_two
    norm_three, normed_three, factor_three = norm_forward(residual, norm3_gain, norm3_shift)
    attend_input = norm_three.astype(jnp.bfloat16)
    query_rows = (linear(attend_input, query_weight) + query_shift).astype(jnp.bfloat16)
    key_state_rows = linear(attend_input, key_weight).astype(jnp.bfloat16)
    value_state_rows = (linear(attend_input, value_weight) + value_shift).astype(jnp.bfloat16)
    all_keys, all_values = (
        lax.all_gather(key_state_rows, "rows", axis=0, tiled=True),
        lax.all_gather(value_state_rows, "rows", axis=0, tiled=True),
    )
    query_sequence = image_to_sequence(query_rows)
    key_sequence = image_to_sequence(all_keys)
    value_sequence = image_to_sequence(all_values)
    attention_scores = (
        jnp.einsum("xao,xno->xan", query_sequence, key_sequence, preferred_element_type=jnp.float32)
        * attention_score_scale
    )
    row_peak = jnp.max(attention_scores, axis=-1, keepdims=True)
    log_total = row_peak + jnp.log(
        jnp.sum(jnp.exp(attention_scores - row_peak), axis=-1, keepdims=True)
    )
    weight_tensors = jnp.exp(attention_scores - log_total).astype(jnp.bfloat16)
    attended_seq = jnp.einsum(
        "afj,ajy->afy", weight_tensors, value_sequence, preferred_element_type=jnp.float32
    )
    attention_output = from_sequence(attended_seq.astype(jnp.bfloat16), height, across)
    output = residual + linear(attention_output, out_weight) + out_shift
    out_shift_grad = jnp.sum(cotangent.astype(jnp.float32), axis=(0, 1, 2))
    out_weight_grad = weight_product(attention_output, cotangent)
    mixed_grad = back_linear(cotangent, out_weight).astype(jnp.bfloat16)
    mixed_sequence = image_to_sequence(mixed_grad)
    scores_again = (
        jnp.einsum("xao,xno->xan", query_sequence, key_sequence, preferred_element_type=jnp.float32)
        * attention_score_scale
    )
    probabilities = jnp.exp(scores_again - log_total)
    probability_gradient = jnp.einsum(
        "xao,xno->xan", mixed_sequence, value_sequence, preferred_element_type=jnp.float32
    )
    delta = jnp.sum(probabilities * probability_gradient, axis=-1, keepdims=True)
    score_gradient = (probabilities * (probability_gradient - delta)).astype(jnp.bfloat16)
    query_local = (
        jnp.einsum("afj,ajy->afy", score_gradient, key_sequence, preferred_element_type=jnp.float32)
        * attention_score_scale
    )
    query_grad = from_sequence(query_local, height, across).astype(jnp.bfloat16)
    key_full = (
        jnp.einsum(
            "svt,svz->stz", score_gradient, query_sequence, preferred_element_type=jnp.float32
        )
        * attention_score_scale
    )
    value_full = jnp.einsum(
        "svt,svz->stz",
        probabilities.astype(jnp.bfloat16),
        mixed_sequence,
        preferred_element_type=jnp.float32,
    )
    stacked = from_sequence(jnp.concatenate([key_full, value_full], axis=-1), H, across)
    own_grads = lax.psum_scatter(
        stacked.astype(jnp.bfloat16), "rows", scatter_dimension=0, tiled=True
    ).astype(jnp.float32)
    key_grad = own_grads[..., :channels].astype(jnp.bfloat16)
    value_grad = own_grads[..., channels:].astype(jnp.bfloat16)
    query_weight_grad = weight_product(attend_input, query_grad)
    query_shift_grad = jnp.sum(query_grad.astype(jnp.float32), axis=(0, 1, 2))
    key_weight_grad = weight_product(attend_input, key_grad)
    value_weight_grad = weight_product(attend_input, value_grad)
    value_shift_grad = jnp.sum(value_grad.astype(jnp.float32), axis=(0, 1, 2))
    attend_grad = (
        back_linear(query_grad, query_weight)
        + back_linear(key_grad, key_weight)
        + back_linear(value_grad, value_weight)
    )
    resid_part, norm3_gain_grad, norm3_shift_grad = norm_backward(
        attend_grad, normed_three, factor_three, norm3_gain
    )
    resid_grad = cotangent.astype(jnp.float32) + resid_part
    conv_two_in, conv2_kernel_grad, conv2_shift_grad = conv_backward(
        resid_grad.astype(jnp.bfloat16), padded_two, conv2_kernel
    )
    conv_one_out, norm2_gain_grad, norm2_shift_grad = norm_backward(
        conv_two_in * slope_two, normed_two, factor_two, norm2_gain
    )
    conv_one_in, conv1_kernel_grad, conv1_shift_grad = conv_backward(
        conv_one_out.astype(jnp.bfloat16), padded_one, conv1_kernel
    )
    inputs_part, norm1_gain_grad, norm1_shift_grad = norm_backward(
        conv_one_in * slope_one, normed_one, factor_one, norm1_gain
    )
    features_grad = resid_grad + inputs_part
    reduced = reduce_all(
        [
            norm1_gain_grad,
            norm1_shift_grad,
            conv1_kernel_grad,
            conv1_shift_grad,
            norm2_gain_grad,
            norm2_shift_grad,
            conv2_kernel_grad,
            conv2_shift_grad,
            norm3_gain_grad,
            norm3_shift_grad,
            query_weight_grad,
            query_shift_grad,
            key_weight_grad,
            value_weight_grad,
            value_shift_grad,
            out_weight_grad,
            out_shift_grad,
        ]
    )
    return (output, features_grad) + tuple(reduced)


F32 = jnp.float32
BF16 = jnp.bfloat16
AXES = ("rows", "imgs")
MEGA = 1024 * 1024
TILE = 64
MM_TILE = 256
ACROSS = 32
WEIGHT = 4
FORWARD_LIMIT = 24
ATTEND_LIMIT = 28
PLAN = (
    ("W2", ""),
    ("D2", "B"),
    ("W1", ""),
    ("O", "C"),
    ("D1", "BO"),
    ("", "CBSO"),
    ("", "CBSGO"),
    ("", "CBSG"),
    ("", "CBSG"),
    ("", "CBS"),
    ("", "CB"),
    ("", "CB"),
    ("", "BC"),
    ("", "C"),
)
STEPS = ("core", "plane_a", "plane_b", "near", "far")
VMEM = pl.BlockSpec(memory_space=pltpu.VMEM)
SMEM = pl.BlockSpec(memory_space=pltpu.SMEM)
HBM = pl.BlockSpec(memory_space=pltpu.HBM)


def shape_of(shape, dtype):
    return jax.ShapeDtypeStruct(shape, dtype)


def kernel_call(body, out_shape, in_specs, scratch=(), limit=24, flops=0, moved=0):
    return pl.pallas_call(
        body,
        out_shape=out_shape,
        in_specs=in_specs,
        out_specs=jax.tree.map(lambda _: VMEM, out_shape),
        scratch_shapes=list(scratch),
        compiler_params=pltpu.CompilerParams(vmem_limit_bytes=limit * MEGA),
        cost_estimate=pl.CostEstimate(
            flops=WEIGHT * flops, bytes_accessed=WEIGHT * moved, transcendentals=0
        ),
    )


def tiles(total, size, body):
    def step(index, carry):
        body(pl.multiple_of(index * size, size))
        return carry

    lax.fori_loop(0, total // size, step, 0)


def fold_tiles(total, size, body, carry):
    def step(index, held):
        return body(pl.multiple_of(index * size, size), held)

    return lax.fori_loop(0, total // size, step, carry)


def fold_rows(tensor):
    return jnp.sum(tensor.reshape(tensor.shape[0] // 8, 8, tensor.shape[1]), axis=0)


def column(partial):
    return jnp.sum(partial, axis=0, keepdims=True)


def group_mean(column_sum, members):
    channels = column_sum.shape[1]
    size = channels // GROUPS
    one = lax.broadcasted_iota(jnp.int32, (channels, channels), 0) // size
    two = lax.broadcasted_iota(jnp.int32, (channels, channels), 1) // size
    same = jnp.where(one == two, 1.0, 0.0).astype(F32)
    summed = jnp.dot(
        jnp.broadcast_to(column_sum, (8, channels)),
        same,
        precision=lax.Precision.HIGHEST,
        preferred_element_type=F32,
    )
    return summed[:1] * (1.0 / members)


def norm_stats(read, total, channels):
    members = total * (channels // GROUPS)
    zero = jnp.zeros((8, channels), F32)
    sums = fold_tiles(total, TILE, lambda at, held: held + fold_rows(read(at)), zero)
    centre = group_mean(column(sums), members)
    squares = fold_tiles(
        total, TILE, lambda at, held: held + fold_rows(jnp.square(read(at) - centre)), zero
    )
    return centre, lax.rsqrt(group_mean(column(squares), members) + EPSILON)


def fill_shifted(cat_ref, at, tile):
    size, channels = tile.shape
    place = lax.broadcasted_iota(jnp.int32, tile.shape, 0) % ACROSS
    before = jnp.where(place == 0, 0.0, pltpu.roll(tile, 1, 0))
    after = jnp.where(place == ACROSS - 1, 0.0, pltpu.roll(tile, size - 1, 0))
    rows = pl.ds(pl.multiple_of(ACROSS + at, ACROSS), size)
    cat_ref[rows, 0:channels] = before.astype(BF16)
    cat_ref[rows, channels : 2 * channels] = tile.astype(BF16)
    cat_ref[rows, 2 * channels : 3 * channels] = after.astype(BF16)


def clear_border(cat_ref):
    total, width = cat_ref.shape
    cat_ref[0:ACROSS, :] = jnp.zeros((ACROSS, width), BF16)
    cat_ref[total - ACROSS : total, :] = jnp.zeros((ACROSS, width), BF16)


def window_product(cat_ref, weight_ref, at, size):
    total = None
    for row_off in range(3):
        rows = pl.ds(pl.multiple_of(at + row_off * ACROSS, ACROSS), size)
        part = jnp.dot(cat_ref[rows, :], weight_ref[row_off], preferred_element_type=F32)
        total = part if total is None else total + part
    return total


def window_product_turned(cat_ref, weight_ref, at, size):
    channels = weight_ref.shape[2]
    total = None
    for row_off in range(3):
        rows = pl.ds(pl.multiple_of(at + (2 - row_off) * ACROSS, ACROSS), size)
        for col_off in range(3):
            low = (2 - col_off) * channels
            tap = weight_ref[row_off, col_off * channels : (col_off + 1) * channels, :]
            part = dot_t(cat_ref[rows, low : low + channels], tap)
            total = part if total is None else total + part
    return total


def dot_t(left, right):
    return lax.dot_general(left, right, (((1,), (1,)), ((), ())), preferred_element_type=F32)


def t_dot(left, right):
    return lax.dot_general(left, right, (((0,), (0,)), ((), ())), preferred_element_type=F32)


def dot(left, right):
    return jnp.dot(left, right, preferred_element_type=F32)


def line(lines_ref, row):
    return lines_ref[row : row + 1, :]


def forward_body(place_ref, *refs):
    pieces = refs[:8]
    (lines_ref, weight1_ref, weight2_ref, q_weight_ref, k_weight_ref, v_weight_ref,
     image_ref, act1_ref, conv_ref, act2_ref, resid_ref, stats_ref, norm_ref, q_ref, k_ref, v_ref,
     cat_ref) = refs[8:]
    total, channels = image_ref.shape
    share = total // 8
    me = place_ref[0]
    for index in range(8):
        at = pl.multiple_of((me ^ index) * share, share)
        image_ref[pl.ds(at, share), :] = pieces[index][...]
    clear_border(cat_ref)

    def activate_all(read, stats_row, gain_row, act_ref):
        centre, factor = norm_stats(read, total, channels)
        stats_ref[stats_row : stats_row + 1, :] = centre
        stats_ref[stats_row + 1 : stats_row + 2, :] = factor
        gain, shift = line(lines_ref, gain_row), line(lines_ref, gain_row + 1)

        def activate(at):
            held = (read(at) - centre) * factor * gain + shift
            act = held * jax.nn.sigmoid(held)
            act_ref[pl.ds(at, TILE), :] = act.astype(BF16)
            fill_shifted(cat_ref, at, act)

        tiles(total, TILE, activate)

    def read_image(at):
        return image_ref[pl.ds(at, TILE), :].astype(F32)

    activate_all(read_image, 0, 0, act1_ref)
    bias1 = line(lines_ref, 6)

    def convolve1(at):
        conv_ref[pl.ds(at, MM_TILE), :] = window_product(cat_ref, weight1_ref, at, MM_TILE) + bias1

    tiles(total, MM_TILE, convolve1)
    activate_all(lambda at: conv_ref[pl.ds(at, TILE), :], 2, 2, act2_ref)
    bias2 = line(lines_ref, 7)

    def convolve2(at):
        rows = pl.ds(at, MM_TILE)
        resid_ref[rows, :] = (
            window_product(cat_ref, weight2_ref, at, MM_TILE)
            + bias2
            + image_ref[rows, :].astype(F32)
        )

    tiles(total, MM_TILE, convolve2)
    centre3, factor3 = norm_stats(lambda at: resid_ref[pl.ds(at, TILE), :], total, channels)
    stats_ref[4:5, :] = centre3
    stats_ref[5:6, :] = factor3
    stats_ref[6:8, :] = jnp.zeros((2, channels), F32)
    gain3, shift3 = line(lines_ref, 4), line(lines_ref, 5)
    q_shift, v_shift = line(lines_ref, 8), line(lines_ref, 9)

    def project(at):
        rows = pl.ds(at, MM_TILE)
        held = ((resid_ref[rows, :] - centre3) * factor3 * gain3 + shift3).astype(BF16)
        norm_ref[rows, :] = held
        q_ref[rows, :] = (dot(held, q_weight_ref[...]) + q_shift).astype(BF16)
        k_ref[rows, :] = dot(held, k_weight_ref[...]).astype(BF16)
        v_ref[rows, :] = (dot(held, v_weight_ref[...]) + v_shift).astype(BF16)

    tiles(total, MM_TILE, project)


def z_bits(core):
    return 2 << core, 4 >> core


def return_pieces(place_ref, out_ref, sent_ref, kept_ref):
    share = out_ref.shape[0] // 8
    me, core = place_ref[0], place_ref[1]
    for target, side in ((kept_ref, 0), (sent_ref, 1)):
        first, second = z_bits(core if side == 0 else 1 - core)
        for index in range(4):
            offset = side + (index // 2) * first + (index % 2) * second
            at = pl.multiple_of((me ^ offset) * share, share)
            target[index] = out_ref[pl.ds(at, share), :]


def attention_body(place_ref, *refs):
    cot_pieces = refs[:4]
    (q_ref, k_ref, v_ref, norm_ref, resid_ref, stats_ref, lines_ref,
     o_weight_ref, q_weight_ref, k_weight_ref, v_weight_ref) = refs[4:15]
    (out_sent_ref, out_kept_ref, sent_ref, kept_ref, small_ref, d_resid_ref, d_conv_ref,
     cot_ref, out_ref, mixed_ref, d_q_ref, d_k_acc, d_v_acc, d_k_ref, d_v_ref) = refs[15:]
    total, channels = q_ref.shape
    share = total // 8
    scale = 1.0 / math.sqrt(channels)
    me = place_ref[0]
    for index in range(8):
        at = pl.multiple_of((me ^ index) * share, share)
        cot_ref[pl.ds(at, share), :] = cot_pieces[index // 2][index % 2]
    o_shift = line(lines_ref, 10)
    d_k_acc[...] = jnp.zeros(d_k_acc.shape, F32)
    d_v_acc[...] = jnp.zeros(d_v_acc.shape, F32)


    def attend(at):
        rows = pl.ds(at, MM_TILE)
        query = q_ref[rows, :]
        scores = dot_t(query, k_ref[...]) * scale
        exps = jnp.exp(scores - jnp.max(scores, axis=-1, keepdims=True))
        probs = exps * (1.0 / jnp.sum(exps, axis=-1, keepdims=True))
        weights = probs.astype(BF16)
        mixed = dot(weights, v_ref[...]).astype(BF16)
        mixed_ref[rows, :] = mixed
        out_ref[rows, :] = (
            resid_ref[rows, :] + dot(mixed, o_weight_ref[...]) + o_shift
        ).astype(BF16)
        d_mixed = dot_t(cot_ref[rows, :], o_weight_ref[...]).astype(BF16)
        d_prob = dot_t(d_mixed, v_ref[...])
        delta = jnp.sum(probs * d_prob, axis=-1, keepdims=True)
        d_scores = (probs * (d_prob - delta)).astype(BF16)
        d_q_ref[rows, :] = (dot(d_scores, k_ref[...]) * scale).astype(BF16)
        d_k_acc[...] += t_dot(d_scores, query)
        d_v_acc[...] += t_dot(weights, d_mixed)

    tiles(total, MM_TILE, attend)
    return_pieces(place_ref, out_ref, out_sent_ref, out_kept_ref)
    d_k_ref[...] = (d_k_acc[...] * scale).astype(BF16)
    d_v_ref[...] = d_v_acc[...].astype(BF16)
    half = channels // 2
    core = place_ref[1]
    for index, (left, right) in enumerate(
        ((norm_ref, d_q_ref), (norm_ref, d_k_ref), (norm_ref, d_v_ref), (mixed_ref, cot_ref))
    ):
        for target, part in ((sent_ref, 1 - core), (kept_ref, core)):
            lanes = pl.ds(pl.multiple_of(part * half, half), half)
            target[index] = t_dot(left[:, lanes], right[...]).astype(BF16)

    def back(at):
        rows = pl.ds(at, MM_TILE)
        d_resid_ref[rows, :] = (
            dot_t(d_q_ref[rows, :], q_weight_ref[...])
            + dot_t(d_k_ref[rows, :], k_weight_ref[...])
            + dot_t(d_v_ref[rows, :], v_weight_ref[...])
        )

    tiles(total, MM_TILE, back)
    centre, factor = stats_ref[4:5, :], stats_ref[5:6, :]
    gain = line(lines_ref, 4)
    zero = jnp.zeros((8, channels), F32)

    def gather(at, held):
        rows = pl.ds(at, TILE)
        grad = d_resid_ref[rows, :]
        normed = (resid_ref[rows, :] - centre) * factor
        return (
            held[0] + fold_rows(grad),
            held[1] + fold_rows(grad * normed),
            held[2] + fold_rows(cot_ref[rows, :].astype(F32)),
            held[3] + fold_rows(d_q_ref[rows, :].astype(F32)),
            held[4] + fold_rows(d_v_ref[rows, :].astype(F32)),
        )

    sums = fold_tiles(total, TILE, gather, (zero,) * 5)
    shift_grad, gain_grad, o_shift_grad, q_shift_grad, v_shift_grad = [column(s) for s in sums]
    members = total * (channels // GROUPS)
    mean_grad = group_mean(shift_grad * gain, members)
    cross_grad = group_mean(gain_grad * gain, members)

    def finish(at, held):
        rows = pl.ds(at, TILE)
        normed = (resid_ref[rows, :] - centre) * factor
        grad = cot_ref[rows, :].astype(F32) + factor * (
            d_resid_ref[rows, :] * gain - mean_grad - normed * cross_grad
        )
        d_resid_ref[rows, :] = grad
        rounded = grad.astype(BF16)
        d_conv_ref[rows, :] = rounded
        return held + fold_rows(rounded.astype(F32))

    conv_shift_grad = column(fold_tiles(total, TILE, finish, zero))
    small_ref[0:1, :] = gain_grad
    small_ref[1:2, :] = shift_grad
    small_ref[2:3, :] = q_shift_grad
    small_ref[3:4, :] = v_shift_grad
    small_ref[4:5, :] = o_shift_grad
    small_ref[5:6, :] = conv_shift_grad
    small_ref[6:8, :] = jnp.zeros((2, channels), F32)


def kernel_grad_body(extra, place_ref, act_ref, grad_ref, *refs):
    more, refs = (refs[:2], refs[2:]) if extra else ((), refs)
    sent_ref, kept_ref, cat_ref, turned_ref = refs
    total, channels = act_ref.shape
    for source, target in zip(more, (sent_ref, kept_ref)):
        for index in range(extra):
            target[9 + index] = source[index]
    half = channels // 2
    clear_border(cat_ref)

    def fill(at):
        fill_shifted(cat_ref, at, grad_ref[pl.ds(at, TILE), :].astype(F32))

    tiles(total, TILE, fill)
    turned_ref[...] = act_ref[...].T
    core = place_ref[1]
    for target, part in ((sent_ref, 1 - core), (kept_ref, core)):
        rows = pl.ds(pl.multiple_of(part * half, half), half)
        for row_off in range(3):
            first = (2 - row_off) * ACROSS
            product = dot(turned_ref[rows, :], cat_ref[first : first + total, :]).astype(BF16)
            for col_off in range(3):
                low = (2 - col_off) * channels
                target[row_off * 3 + col_off] = product[:, low : low + channels]


def input_grad_body(with_rest, stats_row, place_ref, *refs):
    grad_ref, weight_ref, source_ref, stats_ref, lines_ref = refs[:5]
    rest_ref = refs[5] if with_rest else None
    refs = refs[6:] if with_rest else refs[5:]
    if with_rest:
        sent_ref, kept_ref, small_ref, cat_ref, held_ref, out_ref = refs
    else:
        out_ref, small_ref, cat_ref, held_ref = refs
    total, channels = grad_ref.shape
    centre = stats_ref[stats_row : stats_row + 1, :]
    factor = stats_ref[stats_row + 1 : stats_row + 2, :]
    gain, shift = line(lines_ref, stats_row), line(lines_ref, stats_row + 1)
    clear_border(cat_ref)

    def fill(at):
        fill_shifted(cat_ref, at, grad_ref[pl.ds(at, TILE), :].astype(F32))

    tiles(total, TILE, fill)

    def product(at):
        held_ref[pl.ds(at, MM_TILE), :] = window_product_turned(cat_ref, weight_ref, at, MM_TILE)

    tiles(total, MM_TILE, product)
    zero = jnp.zeros((8, channels), F32)

    def slope(at, held):
        rows = pl.ds(at, TILE)
        normed = (source_ref[rows, :].astype(F32) - centre) * factor
        pre = normed * gain + shift
        logistic = jax.nn.sigmoid(pre)
        grad = held_ref[rows, :] * (logistic * (1.0 + pre * (1.0 - logistic)))
        held_ref[rows, :] = grad
        return held[0] + fold_rows(grad), held[1] + fold_rows(grad * normed)

    shift_sum, gain_sum = fold_tiles(total, TILE, slope, (zero, zero))
    shift_grad, gain_grad = column(shift_sum), column(gain_sum)
    members = total * (channels // GROUPS)
    mean_grad = group_mean(shift_grad * gain, members)
    cross_grad = group_mean(gain_grad * gain, members)

    def finish(at, held):
        rows = pl.ds(at, TILE)
        normed = (source_ref[rows, :].astype(F32) - centre) * factor
        grad = factor * (held_ref[rows, :] * gain - mean_grad - normed * cross_grad)
        if with_rest:
            grad = grad + rest_ref[rows, :]
        rounded = grad.astype(BF16)
        out_ref[rows, :] = rounded
        return held + fold_rows(rounded.astype(F32))

    out_sum = column(fold_tiles(total, TILE, finish, zero))
    small_ref[0:1, :] = gain_grad
    small_ref[1:2, :] = shift_grad
    small_ref[2:3, :] = out_sum
    small_ref[3:8, :] = jnp.zeros((5, channels), F32)
    if with_rest:
        return_pieces(place_ref, out_ref, sent_ref, kept_ref)


def pack_body(place_ref, block_ref, *piece_refs):
    me = place_ref[0]
    for index in range(8):
        for row in range(block_ref.shape[0]):
            piece_refs[index][pl.ds(row * ACROSS, ACROSS), :] = block_ref[row, me ^ index]


def pack(place, block):
    rows, _, across, channels = block.shape
    piece = shape_of((rows * across, channels), BF16)
    return kernel_call(pack_body, [piece] * 8, [SMEM, VMEM], limit=8, moved=2 * MEGA)(place, block)


def pack_by_core_body(place_ref, block_ref, sent_ref, kept_ref):
    me = place_ref[0]
    for target, side in ((kept_ref, 0), (sent_ref, 1)):
        for index in range(4):
            for row in range(block_ref.shape[0]):
                rows = pl.ds(row * ACROSS, ACROSS)
                target[index, rows, :] = block_ref[row, me ^ (2 * index + side)]


def pair_body(place_ref, kept_ref, got_ref, *pair_refs):
    for index in range(4):
        pair_refs[index][0] = kept_ref[index]
        pair_refs[index][1] = got_ref[index]


def swap_by_core(place, block):
    rows, _, across, channels = block.shape
    four = shape_of((4, rows * across, channels), BF16)
    sent, kept = kernel_call(
        pack_by_core_body, [four] * 2, [SMEM, VMEM], limit=8, moved=2 * MEGA
    )(place, block)
    got = exchange(sent, "core")
    pair = shape_of((2, rows * across, channels), BF16)
    return kernel_call(
        pair_body, [pair] * 4, [SMEM, VMEM, VMEM], limit=8, moved=2 * MEGA
    )(place, kept, got)


def swap_pieces(pieces, unit):
    count = len(pieces)
    return [pieces[0]] + [
        lax.ppermute(pieces[k], "rows", [(r, r ^ (unit * k)) for r in range(count * unit)])
        for k in range(1, count)
    ]


def stage_body(place_ref, *refs):
    count = (len(refs) - 1) // 2
    sems = refs[-1]
    copies = [
        pltpu.make_async_copy(refs[index], refs[count + index], sems.at[index])
        for index in range(count)
    ]
    for copy in copies:
        copy.start()
    for copy in copies:
        copy.wait()


def stage(place, arrays):
    return kernel_call(
        stage_body, [shape_of(a.shape, a.dtype) for a in arrays], [SMEM] + [HBM] * len(arrays),
        [pltpu.SemaphoreType.DMA((len(arrays),))], limit=16, moved=12 * MEGA,
    )(place, *arrays)


def partner_table(kind):
    table = []
    for row in range(8):
        for img in range(4):
            core = row & 1
            if kind == "core":
                other = (row ^ 1, img)
            elif kind == "near":
                other = (row ^ (4 if core else 2), img)
            elif kind == "far":
                other = (row ^ (2 if core else 4), img)
            elif kind == "plane_a":
                other = (row, img ^ (2 if core else 1))
            else:
                other = (row, img ^ (1 if core else 2))
            table.append((row * 4 + img, other[0] * 4 + other[1]))
    return table


def exchange(tensor, kind):
    return lax.ppermute(tensor, AXES, partner_table(kind))


def own_place():
    row, img = lax.axis_index("rows"), lax.axis_index("imgs")
    core, near, far = row & 1, (row >> 1) & 1, (row >> 2) & 1
    low, high = img & 1, (img >> 1) & 1
    plane_a = jnp.where(core == 1, high, low)
    plane_b = jnp.where(core == 1, low, high)
    first_z = jnp.where(core == 1, far, near)
    second_z = jnp.where(core == 1, near, far)
    return jnp.stack([row, core, plane_a, plane_b, first_z, second_z, row, row]).astype(jnp.int32)


def add_split(slot, place_ref, ins, outs):
    kept_ref, got_ref = ins
    count, rows, _ = kept_ref.shape
    half = rows // 2
    bit = place_ref[slot]

    def one(index, carry):
        for target, part in zip(outs, (1 - bit, bit)):
            span = pl.ds(pl.multiple_of(part * half, half), half)
            target[index] = (
                kept_ref[index, span, :].astype(F32) + got_ref[index, span, :].astype(F32)
            ).astype(BF16)
        return carry

    lax.fori_loop(0, count, one, 0)


def add_last(slot, place_ref, ins, outs):
    outs[0][...] = (ins[0][...].astype(F32) + ins[1][...].astype(F32)).astype(BF16)


def join(slot, place_ref, ins, outs):
    count, rows, _ = ins[0].shape
    bit = place_ref[slot]

    def one(index, carry):
        for source, part in zip(ins, (bit, 1 - bit)):
            span = pl.ds(pl.multiple_of(part * rows, rows), rows)
            outs[0][index, span, :] = source[index]
        return carry

    lax.fori_loop(0, count, one, 0)


def add_rows(slot, place_ref, ins, outs):
    outs[0][...] = ins[0][...] + ins[1][...]


def turn_pairs(slot, place_ref, ins, outs):
    kept_ref, got_ref = ins
    for target, part in zip(outs, (1, 0)):
        for index in range(2):
            if slot == 0:
                target[index] = kept_ref[2 * part + index]
                target[2 + index] = got_ref[2 * part + index]
            else:
                target[index] = kept_ref[2 * index + part]
                target[2 + index] = got_ref[2 * index + part]


def spread(slot, place_ref, ins, outs):
    me, core = place_ref[0], place_ref[1]
    first, second = z_bits(core)
    out_ref = outs[0]
    for source, side in zip(ins, (0, 1)):
        for index in range(4):
            image = me ^ ((index % 2) + (index // 2) * first + side * second)
            for row in range(out_ref.shape[0]):
                rows = pl.ds(row * ACROSS, ACROSS)
                out_ref[row, image] = source[index, rows, :].astype(F32)


def join_last(place, mine, got, start, count):
    _, rows, channels = mine.shape

    def body(place_ref, mine_ref, got_ref, out_ref):
        core = place_ref[1]
        for source, part in ((mine_ref, core), (got_ref, 1 - core)):
            span = pl.ds(pl.multiple_of(part * rows, rows), rows)
            out_ref[0, span, :] = source[0].astype(F32)

    moved = 12 * count * rows * channels
    return pl.pallas_call(
        body,
        grid=(count,),
        out_shape=shape_of((count, 2 * rows, channels), F32),
        in_specs=[
            SMEM,
            pl.BlockSpec((1, rows, channels), lambda i: (i + start, 0, 0)),
            pl.BlockSpec((1, rows, channels), lambda i: (i + start, 0, 0)),
        ],
        out_specs=pl.BlockSpec((1, 2 * rows, channels), lambda i: (i, 0, 0)),
        compiler_params=pltpu.CompilerParams(vmem_limit_bytes=10 * MEGA),
        cost_estimate=pl.CostEstimate(
            flops=0, bytes_accessed=WEIGHT * moved, transcendentals=0
        ),
    )(place, mine, got)


def after(values, token):
    tied = lax.optimization_barrier(tuple(values) + (token,))
    return tied[:-1]


class SumChain:
    def __init__(self, sent, kept):
        self.kept, self.at = kept, 0
        self.got = exchange(sent, "core")

    def todo(self):
        count, rows, channels = self.kept.shape
        at = self.at
        if at < 4:
            half = shape_of((count, rows // 2, channels), BF16)
            return add_split, at + 2, [half, half]
        if at == 4:
            return add_last, 0, [shape_of(self.kept.shape, BF16)]
        if at < 9:
            return join, 10 - at, [shape_of((count, 2 * rows, channels), BF16)]
        return None

    def take(self, outs):
        at = self.at
        self.at += 1
        self.kept = outs[-1]
        if at < 4:
            self.got = exchange(outs[0], STEPS[at + 1])
        else:
            self.got = exchange(outs[0], STEPS[8 - at])


class RowChain:
    def __init__(self, rows):
        self.kept, self.at = rows, 0
        self.got = exchange(rows, STEPS[0])

    def todo(self):
        return add_rows, 0, [shape_of(self.kept.shape, F32)]

    def take(self, outs):
        self.kept = outs[0]
        self.at += 1
        if self.at < len(STEPS):
            self.got = exchange(self.kept, STEPS[self.at])


class ReturnChain:
    def __init__(self, sent, kept, block_shape):
        self.kept, self.at, self.block_shape = kept, 0, block_shape
        self.got = exchange(sent, "core")

    def todo(self):
        if self.at < 2:
            return turn_pairs, self.at, [shape_of(self.kept.shape, BF16)] * 2
        return spread, 0, [shape_of(self.block_shape, F32)]

    def take(self, outs):
        self.kept = outs[-1]
        if self.at < 2:
            self.got = exchange(outs[0], ("near", "far")[self.at])
        self.at += 1


def step_all(place, chains, token):
    todos = [chain.todo() for chain in chains]
    arrays = after([a for chain in chains for a in (chain.kept, chain.got)], token)
    shapes = [shape for _, _, outs in todos for shape in outs]

    def body(place_ref, *refs):
        ins, outs = refs[: len(arrays)], refs[len(arrays) :]
        for number, (work, slot, shapes) in enumerate(todos):
            work(slot, place_ref, ins[2 * number : 2 * number + 2], outs[: len(shapes)])
            outs = outs[len(shapes) :]

    moved = 2 * sum(a.size * a.dtype.itemsize for a in arrays)
    results = kernel_call(
        body, shapes, [SMEM] + [VMEM] * len(arrays), limit=4 + 2 * moved // MEGA, moved=moved
    )(place, *arrays)
    token = results[0]
    for chain, (_, _, outs) in zip(chains, todos):
        chain.take(results[: len(outs)])
        results = results[len(outs) :]
    return token


def per_device_by_images(
    features,
    cotangent,
    norm1_gain,
    norm1_shift,
    conv1_kernel,
    conv1_shift,
    norm2_gain,
    norm2_shift,
    conv2_kernel,
    conv2_shift,
    norm3_gain,
    norm3_shift,
    query_weight,
    query_shift,
    key_weight,
    value_weight,
    value_shift,
    out_weight,
    out_shift,
):
    rows, images, across, channels = features.shape
    total = rows * images * across
    place = own_place()
    lines = jnp.stack([
        norm1_gain, norm1_shift, norm2_gain, norm2_shift, norm3_gain, norm3_shift,
        conv1_shift, conv2_shift, query_shift, value_shift, out_shift, out_shift,
    ] + [out_shift] * 4)

    image = shape_of((total, channels), BF16)
    image_f32 = shape_of((total, channels), F32)
    piece = shape_of((total // 8, channels), BF16)
    stats_shape = shape_of((8, channels), F32)
    cat = pltpu.VMEM((total + 2 * across, 3 * channels), BF16)
    bf16_image = pltpu.VMEM((total, channels), BF16)
    f32_image = pltpu.VMEM((total, channels), F32)
    tall = (3, 3 * channels, channels)
    linear_flops = 2 * total * channels * channels

    feature_sent = pack(place, features)
    feature_pieces = swap_pieces(feature_sent, 1)
    cot_pairs = swap_by_core(place, after((cotangent,), feature_sent[0])[0])
    weight1, weight2, q_weight, k_weight, v_weight, o_weight = stage(place, after(
        (conv1_kernel.reshape(tall), conv2_kernel.reshape(tall), query_weight, key_weight,
         value_weight, out_weight), cot_pairs[0]))
    cot_pieces = swap_pieces(after(cot_pairs, feature_pieces[7]), 2)

    (image_in, act_one, conv_one, act_two, residual, stats, normed, query, key, value) = kernel_call(
        forward_body,
        [image, image, image_f32, image, image_f32, stats_shape] + [image] * 4,
        [SMEM] + [VMEM] * 14,
        [cat],
        limit=FORWARD_LIMIT,
        flops=21 * linear_flops,
        moved=24 * MEGA,
    )(place, *feature_pieces, lines, weight1, weight2, q_weight, k_weight, v_weight)
    four = shape_of((4, total // 8, channels), BF16)
    halves = shape_of((4, channels // 2, channels), BF16)
    out_sent, out_kept, linear_sent, linear_kept, small_three, d_resid, d_conv_two = kernel_call(
        attention_body,
        [four, four, halves, halves, stats_shape, image_f32, image],
        [SMEM] + [VMEM] * 15,
        [bf16_image] * 4 + [f32_image] * 2 + [bf16_image] * 2,
        limit=ATTEND_LIMIT,
        flops=21 * linear_flops,
        moved=16 * MEGA,
    )(
        place, *cot_pieces, query, key, value, normed, residual, stats, lines,
        o_weight, q_weight, k_weight, v_weight,
    )

    def kernel_grad(act, grad, *more):
        extra = more[0].shape[0] if more else 0
        part = shape_of((9 + extra, channels // 2, channels), BF16)
        return kernel_call(
            lambda *refs: kernel_grad_body(extra, *refs), [part, part],
            [SMEM] + [VMEM] * (2 + len(more)),
            [cat, pltpu.VMEM((channels, total), BF16)],
            limit=12 + 2 * extra, flops=9 * linear_flops, moved=8 * MEGA,
        )(place, act, grad, *more)

    def second_input_grad(grad):
        return kernel_call(
            lambda *refs: input_grad_body(False, 2, *refs), [image, stats_shape],
            [SMEM] + [VMEM] * 5, [cat, f32_image],
            limit=16, flops=9 * linear_flops, moved=10 * MEGA,
        )(place, grad, weight2, conv_one, stats, lines)

    def first_input_grad(grad):
        return kernel_call(
            lambda *refs: input_grad_body(True, 0, *refs), [four, four, stats_shape],
            [SMEM] + [VMEM] * 6, [cat, f32_image, bf16_image],
            limit=16, flops=9 * linear_flops, moved=10 * MEGA,
        )(place, grad, weight1, image_in, stats, lines, d_resid)

    chains = {}
    token = small_three
    for kernel, names in PLAN:
        if kernel == "W2":
            halves = kernel_grad(act_two, d_conv_two, linear_sent, linear_kept)
            chains["B"] = SumChain(*halves)
            token = halves[0]
        elif kernel == "D2":
            d_conv_one, small_two = second_input_grad(after((d_conv_two,), token)[0])
            token = small_two
        elif kernel == "W1":
            halves = kernel_grad(act_one, after((d_conv_one,), token)[0])
            chains["C"] = SumChain(*halves)
            token = halves[0]
        elif kernel == "D1":
            sent, kept, small_one = first_input_grad(after((d_conv_one,), token)[0])
            token = small_one
            chains["G"] = ReturnChain(sent, kept, features.shape)
            chains["S"] = RowChain(jnp.concatenate([small_one, small_two, small_three]))
        elif kernel == "O":
            chains["O"] = ReturnChain(*after((out_sent, out_kept), token), features.shape)
        if names:
            stepping = [chains[name] for name in names if chains[name].todo() is not None]
            if stepping:
                token = step_all(place, stepping, token)
            for name in names:
                chain = chains[name]
                if name in "BC" and chain not in stepping:
                    kept, got = after((chain.kept, chain.got), token)
                    chain.first = join_last(place, kept, got, 0, 9)
                    if name == "B":
                        chain.second = join_last(place, kept, got, 9, 4)
                    token = chain.first

    output, features_grad = chains["O"].kept, chains["G"].kept
    small = chains["S"].kept
    linear_sum, conv2_sum = chains["B"].second, chains["B"].first
    conv1_sum = chains["C"].first
    return (
        output,
        features_grad,
        small[0],
        small[1],
        conv1_sum.reshape(conv1_kernel.shape),
        small[10],
        small[8],
        small[9],
        conv2_sum.reshape(conv2_kernel.shape),
        small[21],
        small[16],
        small[17],
        linear_sum[0],
        small[18],
        linear_sum[1],
        linear_sum[2],
        small[19],
        linear_sum[3],
        small[20],
    )


def per_device(features, *rest):
    rows, imgs = lax.axis_size("rows"), lax.axis_size("imgs")
    if (rows, imgs) == (8, 4) and features.shape[1] == rows and features.shape[2] == ACROSS:
        return per_device_by_images(features, *rest)
    return per_device_by_rows(features, *rest)


def solution(mesh):
    placed = (
        P("rows", "imgs", None, None),
        P("rows", "imgs", None, None),
        P(),
        P(),
        P(),
        P(),
        P(),
        P(),
        P(),
        P(),
        P(),
        P(),
        P(),
        P(),
        P(),
        P(),
        P(),
        P(),
        P(),
    )
    return jax.shard_map(
        per_device,
        mesh=mesh,
        in_specs=placed,
        out_specs=(
            P("rows", "imgs", None, None),
            P("rows", "imgs", None, None),
            P(),
            P(),
            P(),
            P(),
            P(),
            P(),
            P(),
            P(),
            P(),
            P(),
            P(),
            P(),
            P(),
            P(),
            P(),
            P(),
            P(),
        ),
        check_vma=False,
    )
```

```python
import math

import jax
import jax.numpy as jnp
from jax import lax
from jax.experimental import pallas as pl
from jax.experimental.pallas import tpu as pltpu
from jax.sharding import PartitionSpec as P

GROUPS = 32
H = 32


EPSILON = 1e-06


def padded_2(block, sides, width):
    for axis, dim in sides:
        count = lax.axis_size(axis)
        forward = [(i, i + 1) for i in range(count - 1)]
        backward = [(target, source) for source, target in forward]
        low = lax.ppermute(
            lax.slice_in_dim(block, block.shape[dim] - width, None, axis=dim), axis, forward
        )
        high = lax.ppermute(lax.slice_in_dim(block, 0, width, axis=dim), axis, backward)
        block = jnp.concatenate([low, block, high], axis=dim)
    return block


def sigmoid_pair(tensor):
    logistic = jax.nn.sigmoid(tensor)
    return (tensor * logistic, logistic * (1.0 + tensor * (1.0 - logistic)))


def group_view(tensor):
    height, images, across, channels = tensor.shape
    return tensor.reshape(height, images, across, GROUPS, channels // GROUPS)


def spread_back(statistic):
    return statistic[None, :, None, :, None]


def norm_forward(tensor, norm_gain, norm_offset):
    grouped = group_view(tensor)
    members = H * tensor.shape[2] * (tensor.shape[3] // GROUPS)
    centre = lax.psum(jnp.sum(grouped, axis=(0, 2, 4)), "rows") / members
    centered = grouped - spread_back(centre)
    spread = lax.psum(jnp.sum(jnp.square(centered), axis=(0, 2, 4)), "rows") / members
    factor = lax.rsqrt(spread + EPSILON)
    normed = (centered * spread_back(factor)).reshape(tensor.shape)
    return (normed * norm_gain + norm_offset, normed, factor)


def norm_backward(gradient, normed, factor, norm_gain):
    gain_grad = jnp.sum(gradient * normed, axis=(0, 1, 2))
    offset_grad = jnp.sum(gradient, axis=(0, 1, 2))
    scaled = group_view(gradient * norm_gain)
    flat_normed = group_view(normed)
    members = H * gradient.shape[2] * (gradient.shape[3] // GROUPS)
    mean_grad, cross_grad = lax.psum(
        (jnp.sum(scaled, axis=(0, 2, 4)), jnp.sum(scaled * flat_normed, axis=(0, 2, 4))), "rows"
    )
    input_grad = (
        scaled - spread_back(mean_grad / members) - flat_normed * spread_back(cross_grad / members)
    ) * spread_back(factor)
    return (input_grad.reshape(gradient.shape), gain_grad, offset_grad)


def widen(tensor):
    return jnp.pad(tensor, ((0, 0), (0, 0), (1, 1), (0, 0)))


def conv_forward(tensor, kernel, offset):
    height, across = (tensor.shape[0], tensor.shape[2])
    padded = widen(padded_2(tensor, (("rows", 0),), 1))
    summed = jnp.zeros(tensor.shape[:3] + (kernel.shape[3],), jnp.float32)
    for row_off in range(3):
        for col_off in range(3):
            window = padded[row_off : row_off + height, :, col_off : col_off + across, :]
            summed = summed + jnp.einsum(
                "rbwc,cd->rbwd",
                window,
                kernel[row_off, col_off],
                preferred_element_type=jnp.float32,
            )
    return (summed + offset, padded)


def conv_backward(gradient, padded, kernel):
    height, across = (gradient.shape[0], gradient.shape[2])
    beside_all = widen(padded_2(gradient, (("rows", 0),), 1))
    input_grad = jnp.zeros(gradient.shape[:3] + (kernel.shape[2],), jnp.float32)
    tap_grads = []
    for row_off in range(3):
        for col_off in range(3):
            window = beside_all[
                2 - row_off : 2 - row_off + height, :, 2 - col_off : 2 - col_off + across, :
            ]
            input_grad = input_grad + jnp.einsum(
                "rbwd,cd->rbwc",
                window,
                kernel[row_off, col_off],
                preferred_element_type=jnp.float32,
            )
            source = padded[row_off : row_off + height, :, col_off : col_off + across, :]
            tap_grads.append(
                jnp.einsum("rbwc,rbwd->cd", source, gradient, preferred_element_type=jnp.float32)
            )
    kernel_grad = jnp.stack(tap_grads).reshape(kernel.shape)
    offset_grad = jnp.sum(gradient.astype(jnp.float32), axis=(0, 1, 2))
    return (input_grad, kernel_grad, offset_grad)


def linear(tensor, weight):
    return jnp.einsum("rbwc,cd->rbwd", tensor, weight, preferred_element_type=jnp.float32)


def back_linear(gradient, weight):
    return jnp.einsum("rbwd,cd->rbwc", gradient, weight, preferred_element_type=jnp.float32)


def weight_product(tensor, gradient):
    return jnp.einsum("rbwc,rbwd->cd", tensor, gradient, preferred_element_type=jnp.float32)


def image_to_sequence(tensor):
    height, images, across, channels = tensor.shape
    return tensor.transpose(1, 0, 2, 3).reshape(images, height * across, channels)


def from_sequence(sequence, height, across):
    images, length, channels = sequence.shape
    return sequence.reshape(images, height, across, channels).transpose(1, 0, 2, 3)


def reduce_all(gradients):
    flattened = jnp.concatenate([gradient.reshape(-1) for gradient in gradients])
    length = flattened.shape[0]
    devices = lax.axis_size("rows") * lax.axis_size("imgs")
    per_share = -(-length // (devices * 128)) * 128
    padded_len = per_share * devices
    strided = jnp.pad(flattened, (0, padded_len - length)).reshape(per_share, devices).T
    packed = strided.reshape(padded_len // 128, 128)
    my_share = lax.psum_scatter(packed, ("rows", "imgs"), scatter_dimension=0, tiled=True)
    summed_all = lax.all_gather(
        my_share.astype(jnp.bfloat16), ("rows", "imgs"), axis=0, tiled=True
    ).astype(my_share.dtype)
    summed_all = summed_all.reshape(devices, per_share).T.reshape(-1)
    results = []
    offset_at = 0
    for gradient in gradients:
        results.append(summed_all[offset_at : offset_at + gradient.size].reshape(gradient.shape))
        offset_at = offset_at + gradient.size
    return results


def per_device_by_rows(
    features,
    cotangent,
    norm1_gain,
    norm1_shift,
    conv1_kernel,
    conv1_shift,
    norm2_gain,
    norm2_shift,
    conv2_kernel,
    conv2_shift,
    norm3_gain,
    norm3_shift,
    query_weight,
    query_shift,
    key_weight,
    value_weight,
    value_shift,
    out_weight,
    out_shift,
):
    height, images, across, channels = features.shape
    attention_score_scale = 1.0 / math.sqrt(channels)
    inputs = features.astype(jnp.float32)
    norm_one, normed_one, factor_one = norm_forward(inputs, norm1_gain, norm1_shift)
    act_one, slope_one = sigmoid_pair(norm_one)
    conv_one, padded_one = conv_forward(act_one.astype(jnp.bfloat16), conv1_kernel, conv1_shift)
    norm_two, normed_two, factor_two = norm_forward(conv_one, norm2_gain, norm2_shift)
    act_two, slope_two = sigmoid_pair(norm_two)
    conv_two, padded_two = conv_forward(act_two.astype(jnp.bfloat16), conv2_kernel, conv2_shift)
    residual = inputs + conv_two
    norm_three, normed_three, factor_three = norm_forward(residual, norm3_gain, norm3_shift)
    attend_input = norm_three.astype(jnp.bfloat16)
    query_rows = (linear(attend_input, query_weight) + query_shift).astype(jnp.bfloat16)
    key_state_rows = linear(attend_input, key_weight).astype(jnp.bfloat16)
    value_state_rows = (linear(attend_input, value_weight) + value_shift).astype(jnp.bfloat16)
    all_keys, all_values = (
        lax.all_gather(key_state_rows, "rows", axis=0, tiled=True),
        lax.all_gather(value_state_rows, "rows", axis=0, tiled=True),
    )
    query_sequence = image_to_sequence(query_rows)
    key_sequence = image_to_sequence(all_keys)
    value_sequence = image_to_sequence(all_values)
    attention_scores = (
        jnp.einsum("xao,xno->xan", query_sequence, key_sequence, preferred_element_type=jnp.float32)
        * attention_score_scale
    )
    row_peak = jnp.max(attention_scores, axis=-1, keepdims=True)
    log_total = row_peak + jnp.log(
        jnp.sum(jnp.exp(attention_scores - row_peak), axis=-1, keepdims=True)
    )
    weight_tensors = jnp.exp(attention_scores - log_total).astype(jnp.bfloat16)
    attended_seq = jnp.einsum(
        "afj,ajy->afy", weight_tensors, value_sequence, preferred_element_type=jnp.float32
    )
    attention_output = from_sequence(attended_seq.astype(jnp.bfloat16), height, across)
    output = residual + linear(attention_output, out_weight) + out_shift
    out_shift_grad = jnp.sum(cotangent.astype(jnp.float32), axis=(0, 1, 2))
    out_weight_grad = weight_product(attention_output, cotangent)
    mixed_grad = back_linear(cotangent, out_weight).astype(jnp.bfloat16)
    mixed_sequence = image_to_sequence(mixed_grad)
    scores_again = (
        jnp.einsum("xao,xno->xan", query_sequence, key_sequence, preferred_element_type=jnp.float32)
        * attention_score_scale
    )
    probabilities = jnp.exp(scores_again - log_total)
    probability_gradient = jnp.einsum(
        "xao,xno->xan", mixed_sequence, value_sequence, preferred_element_type=jnp.float32
    )
    delta = jnp.sum(probabilities * probability_gradient, axis=-1, keepdims=True)
    score_gradient = (probabilities * (probability_gradient - delta)).astype(jnp.bfloat16)
    query_local = (
        jnp.einsum("afj,ajy->afy", score_gradient, key_sequence, preferred_element_type=jnp.float32)
        * attention_score_scale
    )
    query_grad = from_sequence(query_local, height, across).astype(jnp.bfloat16)
    key_full = (
        jnp.einsum(
            "svt,svz->stz", score_gradient, query_sequence, preferred_element_type=jnp.float32
        )
        * attention_score_scale
    )
    value_full = jnp.einsum(
        "svt,svz->stz",
        probabilities.astype(jnp.bfloat16),
        mixed_sequence,
        preferred_element_type=jnp.float32,
    )
    stacked = from_sequence(jnp.concatenate([key_full, value_full], axis=-1), H, across)
    own_grads = lax.psum_scatter(
        stacked.astype(jnp.bfloat16), "rows", scatter_dimension=0, tiled=True
    ).astype(jnp.float32)
    key_grad = own_grads[..., :channels].astype(jnp.bfloat16)
    value_grad = own_grads[..., channels:].astype(jnp.bfloat16)
    query_weight_grad = weight_product(attend_input, query_grad)
    query_shift_grad = jnp.sum(query_grad.astype(jnp.float32), axis=(0, 1, 2))
    key_weight_grad = weight_product(attend_input, key_grad)
    value_weight_grad = weight_product(attend_input, value_grad)
    value_shift_grad = jnp.sum(value_grad.astype(jnp.float32), axis=(0, 1, 2))
    attend_grad = (
        back_linear(query_grad, query_weight)
        + back_linear(key_grad, key_weight)
        + back_linear(value_grad, value_weight)
    )
    resid_part, norm3_gain_grad, norm3_shift_grad = norm_backward(
        attend_grad, normed_three, factor_three, norm3_gain
    )
    resid_grad = cotangent.astype(jnp.float32) + resid_part
    conv_two_in, conv2_kernel_grad, conv2_shift_grad = conv_backward(
        resid_grad.astype(jnp.bfloat16), padded_two, conv2_kernel
    )
    conv_one_out, norm2_gain_grad, norm2_shift_grad = norm_backward(
        conv_two_in * slope_two, normed_two, factor_two, norm2_gain
    )
    conv_one_in, conv1_kernel_grad, conv1_shift_grad = conv_backward(
        conv_one_out.astype(jnp.bfloat16), padded_one, conv1_kernel
    )
    inputs_part, norm1_gain_grad, norm1_shift_grad = norm_backward(
        conv_one_in * slope_one, normed_one, factor_one, norm1_gain
    )
    features_grad = resid_grad + inputs_part
    reduced = reduce_all(
        [
            norm1_gain_grad,
            norm1_shift_grad,
            conv1_kernel_grad,
            conv1_shift_grad,
            norm2_gain_grad,
            norm2_shift_grad,
            conv2_kernel_grad,
            conv2_shift_grad,
            norm3_gain_grad,
            norm3_shift_grad,
            query_weight_grad,
            query_shift_grad,
            key_weight_grad,
            value_weight_grad,
            value_shift_grad,
            out_weight_grad,
            out_shift_grad,
        ]
    )
    return (output, features_grad) + tuple(reduced)


F32 = jnp.float32
BF16 = jnp.bfloat16
AXES = ("rows", "imgs")
MEGA = 1024 * 1024
TILE = 64
MM_TILE = 256
ACROSS = 32
FLOPS = 3 * 10**10
BYTES = 1
FORWARD_LIMIT = 18
ATTEND_LIMIT = 22
SECOND_GROUPS = (((0, 1, 2), False, "XYNF"), ((), True, "NFXY"))
FIRST_GROUPS = (((0, 1, 2), False, "XYNF"),)
ORDER_SLOTS = {"X": 2, "Y": 3, "N": 4, "F": 5}
TAIL = 32
SMALL = 16
PLAN = (
    "D2 W2 W1 O!", "D1 O B0 B1", "C0 B0 B1 C0", "B1 B0 C0 B0",
    "C0 B0 C0 B1", "O B0 B1 C0", "B1 G B0 B1", "C0 O B0 G",
    "B0 B1 C0 C0<", "G B1 C0>",
)
STEPS = ("core", "plane_a", "plane_b", "near", "far")
VMEM = pl.BlockSpec(memory_space=pltpu.VMEM)
SMEM = pl.BlockSpec(memory_space=pltpu.SMEM)
HBM = pl.BlockSpec(memory_space=pltpu.HBM)


def shape_of(shape, dtype):
    return jax.ShapeDtypeStruct(shape, dtype)


def kernel_call(
    body, out_shape, in_specs, scratch=(), limit=24, moved=0
):
    return pl.pallas_call(
        body,
        out_shape=out_shape,
        in_specs=in_specs,
        out_specs=jax.tree.map(lambda _: VMEM, out_shape),
        scratch_shapes=list(scratch),
        compiler_params=pltpu.CompilerParams(vmem_limit_bytes=limit * MEGA),
        cost_estimate=pl.CostEstimate(
            flops=FLOPS, bytes_accessed=BYTES * moved, transcendentals=0
        ),
    )


def tiles(total, size, body):
    def step(index, carry):
        body(pl.multiple_of(index * size, size))
        return carry

    lax.fori_loop(0, total // size, step, 0)


def fold_tiles(total, size, body, carry):
    def step(index, held):
        return body(pl.multiple_of(index * size, size), held)

    return lax.fori_loop(0, total // size, step, carry)


def fold_rows(tensor):
    return jnp.sum(tensor.reshape(tensor.shape[0] // 8, 8, tensor.shape[1]), axis=0)


def column(partial):
    return jnp.sum(partial, axis=0, keepdims=True)


def group_means(same_ref, columns, members):
    channels = columns[0].shape[1]
    place = lax.broadcasted_iota(jnp.int32, (8, channels), 0)
    rows = jnp.zeros((8, channels), F32)
    for number, values in enumerate(columns):
        left = values
        for term in range(3):
            part = left.astype(BF16).astype(F32)
            left = left - part
            rows = jnp.where(place == 3 * number + term, part, rows)
    summed = dot(rows.astype(BF16), same_ref[...])
    return [
        (summed[3 * n : 3 * n + 1] + summed[3 * n + 1 : 3 * n + 2] + summed[3 * n + 2 : 3 * n + 3])
        * (1.0 / members)
        for n in range(len(columns))
    ]


def pivot_sums(values, pivot):
    moved = values - pivot
    return fold_rows(moved), fold_rows(moved * moved)


def norm_stats(same_ref, sums, squares, pivot, total):
    channels = pivot.shape[1]
    size = channels // GROUPS
    sums, squares = column(sums), column(squares)
    (centre,) = group_means(same_ref, [sums + total * pivot], total * size)
    offset = pivot - centre
    (spread,) = group_means(
        same_ref, [squares + offset * (2.0 * sums + total * offset)], total * size
    )
    return centre, lax.rsqrt(spread + EPSILON)


def fill_shifted(cat_ref, at, tile):
    size, channels = tile.shape
    place = lax.broadcasted_iota(jnp.int32, tile.shape, 0) % ACROSS
    before = jnp.where(place == 0, 0.0, pltpu.roll(tile, 1, 0))
    after = jnp.where(place == ACROSS - 1, 0.0, pltpu.roll(tile, size - 1, 0))
    rows = pl.ds(pl.multiple_of(ACROSS + at, ACROSS), size)
    cat_ref[rows, 0:channels] = before.astype(BF16)
    cat_ref[rows, channels : 2 * channels] = tile.astype(BF16)
    cat_ref[rows, 2 * channels : 3 * channels] = after.astype(BF16)


def clear_border(cat_ref):
    total, width = cat_ref.shape
    cat_ref[0:ACROSS, :] = jnp.zeros((ACROSS, width), BF16)
    cat_ref[total - ACROSS : total, :] = jnp.zeros((ACROSS, width), BF16)


def window_product(cat_ref, weight_ref, at, size):
    total = None
    for row_off in range(3):
        rows = pl.ds(pl.multiple_of(at + row_off * ACROSS, ACROSS), size)
        part = jnp.dot(cat_ref[rows, :], weight_ref[row_off], preferred_element_type=F32)
        total = part if total is None else total + part
    return total


def window_product_turned(cat_ref, weight_ref, at, size):
    channels = weight_ref.shape[2]
    total = None
    for row_off in range(3):
        rows = pl.ds(pl.multiple_of(at + (2 - row_off) * ACROSS, ACROSS), size)
        for col_off in range(3):
            low = (2 - col_off) * channels
            tap = weight_ref[row_off, col_off * channels : (col_off + 1) * channels, :]
            part = dot_t(cat_ref[rows, low : low + channels], tap)
            total = part if total is None else total + part
    return total


def dot_t(left, right):
    return lax.dot_general(left, right, (((1,), (1,)), ((), ())), preferred_element_type=F32)


def t_dot(left, right):
    return lax.dot_general(left, right, (((0,), (0,)), ((), ())), preferred_element_type=F32)


def dot(left, right):
    return jnp.dot(left, right, preferred_element_type=F32)


def line(lines_ref, row):
    return lines_ref[row : row + 1, :]


def forward_body(place_ref, *refs):
    pairs = refs[:4]
    (lines_ref, same_ref, weight1_ref, weight2_ref, q_weight_ref, k_weight_ref, v_weight_ref,
     image_ref, act1_ref, conv_ref, act2_ref, resid_ref, stats_ref, norm_ref, q_ref, k_ref, v_ref,
     cat_ref, pivot_ref) = refs[4:]
    total, channels = image_ref.shape
    share = total // 8
    me = place_ref[0]
    for index in range(8):
        at = pl.multiple_of((me ^ index) * share, share)
        image_ref[pl.ds(at, share), :] = pairs[index // 2][index % 2]
    clear_border(cat_ref)
    zero = jnp.zeros((8, channels), F32)

    def activate_all(read, stats, stats_row, gain_row, act_ref):
        centre, factor = stats
        stats_ref[stats_row : stats_row + 1, :] = centre
        stats_ref[stats_row + 1 : stats_row + 2, :] = factor
        scale = factor * line(lines_ref, gain_row)
        shift = line(lines_ref, gain_row + 1) - centre * scale

        def activate(at):
            held = read(at) * scale + shift
            act = held * jax.nn.sigmoid(held)
            act_ref[pl.ds(at, TILE), :] = act.astype(BF16)
            fill_shifted(cat_ref, at, act)

        tiles(total, TILE, activate)

    def read_image(at):
        return image_ref[pl.ds(at, TILE), :].astype(F32)

    pivot1 = read_image(0)[0:1, :]

    def sum_image(at, held):
        sums, squares = pivot_sums(read_image(at), pivot1)
        return held[0] + sums, held[1] + squares

    sums, squares = fold_tiles(total, TILE, sum_image, (zero, zero))
    stats1 = norm_stats(same_ref, sums, squares, pivot1, total)
    activate_all(read_image, stats1, 0, 0, act1_ref)

    def convolve_all(weight_ref, bias, more, target_ref):
        def convolve(at, held):
            rows = pl.ds(at, MM_TILE)
            values = window_product(cat_ref, weight_ref, at, MM_TILE) + bias
            if more is not None:
                values = values + more[rows, :].astype(F32)

            @pl.when(at == 0)
            def _():
                pivot_ref[0:1, :] = values[0:1, :]

            target_ref[rows, :] = values
            sums, squares = pivot_sums(values, pivot_ref[0:1, :])
            return held[0] + sums, held[1] + squares

        sums, squares = fold_tiles(total, MM_TILE, convolve, (zero, zero))
        return norm_stats(same_ref, sums, squares, pivot_ref[0:1, :], total)

    stats2 = convolve_all(weight1_ref, line(lines_ref, 6), None, conv_ref)
    activate_all(lambda at: conv_ref[pl.ds(at, TILE), :], stats2, 2, 2, act2_ref)
    centre3, factor3 = convolve_all(weight2_ref, line(lines_ref, 7), image_ref, resid_ref)
    stats_ref[4:5, :] = centre3
    stats_ref[5:6, :] = factor3
    stats_ref[6:8, :] = jnp.zeros((2, channels), F32)
    scale3 = factor3 * line(lines_ref, 4)
    shift3 = line(lines_ref, 5) - centre3 * scale3
    q_shift, v_shift = line(lines_ref, 8), line(lines_ref, 9)

    def project(at):
        rows = pl.ds(at, MM_TILE)
        held = (resid_ref[rows, :] * scale3 + shift3).astype(BF16)
        norm_ref[rows, :] = held
        q_ref[rows, :] = (dot(held, q_weight_ref[...]) + q_shift).astype(BF16)
        k_ref[rows, :] = dot(held, k_weight_ref[...]).astype(BF16)
        v_ref[rows, :] = (dot(held, v_weight_ref[...]) + v_shift).astype(BF16)

    tiles(total, MM_TILE, project)


def lane_half(part, half):
    return pl.ds(pl.multiple_of(part * half, half), half)


def z_bits(core):
    return 2 << core, 4 >> core


def return_pieces(place_ref, out_ref, sent_ref, kept_ref):
    share = out_ref.shape[0] // 8
    me, core = place_ref[0], place_ref[1]
    for target, side in ((kept_ref, 0), (sent_ref, 1)):
        first, second = z_bits(core if side == 0 else 1 - core)
        for index in range(4):
            offset = side + (index // 2) * first + (index % 2) * second
            at = pl.multiple_of((me ^ offset) * share, share)
            target[index] = out_ref[pl.ds(at, share), :]


def attention_body(place_ref, *refs):
    cot_pieces = refs[:4]
    (q_ref, k_ref, v_ref, norm_ref, resid_ref, stats_ref, lines_ref, same_ref,
     o_weight_ref, q_weight_ref, k_weight_ref, v_weight_ref) = refs[4:16]
    (out_sent_ref, out_kept_ref, sent_ref, kept_ref, small_ref, d_resid_ref, d_conv_ref, d_sent_ref,
     cot_ref, out_ref, mixed_ref, d_mixed_ref, d_q_ref, d_k_ref, d_v_ref,
     weights_ref, d_scores_ref) = refs[16:]
    total, channels = q_ref.shape
    share = total // 8
    scale = 1.0 / math.sqrt(channels)
    me = place_ref[0]
    for index in range(8):
        at = pl.multiple_of((me ^ index) * share, share)
        cot_ref[pl.ds(at, share), :] = cot_pieces[index // 2][index % 2]
    o_shift = line(lines_ref, 10)
    zero = jnp.zeros((8, channels), F32)

    def attend(at, held):
        rows = pl.ds(at, MM_TILE)
        query = q_ref[rows, :]
        cot = cot_ref[rows, :]
        scores = dot_t(query, k_ref[...]) * scale
        d_mixed = dot_t(cot, o_weight_ref[...]).astype(BF16)
        d_mixed_ref[rows, :] = d_mixed
        d_prob = dot_t(d_mixed, v_ref[...])
        exps = jnp.exp(scores - jnp.max(scores, axis=-1, keepdims=True))
        probs = exps * (1.0 / jnp.sum(exps, axis=-1, keepdims=True))
        weights = probs.astype(BF16)
        weights_ref[rows, :] = weights
        mixed = dot(weights, v_ref[...]).astype(BF16)
        mixed_ref[rows, :] = mixed
        out_ref[rows, :] = (
            resid_ref[rows, :] + dot(mixed, o_weight_ref[...]) + o_shift
        ).astype(BF16)
        delta = jnp.sum(probs * d_prob, axis=-1, keepdims=True)
        d_scores = (probs * (d_prob - delta)).astype(BF16)
        d_scores_ref[rows, :] = d_scores
        d_query = (dot(d_scores, k_ref[...]) * scale).astype(BF16)
        d_q_ref[rows, :] = d_query
        return held[0] + fold_rows(cot.astype(F32)), held[1] + fold_rows(d_query.astype(F32))

    cot_sums, d_q_sums = fold_tiles(total, MM_TILE, attend, (zero, zero))
    return_pieces(place_ref, out_ref, out_sent_ref, out_kept_ref)

    def to_keys(at, held):
        rows = pl.ds(at, MM_TILE)
        d_k_ref[rows, :] = (t_dot(d_scores_ref[:, rows], q_ref[...]) * scale).astype(BF16)
        d_value = t_dot(weights_ref[:, rows], d_mixed_ref[...]).astype(BF16)
        d_v_ref[rows, :] = d_value
        return held + fold_rows(d_value.astype(F32))

    d_v_sums = fold_tiles(total, MM_TILE, to_keys, zero)
    half = channels // 2
    core = place_ref[1]
    for index, (left, right) in enumerate(
        ((norm_ref, d_q_ref), (norm_ref, d_k_ref), (norm_ref, d_v_ref), (mixed_ref, cot_ref))
    ):
        for target, part in ((sent_ref, 1 - core), (kept_ref, core)):
            target[index] = t_dot(left[...], right[:, lane_half(part, half)]).astype(BF16)

    centre, factor = stats_ref[4:5, :], stats_ref[5:6, :]
    gain = line(lines_ref, 4)

    def back(at, held):
        rows = pl.ds(at, MM_TILE)
        grad = (
            dot_t(d_q_ref[rows, :], q_weight_ref[...])
            + dot_t(d_k_ref[rows, :], k_weight_ref[...])
            + dot_t(d_v_ref[rows, :], v_weight_ref[...])
        )
        d_resid_ref[rows, :] = grad
        normed = (resid_ref[rows, :] - centre) * factor
        return held[0] + fold_rows(grad), held[1] + fold_rows(grad * normed)

    sums = fold_tiles(total, MM_TILE, back, (zero, zero))
    shift_grad, gain_grad, o_shift_grad, q_shift_grad, v_shift_grad = [
        column(part) for part in (*sums, cot_sums, d_q_sums, d_v_sums)
    ]
    members = total * (channels // GROUPS)
    mean_grad, cross_grad = group_means(same_ref, [shift_grad * gain, gain_grad * gain], members)

    def finish(at, held):
        rows = pl.ds(at, TILE)
        normed = (resid_ref[rows, :] - centre) * factor
        grad = cot_ref[rows, :].astype(F32) + factor * (
            d_resid_ref[rows, :] * gain - mean_grad - normed * cross_grad
        )
        d_resid_ref[rows, :] = grad
        rounded = grad.astype(BF16)
        d_conv_ref[rows, :] = rounded
        d_sent_ref[rows, :] = d_conv_ref[rows, lane_half(1 - core, half)]
        return held + fold_rows(rounded.astype(F32))

    conv_shift_grad = column(fold_tiles(total, TILE, finish, zero))
    small_ref[0:1, :] = gain_grad
    small_ref[1:2, :] = shift_grad
    small_ref[2:3, :] = q_shift_grad
    small_ref[3:4, :] = v_shift_grad
    small_ref[4:5, :] = o_shift_grad
    small_ref[5:6, :] = conv_shift_grad
    small_ref[6:8, :] = jnp.zeros((2, channels), F32)


def kernel_grad_body(groups, place_ref, act_ref, act_got_ref, grad_ref, grad_got_ref, *refs):
    linear = any(carries for _, carries, _ in groups)
    more, refs = (refs[:2], refs[2:]) if linear else ((), refs)
    parts, (cat_ref, cat_got_ref, turned_ref, turned_got_ref) = refs[: 2 * len(groups)], refs[2 * len(groups) :]
    total, channels = act_ref.shape
    half = channels // 2
    core = place_ref[1]
    clear_border(cat_ref)
    clear_border(cat_got_ref)

    def fill(at):
        rows = pl.ds(at, TILE)
        fill_shifted(cat_ref, at, grad_ref[rows, lane_half(core, half)].astype(F32))
        fill_shifted(cat_got_ref, at, grad_got_ref[rows, :].astype(F32))

    tiles(total, TILE, fill)
    turned_ref[...] = act_ref[...].T
    turned_got_ref[...] = act_got_ref[...].T
    for number, (kernel_rows, carries, order) in enumerate(groups):
        bit = place_ref[ORDER_SLOTS[order[0]]]
        for target, part in ((parts[2 * number], 1 - bit), (parts[2 * number + 1], bit)):
            rows = pl.ds(pl.multiple_of(part * half, half), half)
            for index, row_off in enumerate(kernel_rows):
                span = pl.ds((2 - row_off) * ACROSS, total)
                product = (
                    dot(turned_ref[rows, :], cat_ref[span, :])
                    + dot(turned_got_ref[rows, :], cat_got_ref[span, :])
                ).astype(BF16)
                for col_off in range(3):
                    at = (3 * index + col_off) * half
                    low = (2 - col_off) * half
                    target[at : at + half, :] = product[:, low : low + half]
            if carries:
                for index in range(4):
                    at = (3 * len(kernel_rows) + index) * half
                    target[at : at + half, :] = (
                        more[0][index, rows, :].astype(F32) + more[1][index, rows, :].astype(F32)
                    ).astype(BF16)


def input_grad_body(with_rest, stats_row, place_ref, *refs):
    grad_ref, weight_ref, source_ref, stats_ref, lines_ref, same_ref = refs[:6]
    if with_rest:
        rest_ref, small_two_ref, small_three_ref = refs[6:9]
    refs = refs[9:] if with_rest else refs[6:]
    if with_rest:
        sent_ref, kept_ref, small_ref, cat_ref, held_ref, out_ref, rows_ref = refs
    else:
        out_ref, d_sent_ref, small_ref, cat_ref, held_ref = refs
    core = place_ref[1]
    total, channels = grad_ref.shape
    centre = stats_ref[stats_row : stats_row + 1, :]
    factor = stats_ref[stats_row + 1 : stats_row + 2, :]
    gain, shift = line(lines_ref, stats_row), line(lines_ref, stats_row + 1)
    clear_border(cat_ref)

    def fill(at):
        fill_shifted(cat_ref, at, grad_ref[pl.ds(at, TILE), :].astype(F32))

    tiles(total, TILE, fill)

    zero = jnp.zeros((8, channels), F32)

    def product(at, held):
        rows = pl.ds(at, MM_TILE)
        normed = (source_ref[rows, :].astype(F32) - centre) * factor
        pre = normed * gain + shift
        logistic = jax.nn.sigmoid(pre)
        slope = logistic * (1.0 + pre * (1.0 - logistic))
        grad = window_product_turned(cat_ref, weight_ref, at, MM_TILE) * slope
        held_ref[rows, :] = grad
        return held[0] + fold_rows(grad), held[1] + fold_rows(grad * normed)

    shift_sum, gain_sum = fold_tiles(total, MM_TILE, product, (zero, zero))
    shift_grad, gain_grad = column(shift_sum), column(gain_sum)
    members = total * (channels // GROUPS)
    mean_grad, cross_grad = group_means(same_ref, [shift_grad * gain, gain_grad * gain], members)

    def finish(at, held):
        rows = pl.ds(at, TILE)
        normed = (source_ref[rows, :].astype(F32) - centre) * factor
        grad = factor * (held_ref[rows, :] * gain - mean_grad - normed * cross_grad)
        if with_rest:
            grad = grad + rest_ref[rows, :]
        rounded = grad.astype(BF16)
        out_ref[rows, :] = rounded
        if not with_rest:
            d_sent_ref[rows, :] = out_ref[rows, lane_half(1 - core, channels // 2)]
        return held + fold_rows(rounded.astype(F32))

    out_sum = column(fold_tiles(total, TILE, finish, zero))
    if not with_rest:
        small_ref[0:1, :] = gain_grad
        small_ref[1:2, :] = shift_grad
        small_ref[2:3, :] = out_sum
        small_ref[3:8, :] = jnp.zeros((5, channels), F32)
        return
    return_pieces(place_ref, out_ref, sent_ref, kept_ref)
    rows_ref[0:1, :] = gain_grad
    rows_ref[1:2, :] = shift_grad
    rows_ref[2:5, :] = small_two_ref[0:3, :]
    rows_ref[5:11, :] = small_three_ref[0:6, :]
    rows_ref[11:SMALL, :] = jnp.zeros((SMALL - 11, channels), F32)
    half = channels // 2
    small_ref[0:SMALL, :] = rows_ref[:, 0:half].astype(BF16)
    small_ref[SMALL:TAIL, :] = rows_ref[:, half:channels].astype(BF16)


def pack_by_core_body(place_ref, block_ref, sent_ref, kept_ref):
    me = place_ref[0]
    for target, side in ((kept_ref, 0), (sent_ref, 1)):
        for index in range(4):
            for row in range(block_ref.shape[0]):
                rows = pl.ds(row * ACROSS, ACROSS)
                target[index, rows, :] = block_ref[row, me ^ (2 * index + side)]


def pair_body(place_ref, kept_ref, got_ref, *refs):
    count = (len(refs) - 5) // 2
    staged, pair_refs, sems = refs[:count], refs[count : count + 4], refs[-1]
    targets = refs[count + 4 : 2 * count + 4]
    copies = [
        pltpu.make_async_copy(staged[index], targets[index], sems.at[index])
        for index in range(count)
    ]
    for copy in copies:
        copy.start()
    for index in range(4):
        pair_refs[index][0] = kept_ref[index]
        pair_refs[index][1] = got_ref[index]
    if count:
        same_ref = refs[2 * count + 4]
        one, two = (lax.broadcasted_iota(jnp.int32, same_ref.shape, dim) for dim in (0, 1))
        size = same_ref.shape[0] // GROUPS
        same_ref[...] = jnp.where(one // size == two // size, 1.0, 0.0).astype(BF16)
    for copy in copies:
        copy.wait()


def swap_by_core(place, block, staged=()):
    rows, _, across, channels = block.shape
    four = shape_of((4, rows * across, channels), BF16)
    sent, kept = kernel_call(
        pack_by_core_body, [four] * 2, [SMEM, VMEM], limit=8, moved=2 * MEGA
    )(place, block)
    got = exchange(sent, "core")
    pair = shape_of((2, rows * across, channels), BF16)
    results = kernel_call(
        pair_body,
        [pair] * 4
        + [shape_of(array.shape, array.dtype) for array in staged]
        + [shape_of((channels, channels), BF16)] * bool(staged),
        [SMEM, VMEM, VMEM] + [HBM] * len(staged),
        [pltpu.SemaphoreType.DMA((max(len(staged), 1),))],
        limit=16 if staged else 8,
        moved=2 * MEGA,
    )(place, kept, got, *staged)
    return results[:4], results[4:]


def swap_pieces(pieces, unit):
    count = len(pieces)
    return [pieces[0]] + [
        lax.ppermute(pieces[k], "rows", [(r, r ^ (unit * k)) for r in range(count * unit)])
        for k in range(1, count)
    ]


def partner_table(kind):
    table = []
    for row in range(8):
        for img in range(4):
            core = row & 1
            if kind == "core":
                other = (row ^ 1, img)
            elif kind == "near":
                other = (row ^ (4 if core else 2), img)
            elif kind == "far":
                other = (row ^ (2 if core else 4), img)
            elif kind == "plane_a":
                other = (row, img ^ (2 if core else 1))
            else:
                other = (row, img ^ (1 if core else 2))
            table.append((row * 4 + img, other[0] * 4 + other[1]))
    return table


def exchange(tensor, kind):
    return lax.ppermute(tensor, AXES, partner_table(kind))


def own_place():
    row, img = lax.axis_index("rows"), lax.axis_index("imgs")
    core, near, far = row & 1, (row >> 1) & 1, (row >> 2) & 1
    low, high = img & 1, (img >> 1) & 1
    plane_a = jnp.where(core == 1, high, low)
    plane_b = jnp.where(core == 1, low, high)
    first_z = jnp.where(core == 1, far, near)
    second_z = jnp.where(core == 1, near, far)
    return jnp.stack([row, core, plane_a, plane_b, first_z, second_z, row, row]).astype(jnp.int32)


def add_tails(target, target_at, kept_ref, got_ref, at):
    target[target_at : target_at + TAIL, :] = (
        kept_ref[at : at + TAIL, :].astype(F32) + got_ref[at : at + TAIL, :].astype(F32)
    ).astype(BF16)


def add_split(chain, slot, place_ref, ins, outs):
    kept_ref, got_ref = ins[:2]
    count, rows = chain.count, chain.rows
    half = rows // 2
    bit = place_ref[slot]

    def one(index, carry):
        for target, part in zip(outs, (1 - bit, bit)):
            span = pl.ds(pl.multiple_of(index * rows + part * half, half), half)
            target[pl.ds(pl.multiple_of(index * half, half), half), :] = (
                kept_ref[span, :].astype(F32) + got_ref[span, :].astype(F32)
            ).astype(BF16)
        return carry

    lax.fori_loop(0, count, one, 0)
    if chain.small is not None:
        for target in outs:
            if len(ins) > 2:
                target[count * half : count * half + TAIL, :] = ins[2][...]
            else:
                add_tails(target, count * half, kept_ref, got_ref, count * rows)


def add_last(chain, slot, place_ref, ins, outs):
    outs[0][...] = (ins[0][...].astype(F32) + ins[1][...].astype(F32)).astype(BF16)


def join(chain, slot, place_ref, ins, outs):
    count, rows = chain.count, chain.rows
    bit = place_ref[slot]

    def one(index, carry):
        for source, part in zip(ins, (bit, 1 - bit)):
            span = pl.ds(pl.multiple_of((2 * index + part) * rows, rows), rows)
            outs[0][span, :] = source[pl.ds(pl.multiple_of(index * rows, rows), rows), :]
        return carry

    lax.fori_loop(0, count, one, 0)
    if chain.small is not None:
        at = count * rows
        if slot == ORDER_SLOTS["X"]:
            add_tails(outs[0], 2 * at, ins[0], ins[1], at)
        else:
            outs[0][2 * at : 2 * at + TAIL, :] = ins[0][at : at + TAIL, :]


def turn_pairs(chain, slot, place_ref, ins, outs):
    kept_ref, got_ref = ins
    for target, part in zip(outs, (1, 0)):
        for index in range(2):
            if slot == 0:
                target[index] = kept_ref[2 * part + index]
                target[2 + index] = got_ref[2 * part + index]
            else:
                target[index] = kept_ref[2 * index + part]
                target[2 + index] = got_ref[2 * index + part]


def spread(chain, slot, place_ref, ins, outs):
    me, core = place_ref[0], place_ref[1]
    first, second = z_bits(core)
    out_ref = outs[0]
    for source, side in zip(ins, (0, 1)):
        for index in range(4):
            image = me ^ ((index % 2) + (index // 2) * first + side * second)
            for row in range(out_ref.shape[0]):
                rows = pl.ds(row * ACROSS, ACROSS)
                out_ref[row, image] = source[index, rows, :].astype(F32)


def join_last(place, sources, targets):
    half = sources[0][0].shape[1]
    rows = 2 * half
    sides = [side for _, side in sources]
    count = sum(target[4] for target in targets)
    wholes = [target[0] for target in targets if target[0] is not None]

    def body(place_ref, *refs):
        source_refs = refs[: len(sources)]
        out_refs = refs[len(sources) + len(wholes) : -2]
        held_ref, sems = refs[-2:]
        core = place_ref[1]
        copies = []
        for out_ref, (_, _, there, here, planes) in zip(out_refs, targets):
            for plane in range(planes):
                for number, side in enumerate(sides):
                    index = len(copies)
                    at = (here + plane) * rows
                    held_ref[index] = source_refs[number][at : at + rows, :].astype(F32)
                    part = 1 - core if side else core
                    copy = pltpu.make_async_copy(
                        held_ref.at[index],
                        out_ref.at[there + plane, :, lane_half(part, half)],
                        sems.at[index],
                    )
                    copy.start()
                    copies.append(copy)
        for copy in copies:
            copy.wait()

    anywhere = pl.BlockSpec(memory_space=pl.ANY)
    aliases, taken = {}, 0
    for number, target in enumerate(targets):
        if target[0] is not None:
            aliases[1 + len(sources) + taken] = number
            taken += 1
    slots = count * len(sources)
    return pl.pallas_call(
        body,
        out_shape=[shape_of((target[1], rows, rows), F32) for target in targets],
        in_specs=[SMEM] + [VMEM] * len(sources) + [anywhere] * len(wholes),
        out_specs=[anywhere] * len(targets),
        input_output_aliases=aliases,
        scratch_shapes=[pltpu.VMEM((slots, rows, half), F32), pltpu.SemaphoreType.DMA((slots,))],
        compiler_params=pltpu.CompilerParams(vmem_limit_bytes=(slots // 2 + 6) * MEGA),
        cost_estimate=pl.CostEstimate(
            flops=FLOPS, bytes_accessed=BYTES * 6 * slots * rows * half, transcendentals=0
        ),
    )(place, *[array for array, _ in sources], *wholes)


def small_last(place, mine, got):
    half = mine.shape[1]
    block = mine.shape[0] // TAIL - 1

    def body(place_ref, mine_ref, got_ref, out_ref):
        total = mine_ref[...].astype(F32) + got_ref[...].astype(F32)
        out_ref[:, 0:half] = total[0:SMALL]
        out_ref[:, half : 2 * half] = total[SMALL:TAIL]

    spec = pl.BlockSpec((TAIL, half), lambda i: (block, 0))
    return pl.pallas_call(
        body,
        grid=(1,),
        out_shape=shape_of((SMALL, 2 * half), F32),
        in_specs=[SMEM, spec, spec],
        out_specs=pl.BlockSpec((SMALL, 2 * half), lambda i: (0, 0)),
        cost_estimate=pl.CostEstimate(flops=FLOPS, bytes_accessed=MEGA, transcendentals=0),
    )(place, mine, got)


def tie(values, earlier):
    return lax.optimization_barrier(tuple(values) + tuple(earlier))[: len(values)]


def after(values, token):
    tied = lax.optimization_barrier(tuple(values) + (token,))
    return tied[:-1]


class SumChain:
    def __init__(self, sent, kept, order):
        self.kept, self.at, self.small = kept, 0, None
        self.rows = kept.shape[1]
        self.count = kept.shape[0] // self.rows
        self.slots = [ORDER_SLOTS[letter] for letter in order]
        self.got = exchange(sent, STEPS[self.slots[0] - 1])

    def inputs(self):
        with_small = self.small is not None and self.at == 0
        return [self.kept, self.got] + ([self.small] if with_small else [])

    def todo(self):
        tail = 0 if self.small is None else TAIL
        lanes = self.kept.shape[1]
        at, size = self.at, self.count * self.rows
        if at < 3:
            return add_split, self.slots[at + 1], [shape_of((size // 2 + tail, lanes), BF16)] * 2
        if at == 3:
            return add_last, 0, [shape_of((size + tail, lanes), BF16)]
        return join, self.slots[7 - at], [shape_of((2 * size + tail, lanes), BF16)]

    def take(self, outs):
        at = self.at
        self.at += 1
        self.kept = outs[-1]
        if at < 3:
            self.rows //= 2
            slot = self.slots[at + 1]
        elif at == 3:
            slot = self.slots[3]
        else:
            self.rows *= 2
            slot = self.slots[6 - at] if at < 7 else 1
        self.got = exchange(outs[0], STEPS[slot - 1])


class ReturnChain:
    def __init__(self, sent, kept, block_shape):
        self.kept, self.at, self.block_shape = kept, 0, block_shape
        self.got = exchange(sent, "core")

    def inputs(self):
        return [self.kept, self.got]

    def todo(self):
        if self.at < 2:
            return turn_pairs, self.at, [shape_of(self.kept.shape, BF16)] * 2
        return spread, 0, [shape_of(self.block_shape, F32)]

    def take(self, outs):
        self.kept = outs[-1]
        if self.at < 2:
            self.got = exchange(outs[0], ("near", "far")[self.at])
        self.at += 1


def step(place, chain, token):
    work, slot, shapes = chain.todo()
    arrays = after(chain.inputs(), token)

    def body(place_ref, *refs):
        work(chain, slot, place_ref, refs[: len(arrays)], refs[len(arrays) :])

    moved = 2 * sum(a.size * a.dtype.itemsize for a in arrays)
    results = kernel_call(
        body, shapes, [SMEM] + [VMEM] * len(arrays), limit=3 + moved // MEGA, moved=moved
    )(place, *arrays)
    chain.take(results)
    return results[0]


def per_device_by_images(
    features,
    cotangent,
    norm1_gain,
    norm1_shift,
    conv1_kernel,
    conv1_shift,
    norm2_gain,
    norm2_shift,
    conv2_kernel,
    conv2_shift,
    norm3_gain,
    norm3_shift,
    query_weight,
    query_shift,
    key_weight,
    value_weight,
    value_shift,
    out_weight,
    out_shift,
):
    rows, images, across, channels = features.shape
    total = rows * images * across
    place = own_place()
    lines = jnp.stack([
        norm1_gain, norm1_shift, norm2_gain, norm2_shift, norm3_gain, norm3_shift,
        conv1_shift, conv2_shift, query_shift, value_shift, out_shift, out_shift,
    ] + [out_shift] * 4)

    image = shape_of((total, channels), BF16)
    image_f32 = shape_of((total, channels), F32)
    piece = shape_of((total // 8, channels), BF16)
    stats_shape = shape_of((8, channels), F32)
    cat = pltpu.VMEM((total + 2 * across, 3 * channels), BF16)
    bf16_image = pltpu.VMEM((total, channels), BF16)
    f32_image = pltpu.VMEM((total, channels), F32)
    tall = (3, 3 * channels, channels)

    feature_pairs, _ = swap_by_core(place, features)
    feature_pieces = swap_pieces(feature_pairs, 2)
    cot_pairs, (weight1, weight2, q_weight, k_weight, v_weight, o_weight, same) = swap_by_core(
        place,
        after((cotangent,), feature_pairs[0])[0],
        (conv1_kernel.reshape(tall), conv2_kernel.reshape(tall), query_weight, key_weight,
         value_weight, out_weight),
    )
    cot_pieces = swap_pieces(tie(cot_pairs, feature_pieces[1:]), 2)

    (image_in, act_one, conv_one, act_two, residual, stats, normed, query, key, value) = kernel_call(
        forward_body,
        [image, image, image_f32, image, image_f32, stats_shape] + [image] * 4,
        [SMEM] + [VMEM] * 11,
        [cat, pltpu.VMEM((8, channels), F32)],
        limit=FORWARD_LIMIT,
        moved=24 * MEGA,
    )(place, *feature_pieces, lines, same, weight1, weight2, q_weight, k_weight, v_weight)
    act_one_got, act_two_got = exchange(act_one, "core"), exchange(act_two, "core")
    half = channels // 2
    four = shape_of((4, total // 8, channels), BF16)
    halves = shape_of((4, channels, half), BF16)
    grad_half = shape_of((total, half), BF16)
    (out_sent, out_kept, linear_sent, linear_kept, small_three, d_resid, d_conv_two,
     d_sent_two) = kernel_call(
        attention_body,
        [four, four, halves, halves, stats_shape, image_f32, image, grad_half],
        [SMEM] + [VMEM] * 16,
        [bf16_image] * 7 + [pltpu.VMEM((total, total), BF16)] * 2,
        limit=ATTEND_LIMIT,
        moved=16 * MEGA,
    )(
        place, *cot_pieces, query, key, value, normed, residual, stats, lines, same,
        o_weight, q_weight, k_weight, v_weight,
    )
    d_got_two = exchange(d_sent_two, "core")
    linear_got = exchange(linear_sent, "core")
    half_cat = pltpu.VMEM((total + 2 * across, 3 * half), BF16)

    def kernel_grad(made, *arrays):
        parts = []
        for kernel_rows, carries, _ in made:
            planes = 3 * len(kernel_rows) + 4 * carries
            parts += [shape_of((planes * half, half), BF16)] * 2
        return kernel_call(
            lambda *refs: kernel_grad_body(made, *refs), parts, [SMEM] + [VMEM] * len(arrays),
            [half_cat] * 2 + [pltpu.VMEM((channels, total), BF16)] * 2,
            limit=14, moved=8 * MEGA,
        )(place, *arrays)

    def second_input_grad(grad):
        return kernel_call(
            lambda *refs: input_grad_body(False, 2, *refs), [image, grad_half, stats_shape],
            [SMEM] + [VMEM] * 6, [cat, f32_image],
            limit=16, moved=10 * MEGA,
        )(place, grad, weight2, conv_one, stats, lines, same)

    def first_input_grad(grad):
        return kernel_call(
            lambda *refs: input_grad_body(True, 0, *refs),
            [four, four, shape_of((TAIL, half), BF16)],
            [SMEM] + [VMEM] * 9,
            [cat, f32_image, bf16_image, pltpu.VMEM((SMALL, channels), F32)],
            limit=16, moved=10 * MEGA,
        )(place, grad, weight1, image_in, stats, lines, same, d_resid, small_two, small_three)

    chains, groups, sums = {}, {}, {}

    def begin(letter, parts, made):
        for number, group in enumerate(made):
            name = letter + str(number)
            chains[name] = SumChain(*parts[2 * number : 2 * number + 2], group[2])
            groups[name] = group

    def end(name, token, sides):
        chain = chains[name]
        arrays = after([(chain.kept, chain.got)[side] for side in sides], token)
        sources = list(zip(arrays, sides))
        kernel_rows, carries, _ = groups[name]
        taps = 3 * len(kernel_rows)
        targets = {}
        if taps:
            targets[name[0]] = (sums.get(name[0]), 9, 3 * kernel_rows[0], 0, taps)
        if carries:
            targets["linear"] = (None, 4, 0, taps, 4)
        made = join_last(place, sources, list(targets.values()))
        sums.update(zip(targets, made))
        if chain.small is not None and 1 in sides:
            sums["small"] = small_last(place, chain.kept, arrays[-1])
        return made[0]

    token = small_three
    for event in " ".join(PLAN).split():
        if event == "W2":
            parts = kernel_grad(
                SECOND_GROUPS, act_two, act_two_got, after((d_conv_two,), token)[0], d_got_two,
                linear_kept, linear_got,
            )
            begin("B", parts, SECOND_GROUPS)
            token = parts[0]
        elif event == "D2":
            d_conv_one, d_sent_one, small_two = second_input_grad(after((d_conv_two,), token)[0])
            d_got_one = exchange(d_sent_one, "core")
            token = small_two
        elif event == "W1":
            parts = kernel_grad(
                FIRST_GROUPS, act_one, act_one_got, after((d_conv_one,), token)[0], d_got_one
            )
            begin("C", parts, FIRST_GROUPS)
            token = parts[0]
        elif event == "D1":
            sent, kept, small = first_input_grad(after((d_conv_one,), token)[0])
            token = small
            chains["G"] = ReturnChain(sent, kept, features.shape)
            chains["C0"].small = small
        elif event == "O!":
            chains["O"] = ReturnChain(*after((out_sent, out_kept), token), features.shape)
        elif event.endswith("<"):
            token = end(event[:-1], token, (0,))
        elif event.endswith(">"):
            token = end(event[:-1], token, (1,))
        elif event in groups and chains[event].at == 8:
            token = end(event, token, (0, 1))
        else:
            token = step(place, chains[event], token)

    output, features_grad = chains["O"].kept, chains["G"].kept
    small = sums["small"]
    linear_sum, conv2_sum, conv1_sum = sums["linear"], sums["B"], sums["C"]
    return (
        output,
        features_grad,
        small[0],
        small[1],
        conv1_sum.reshape(conv1_kernel.shape),
        small[4],
        small[2],
        small[3],
        conv2_sum.reshape(conv2_kernel.shape),
        small[10],
        small[5],
        small[6],
        linear_sum[0],
        small[7],
        linear_sum[1],
        linear_sum[2],
        small[8],
        linear_sum[3],
        small[9],
    )


def per_device(features, *rest):
    rows, imgs = lax.axis_size("rows"), lax.axis_size("imgs")
    if (rows, imgs) == (8, 4) and features.shape[1] == rows and features.shape[2] == ACROSS:
        return per_device_by_images(features, *rest)
    return per_device_by_rows(features, *rest)


def solution(mesh):
    placed = (
        P("rows", "imgs", None, None),
        P("rows", "imgs", None, None),
        P(),
        P(),
        P(),
        P(),
        P(),
        P(),
        P(),
        P(),
        P(),
        P(),
        P(),
        P(),
        P(),
        P(),
        P(),
        P(),
        P(),
    )
    return jax.shard_map(
        per_device,
        mesh=mesh,
        in_specs=placed,
        out_specs=(
            P("rows", "imgs", None, None),
            P("rows", "imgs", None, None),
            P(),
            P(),
            P(),
            P(),
            P(),
            P(),
            P(),
            P(),
            P(),
            P(),
            P(),
            P(),
            P(),
            P(),
            P(),
            P(),
            P(),
        ),
        check_vma=False,
    )
```

```python
import math

import jax
import jax.numpy as jnp
from jax import lax
from jax.experimental import pallas as pl
from jax.experimental.pallas import tpu as pltpu
from jax.sharding import PartitionSpec as P

GROUPS = 32
H = 32


EPSILON = 1e-06


def padded_2(block, sides, width):
    for axis, dim in sides:
        count = lax.axis_size(axis)
        forward = [(i, i + 1) for i in range(count - 1)]
        backward = [(target, source) for source, target in forward]
        low = lax.ppermute(
            lax.slice_in_dim(block, block.shape[dim] - width, None, axis=dim), axis, forward
        )
        high = lax.ppermute(lax.slice_in_dim(block, 0, width, axis=dim), axis, backward)
        block = jnp.concatenate([low, block, high], axis=dim)
    return block


def sigmoid_pair(tensor):
    logistic = jax.nn.sigmoid(tensor)
    return (tensor * logistic, logistic * (1.0 + tensor * (1.0 - logistic)))


def group_view(tensor):
    height, images, across, channels = tensor.shape
    return tensor.reshape(height, images, across, GROUPS, channels // GROUPS)


def spread_back(statistic):
    return statistic[None, :, None, :, None]


def norm_forward(tensor, norm_gain, norm_offset):
    grouped = group_view(tensor)
    members = H * tensor.shape[2] * (tensor.shape[3] // GROUPS)
    centre = lax.psum(jnp.sum(grouped, axis=(0, 2, 4)), "rows") / members
    centered = grouped - spread_back(centre)
    spread = lax.psum(jnp.sum(jnp.square(centered), axis=(0, 2, 4)), "rows") / members
    factor = lax.rsqrt(spread + EPSILON)
    normed = (centered * spread_back(factor)).reshape(tensor.shape)
    return (normed * norm_gain + norm_offset, normed, factor)


def norm_backward(gradient, normed, factor, norm_gain):
    gain_grad = jnp.sum(gradient * normed, axis=(0, 1, 2))
    offset_grad = jnp.sum(gradient, axis=(0, 1, 2))
    scaled = group_view(gradient * norm_gain)
    flat_normed = group_view(normed)
    members = H * gradient.shape[2] * (gradient.shape[3] // GROUPS)
    mean_grad, cross_grad = lax.psum(
        (jnp.sum(scaled, axis=(0, 2, 4)), jnp.sum(scaled * flat_normed, axis=(0, 2, 4))), "rows"
    )
    input_grad = (
        scaled - spread_back(mean_grad / members) - flat_normed * spread_back(cross_grad / members)
    ) * spread_back(factor)
    return (input_grad.reshape(gradient.shape), gain_grad, offset_grad)


def widen(tensor):
    return jnp.pad(tensor, ((0, 0), (0, 0), (1, 1), (0, 0)))


def conv_forward(tensor, kernel, offset):
    height, across = (tensor.shape[0], tensor.shape[2])
    padded = widen(padded_2(tensor, (("rows", 0),), 1))
    summed = jnp.zeros(tensor.shape[:3] + (kernel.shape[3],), jnp.float32)
    for row_off in range(3):
        for col_off in range(3):
            window = padded[row_off : row_off + height, :, col_off : col_off + across, :]
            summed = summed + jnp.einsum(
                "rbwc,cd->rbwd",
                window,
                kernel[row_off, col_off],
                preferred_element_type=jnp.float32,
            )
    return (summed + offset, padded)


def conv_backward(gradient, padded, kernel):
    height, across = (gradient.shape[0], gradient.shape[2])
    beside_all = widen(padded_2(gradient, (("rows", 0),), 1))
    input_grad = jnp.zeros(gradient.shape[:3] + (kernel.shape[2],), jnp.float32)
    tap_grads = []
    for row_off in range(3):
        for col_off in range(3):
            window = beside_all[
                2 - row_off : 2 - row_off + height, :, 2 - col_off : 2 - col_off + across, :
            ]
            input_grad = input_grad + jnp.einsum(
                "rbwd,cd->rbwc",
                window,
                kernel[row_off, col_off],
                preferred_element_type=jnp.float32,
            )
            source = padded[row_off : row_off + height, :, col_off : col_off + across, :]
            tap_grads.append(
                jnp.einsum("rbwc,rbwd->cd", source, gradient, preferred_element_type=jnp.float32)
            )
    kernel_grad = jnp.stack(tap_grads).reshape(kernel.shape)
    offset_grad = jnp.sum(gradient.astype(jnp.float32), axis=(0, 1, 2))
    return (input_grad, kernel_grad, offset_grad)


def linear(tensor, weight):
    return jnp.einsum("rbwc,cd->rbwd", tensor, weight, preferred_element_type=jnp.float32)


def back_linear(gradient, weight):
    return jnp.einsum("rbwd,cd->rbwc", gradient, weight, preferred_element_type=jnp.float32)


def weight_product(tensor, gradient):
    return jnp.einsum("rbwc,rbwd->cd", tensor, gradient, preferred_element_type=jnp.float32)


def image_to_sequence(tensor):
    height, images, across, channels = tensor.shape
    return tensor.transpose(1, 0, 2, 3).reshape(images, height * across, channels)


def from_sequence(sequence, height, across):
    images, length, channels = sequence.shape
    return sequence.reshape(images, height, across, channels).transpose(1, 0, 2, 3)


def reduce_all(gradients):
    flattened = jnp.concatenate([gradient.reshape(-1) for gradient in gradients])
    length = flattened.shape[0]
    devices = lax.axis_size("rows") * lax.axis_size("imgs")
    per_share = -(-length // (devices * 128)) * 128
    padded_len = per_share * devices
    strided = jnp.pad(flattened, (0, padded_len - length)).reshape(per_share, devices).T
    packed = strided.reshape(padded_len // 128, 128)
    my_share = lax.psum_scatter(packed, ("rows", "imgs"), scatter_dimension=0, tiled=True)
    summed_all = lax.all_gather(
        my_share.astype(jnp.bfloat16), ("rows", "imgs"), axis=0, tiled=True
    ).astype(my_share.dtype)
    summed_all = summed_all.reshape(devices, per_share).T.reshape(-1)
    results = []
    offset_at = 0
    for gradient in gradients:
        results.append(summed_all[offset_at : offset_at + gradient.size].reshape(gradient.shape))
        offset_at = offset_at + gradient.size
    return results


def per_device_by_rows(
    features,
    cotangent,
    norm1_gain,
    norm1_shift,
    conv1_kernel,
    conv1_shift,
    norm2_gain,
    norm2_shift,
    conv2_kernel,
    conv2_shift,
    norm3_gain,
    norm3_shift,
    query_weight,
    query_shift,
    key_weight,
    value_weight,
    value_shift,
    out_weight,
    out_shift,
):
    height, images, across, channels = features.shape
    attention_score_scale = 1.0 / math.sqrt(channels)
    inputs = features.astype(jnp.float32)
    norm_one, normed_one, factor_one = norm_forward(inputs, norm1_gain, norm1_shift)
    act_one, slope_one = sigmoid_pair(norm_one)
    conv_one, padded_one = conv_forward(act_one.astype(jnp.bfloat16), conv1_kernel, conv1_shift)
    norm_two, normed_two, factor_two = norm_forward(conv_one, norm2_gain, norm2_shift)
    act_two, slope_two = sigmoid_pair(norm_two)
    conv_two, padded_two = conv_forward(act_two.astype(jnp.bfloat16), conv2_kernel, conv2_shift)
    residual = inputs + conv_two
    norm_three, normed_three, factor_three = norm_forward(residual, norm3_gain, norm3_shift)
    attend_input = norm_three.astype(jnp.bfloat16)
    query_rows = (linear(attend_input, query_weight) + query_shift).astype(jnp.bfloat16)
    key_state_rows = linear(attend_input, key_weight).astype(jnp.bfloat16)
    value_state_rows = (linear(attend_input, value_weight) + value_shift).astype(jnp.bfloat16)
    all_keys, all_values = (
        lax.all_gather(key_state_rows, "rows", axis=0, tiled=True),
        lax.all_gather(value_state_rows, "rows", axis=0, tiled=True),
    )
    query_sequence = image_to_sequence(query_rows)
    key_sequence = image_to_sequence(all_keys)
    value_sequence = image_to_sequence(all_values)
    attention_scores = (
        jnp.einsum("xao,xno->xan", query_sequence, key_sequence, preferred_element_type=jnp.float32)
        * attention_score_scale
    )
    row_peak = jnp.max(attention_scores, axis=-1, keepdims=True)
    log_total = row_peak + jnp.log(
        jnp.sum(jnp.exp(attention_scores - row_peak), axis=-1, keepdims=True)
    )
    weight_tensors = jnp.exp(attention_scores - log_total).astype(jnp.bfloat16)
    attended_seq = jnp.einsum(
        "afj,ajy->afy", weight_tensors, value_sequence, preferred_element_type=jnp.float32
    )
    attention_output = from_sequence(attended_seq.astype(jnp.bfloat16), height, across)
    output = residual + linear(attention_output, out_weight) + out_shift
    out_shift_grad = jnp.sum(cotangent.astype(jnp.float32), axis=(0, 1, 2))
    out_weight_grad = weight_product(attention_output, cotangent)
    mixed_grad = back_linear(cotangent, out_weight).astype(jnp.bfloat16)
    mixed_sequence = image_to_sequence(mixed_grad)
    scores_again = (
        jnp.einsum("xao,xno->xan", query_sequence, key_sequence, preferred_element_type=jnp.float32)
        * attention_score_scale
    )
    probabilities = jnp.exp(scores_again - log_total)
    probability_gradient = jnp.einsum(
        "xao,xno->xan", mixed_sequence, value_sequence, preferred_element_type=jnp.float32
    )
    delta = jnp.sum(probabilities * probability_gradient, axis=-1, keepdims=True)
    score_gradient = (probabilities * (probability_gradient - delta)).astype(jnp.bfloat16)
    query_local = (
        jnp.einsum("afj,ajy->afy", score_gradient, key_sequence, preferred_element_type=jnp.float32)
        * attention_score_scale
    )
    query_grad = from_sequence(query_local, height, across).astype(jnp.bfloat16)
    key_full = (
        jnp.einsum(
            "svt,svz->stz", score_gradient, query_sequence, preferred_element_type=jnp.float32
        )
        * attention_score_scale
    )
    value_full = jnp.einsum(
        "svt,svz->stz",
        probabilities.astype(jnp.bfloat16),
        mixed_sequence,
        preferred_element_type=jnp.float32,
    )
    stacked = from_sequence(jnp.concatenate([key_full, value_full], axis=-1), H, across)
    own_grads = lax.psum_scatter(
        stacked.astype(jnp.bfloat16), "rows", scatter_dimension=0, tiled=True
    ).astype(jnp.float32)
    key_grad = own_grads[..., :channels].astype(jnp.bfloat16)
    value_grad = own_grads[..., channels:].astype(jnp.bfloat16)
    query_weight_grad = weight_product(attend_input, query_grad)
    query_shift_grad = jnp.sum(query_grad.astype(jnp.float32), axis=(0, 1, 2))
    key_weight_grad = weight_product(attend_input, key_grad)
    value_weight_grad = weight_product(attend_input, value_grad)
    value_shift_grad = jnp.sum(value_grad.astype(jnp.float32), axis=(0, 1, 2))
    attend_grad = (
        back_linear(query_grad, query_weight)
        + back_linear(key_grad, key_weight)
        + back_linear(value_grad, value_weight)
    )
    resid_part, norm3_gain_grad, norm3_shift_grad = norm_backward(
        attend_grad, normed_three, factor_three, norm3_gain
    )
    resid_grad = cotangent.astype(jnp.float32) + resid_part
    conv_two_in, conv2_kernel_grad, conv2_shift_grad = conv_backward(
        resid_grad.astype(jnp.bfloat16), padded_two, conv2_kernel
    )
    conv_one_out, norm2_gain_grad, norm2_shift_grad = norm_backward(
        conv_two_in * slope_two, normed_two, factor_two, norm2_gain
    )
    conv_one_in, conv1_kernel_grad, conv1_shift_grad = conv_backward(
        conv_one_out.astype(jnp.bfloat16), padded_one, conv1_kernel
    )
    inputs_part, norm1_gain_grad, norm1_shift_grad = norm_backward(
        conv_one_in * slope_one, normed_one, factor_one, norm1_gain
    )
    features_grad = resid_grad + inputs_part
    reduced = reduce_all(
        [
            norm1_gain_grad,
            norm1_shift_grad,
            conv1_kernel_grad,
            conv1_shift_grad,
            norm2_gain_grad,
            norm2_shift_grad,
            conv2_kernel_grad,
            conv2_shift_grad,
            norm3_gain_grad,
            norm3_shift_grad,
            query_weight_grad,
            query_shift_grad,
            key_weight_grad,
            value_weight_grad,
            value_shift_grad,
            out_weight_grad,
            out_shift_grad,
        ]
    )
    return (output, features_grad) + tuple(reduced)


F32 = jnp.float32
BF16 = jnp.bfloat16
AXES = ("rows", "imgs")
MEGA = 1024 * 1024
TILE = 64
MM_TILE = 256
ACROSS = 32
UNROLLED = 4
FLOPS = 3 * 10**10
BYTES = 1
BRIEF = 10**7
FORWARD_LIMIT = 18
ATTEND_LIMIT = 22
SECOND_GROUPS = (((0, 1, 2), False, "XYNF"),)
FIRST_GROUPS = (((0, 1, 2), False, "XYNF"),)
LINEAR_ORDER = "NFXY"
ORDER_SLOTS = {"X": 2, "Y": 3, "N": 4, "F": 5}
RIDE = "C0"
TAIL = 32
SMALL = 16
PLAN = (
    "W2 D2 O! B0", "W1 L0 B0 O", "D1 C0 O B0", "L0 B0 C0 L0",
    "B0 L0 C0 L0", "B0 C0 L0 B0", "C0 O G C0", "L0 B0 C0 B0",
    "G L0 C0 C0<", "L0 G C0>",
)
STEPS = ("core", "plane_a", "plane_b", "near", "far")
VMEM = pl.BlockSpec(memory_space=pltpu.VMEM)
SMEM = pl.BlockSpec(memory_space=pltpu.SMEM)
HBM = pl.BlockSpec(memory_space=pltpu.HBM)


def shape_of(shape, dtype):
    return jax.ShapeDtypeStruct(shape, dtype)


def kernel_call(
    body, out_shape, in_specs, scratch=(), limit=24, moved=0, flops=FLOPS
):
    return pl.pallas_call(
        body,
        out_shape=out_shape,
        in_specs=in_specs,
        out_specs=jax.tree.map(lambda _: VMEM, out_shape),
        scratch_shapes=list(scratch),
        compiler_params=pltpu.CompilerParams(vmem_limit_bytes=limit * MEGA),
        cost_estimate=pl.CostEstimate(
            flops=flops, bytes_accessed=BYTES * moved, transcendentals=0
        ),
    )


def tiles(total, size, body):
    if total // size <= UNROLLED:
        for index in range(total // size):
            body(index * size)
        return

    def step(index, carry):
        body(pl.multiple_of(index * size, size))
        return carry

    lax.fori_loop(0, total // size, step, 0)


def fold_tiles(total, size, body, carry):
    if total // size <= UNROLLED:
        for index in range(total // size):
            carry = body(index * size, carry)
        return carry

    def step(index, held):
        return body(pl.multiple_of(index * size, size), held)

    return lax.fori_loop(0, total // size, step, carry)


def fold_rows(tensor):
    return jnp.sum(tensor.reshape(tensor.shape[0] // 8, 8, tensor.shape[1]), axis=0)


def column(partial):
    return jnp.sum(partial, axis=0, keepdims=True)


def group_means(same_ref, columns, members):
    channels = columns[0].shape[1]
    place = lax.broadcasted_iota(jnp.int32, (8, channels), 0)
    rows = jnp.zeros((8, channels), F32)
    for number, values in enumerate(columns):
        left = values
        for term in range(3):
            part = left.astype(BF16).astype(F32)
            left = left - part
            rows = jnp.where(place == 3 * number + term, part, rows)
    summed = dot(rows.astype(BF16), same_ref[...])
    return [
        (summed[3 * n : 3 * n + 1] + summed[3 * n + 1 : 3 * n + 2] + summed[3 * n + 2 : 3 * n + 3])
        * (1.0 / members)
        for n in range(len(columns))
    ]


def pivot_sums(values, pivot):
    moved = values - pivot
    return fold_rows(moved), fold_rows(moved * moved)


def norm_stats(same_ref, sums, squares, pivot, total):
    channels = pivot.shape[1]
    size = channels // GROUPS
    sums, squares = column(sums), column(squares)
    (centre,) = group_means(same_ref, [sums + total * pivot], total * size)
    offset = pivot - centre
    (spread,) = group_means(
        same_ref, [squares + offset * (2.0 * sums + total * offset)], total * size
    )
    return centre, lax.rsqrt(spread + EPSILON)


def fill_shifted(cat_ref, at, tile):
    size, channels = tile.shape
    place = lax.broadcasted_iota(jnp.int32, tile.shape, 0) % ACROSS
    before = jnp.where(place == 0, 0.0, pltpu.roll(tile, 1, 0))
    after = jnp.where(place == ACROSS - 1, 0.0, pltpu.roll(tile, size - 1, 0))
    rows = pl.ds(pl.multiple_of(ACROSS + at, ACROSS), size)
    cat_ref[rows, 0:channels] = before.astype(BF16)
    cat_ref[rows, channels : 2 * channels] = tile.astype(BF16)
    cat_ref[rows, 2 * channels : 3 * channels] = after.astype(BF16)


def clear_border(cat_ref):
    total, width = cat_ref.shape
    cat_ref[0:ACROSS, :] = jnp.zeros((ACROSS, width), BF16)
    cat_ref[total - ACROSS : total, :] = jnp.zeros((ACROSS, width), BF16)


def at_rows(at):
    return at if isinstance(at, int) else pl.multiple_of(at, ACROSS)


def window_product(cat_ref, weight_ref, at, size):
    total = None
    for row_off in range(3):
        rows = pl.ds(at_rows(at + row_off * ACROSS), size)
        part = jnp.dot(cat_ref[rows, :], weight_ref[row_off], preferred_element_type=F32)
        total = part if total is None else total + part
    return total


def window_product_turned(cat_ref, weight_ref, at, size):
    channels = weight_ref.shape[2]
    total = None
    for row_off in range(3):
        rows = pl.ds(at_rows(at + (2 - row_off) * ACROSS), size)
        for col_off in range(3):
            low = (2 - col_off) * channels
            tap = weight_ref[row_off, col_off * channels : (col_off + 1) * channels, :]
            part = dot_t(cat_ref[rows, low : low + channels], tap)
            total = part if total is None else total + part
    return total


def dot_t(left, right):
    return lax.dot_general(left, right, (((1,), (1,)), ((), ())), preferred_element_type=F32)


def t_dot(left, right):
    return lax.dot_general(left, right, (((0,), (0,)), ((), ())), preferred_element_type=F32)


def dot(left, right):
    return jnp.dot(left, right, preferred_element_type=F32)


def line(lines_ref, row):
    return lines_ref[row : row + 1, :]


def forward_body(place_ref, *refs):
    pairs = refs[:4]
    (lines_ref, same_ref, weight1_ref, weight2_ref, q_weight_ref, k_weight_ref, v_weight_ref,
     image_ref, act1_ref, conv_ref, act2_ref, resid_ref, stats_ref, norm_ref, q_ref, k_ref, v_ref,
     cat_ref, pivot_ref) = refs[4:]
    total, channels = image_ref.shape
    share = total // 8
    me = place_ref[0]
    for index in range(8):
        at = pl.multiple_of((me ^ index) * share, share)
        image_ref[pl.ds(at, share), :] = pairs[index // 2][index % 2]
    clear_border(cat_ref)
    zero = jnp.zeros((8, channels), F32)

    def activate_all(read, stats, stats_row, gain_row, act_ref):
        centre, factor = stats
        stats_ref[stats_row : stats_row + 1, :] = centre
        stats_ref[stats_row + 1 : stats_row + 2, :] = factor
        scale = factor * line(lines_ref, gain_row)
        shift = line(lines_ref, gain_row + 1) - centre * scale

        def activate(at):
            held = read(at) * scale + shift
            act = held * jax.nn.sigmoid(held)
            act_ref[pl.ds(at, TILE), :] = act.astype(BF16)
            fill_shifted(cat_ref, at, act)

        tiles(total, TILE, activate)

    def read_image(at):
        return image_ref[pl.ds(at, TILE), :].astype(F32)

    pivot1 = read_image(0)[0:1, :]

    def sum_image(at, held):
        sums, squares = pivot_sums(read_image(at), pivot1)
        return held[0] + sums, held[1] + squares

    sums, squares = fold_tiles(total, TILE, sum_image, (zero, zero))
    stats1 = norm_stats(same_ref, sums, squares, pivot1, total)
    activate_all(read_image, stats1, 0, 0, act1_ref)

    def convolve_all(weight_ref, bias, more, target_ref):
        def convolve(at, held):
            rows = pl.ds(at, MM_TILE)
            values = window_product(cat_ref, weight_ref, at, MM_TILE) + bias
            if more is not None:
                values = values + more[rows, :].astype(F32)

            if isinstance(at, int):
                if at == 0:
                    pivot_ref[0:1, :] = values[0:1, :]
            else:

                @pl.when(at == 0)
                def _():
                    pivot_ref[0:1, :] = values[0:1, :]

            target_ref[rows, :] = values
            sums, squares = pivot_sums(values, pivot_ref[0:1, :])
            return held[0] + sums, held[1] + squares

        sums, squares = fold_tiles(total, MM_TILE, convolve, (zero, zero))
        return norm_stats(same_ref, sums, squares, pivot_ref[0:1, :], total)

    stats2 = convolve_all(weight1_ref, line(lines_ref, 6), None, conv_ref)
    activate_all(lambda at: conv_ref[pl.ds(at, TILE), :], stats2, 2, 2, act2_ref)
    centre3, factor3 = convolve_all(weight2_ref, line(lines_ref, 7), image_ref, resid_ref)
    stats_ref[4:5, :] = centre3
    stats_ref[5:6, :] = factor3
    stats_ref[6:8, :] = jnp.zeros((2, channels), F32)
    scale3 = factor3 * line(lines_ref, 4)
    shift3 = line(lines_ref, 5) - centre3 * scale3
    q_shift, v_shift = line(lines_ref, 8), line(lines_ref, 9)

    def project(at):
        rows = pl.ds(at, MM_TILE)
        held = (resid_ref[rows, :] * scale3 + shift3).astype(BF16)
        norm_ref[rows, :] = held
        q_ref[rows, :] = (dot(held, q_weight_ref[...]) + q_shift).astype(BF16)
        k_ref[rows, :] = dot(held, k_weight_ref[...]).astype(BF16)
        v_ref[rows, :] = (dot(held, v_weight_ref[...]) + v_shift).astype(BF16)

    tiles(total, MM_TILE, project)


def lane_half(part, half):
    return pl.ds(pl.multiple_of(part * half, half), half)


def z_bits(core):
    return 2 << core, 4 >> core


def return_pieces(place_ref, out_ref, sent_ref, kept_ref):
    share = out_ref.shape[0] // 8
    me, core = place_ref[0], place_ref[1]
    for target, side in ((kept_ref, 0), (sent_ref, 1)):
        first, second = z_bits(core if side == 0 else 1 - core)
        for index in range(4):
            offset = side + (index // 2) * first + (index % 2) * second
            at = pl.multiple_of((me ^ offset) * share, share)
            target[index] = out_ref[pl.ds(at, share), :]


def attention_body(place_ref, *refs):
    cot_pieces = refs[:4]
    (q_ref, k_ref, v_ref, norm_ref, resid_ref, stats_ref, lines_ref, same_ref,
     o_weight_ref, q_weight_ref, k_weight_ref, v_weight_ref) = refs[4:16]
    (out_sent_ref, out_kept_ref, sent_ref, kept_ref, small_ref, d_resid_ref, d_conv_ref, d_sent_ref,
     cot_ref, out_ref, mixed_ref, d_mixed_ref, d_q_ref, d_k_ref, d_v_ref,
     weights_ref, d_scores_ref) = refs[16:]
    total, channels = q_ref.shape
    share = total // 8
    scale = 1.0 / math.sqrt(channels)
    me = place_ref[0]
    for index in range(8):
        at = pl.multiple_of((me ^ index) * share, share)
        cot_ref[pl.ds(at, share), :] = cot_pieces[index // 2][index % 2]
    o_shift = line(lines_ref, 10)
    zero = jnp.zeros((8, channels), F32)

    def attend(at, held):
        rows = pl.ds(at, MM_TILE)
        query = q_ref[rows, :]
        cot = cot_ref[rows, :]
        scores = dot_t(query, k_ref[...]) * scale
        d_mixed = dot_t(cot, o_weight_ref[...]).astype(BF16)
        d_mixed_ref[rows, :] = d_mixed
        d_prob = dot_t(d_mixed, v_ref[...])
        exps = jnp.exp(scores - jnp.max(scores, axis=-1, keepdims=True))
        probs = exps * (1.0 / jnp.sum(exps, axis=-1, keepdims=True))
        weights = probs.astype(BF16)
        weights_ref[rows, :] = weights
        mixed = dot(weights, v_ref[...]).astype(BF16)
        mixed_ref[rows, :] = mixed
        out_ref[rows, :] = (
            resid_ref[rows, :] + dot(mixed, o_weight_ref[...]) + o_shift
        ).astype(BF16)
        delta = jnp.sum(probs * d_prob, axis=-1, keepdims=True)
        d_scores = (probs * (d_prob - delta)).astype(BF16)
        d_scores_ref[rows, :] = d_scores
        d_query = (dot(d_scores, k_ref[...]) * scale).astype(BF16)
        d_q_ref[rows, :] = d_query
        return held[0] + fold_rows(cot.astype(F32)), held[1] + fold_rows(d_query.astype(F32))

    cot_sums, d_q_sums = fold_tiles(total, MM_TILE, attend, (zero, zero))
    return_pieces(place_ref, out_ref, out_sent_ref, out_kept_ref)

    def to_keys(at, held):
        rows = pl.ds(at, MM_TILE)
        d_k_ref[rows, :] = (t_dot(d_scores_ref[:, rows], q_ref[...]) * scale).astype(BF16)
        d_value = t_dot(weights_ref[:, rows], d_mixed_ref[...]).astype(BF16)
        d_v_ref[rows, :] = d_value
        return held + fold_rows(d_value.astype(F32))

    d_v_sums = fold_tiles(total, MM_TILE, to_keys, zero)
    half = channels // 2
    core = place_ref[1]
    for index, (left, right) in enumerate(
        ((norm_ref, d_q_ref), (norm_ref, d_k_ref), (norm_ref, d_v_ref), (mixed_ref, cot_ref))
    ):
        for target, part in ((sent_ref, 1 - core), (kept_ref, core)):
            target[index] = t_dot(left[...], right[:, lane_half(part, half)]).astype(BF16)

    centre, factor = stats_ref[4:5, :], stats_ref[5:6, :]
    gain = line(lines_ref, 4)

    def back(at, held):
        rows = pl.ds(at, MM_TILE)
        grad = (
            dot_t(d_q_ref[rows, :], q_weight_ref[...])
            + dot_t(d_k_ref[rows, :], k_weight_ref[...])
            + dot_t(d_v_ref[rows, :], v_weight_ref[...])
        )
        d_resid_ref[rows, :] = grad
        normed = (resid_ref[rows, :] - centre) * factor
        return held[0] + fold_rows(grad), held[1] + fold_rows(grad * normed)

    sums = fold_tiles(total, MM_TILE, back, (zero, zero))
    shift_grad, gain_grad, o_shift_grad, q_shift_grad, v_shift_grad = [
        column(part) for part in (*sums, cot_sums, d_q_sums, d_v_sums)
    ]
    members = total * (channels // GROUPS)
    mean_grad, cross_grad = group_means(same_ref, [shift_grad * gain, gain_grad * gain], members)

    def finish(at, held):
        rows = pl.ds(at, TILE)
        normed = (resid_ref[rows, :] - centre) * factor
        grad = cot_ref[rows, :].astype(F32) + factor * (
            d_resid_ref[rows, :] * gain - mean_grad - normed * cross_grad
        )
        d_resid_ref[rows, :] = grad
        rounded = grad.astype(BF16)
        d_conv_ref[rows, :] = rounded
        d_sent_ref[rows, :] = d_conv_ref[rows, lane_half(1 - core, half)]
        return held + fold_rows(rounded.astype(F32))

    conv_shift_grad = column(fold_tiles(total, TILE, finish, zero))
    small_ref[0:1, :] = gain_grad
    small_ref[1:2, :] = shift_grad
    small_ref[2:3, :] = q_shift_grad
    small_ref[3:4, :] = v_shift_grad
    small_ref[4:5, :] = o_shift_grad
    small_ref[5:6, :] = conv_shift_grad
    small_ref[6:8, :] = jnp.zeros((2, channels), F32)


def kernel_grad_body(groups, place_ref, act_ref, act_got_ref, grad_ref, grad_got_ref, *refs):
    linear = any(carries for _, carries, _ in groups)
    more, refs = (refs[:2], refs[2:]) if linear else ((), refs)
    parts, (cat_ref, cat_got_ref, turned_ref, turned_got_ref) = refs[: 2 * len(groups)], refs[2 * len(groups) :]
    total, channels = act_ref.shape
    half = channels // 2
    core = place_ref[1]
    clear_border(cat_ref)
    clear_border(cat_got_ref)

    def fill(at):
        rows = pl.ds(at, TILE)
        fill_shifted(cat_ref, at, grad_ref[rows, lane_half(core, half)].astype(F32))
        fill_shifted(cat_got_ref, at, grad_got_ref[rows, :].astype(F32))

    tiles(total, TILE, fill)
    turned_ref[...] = act_ref[...].T
    turned_got_ref[...] = act_got_ref[...].T
    for number, (kernel_rows, carries, order) in enumerate(groups):
        bit = place_ref[ORDER_SLOTS[order[0]]]
        for target, part in ((parts[2 * number], 1 - bit), (parts[2 * number + 1], bit)):
            rows = pl.ds(pl.multiple_of(part * half, half), half)
            for index, row_off in enumerate(kernel_rows):
                span = pl.ds((2 - row_off) * ACROSS, total)
                product = (
                    dot(turned_ref[rows, :], cat_ref[span, :])
                    + dot(turned_got_ref[rows, :], cat_got_ref[span, :])
                ).astype(BF16)
                for col_off in range(3):
                    at = (3 * index + col_off) * half
                    low = (2 - col_off) * half
                    target[at : at + half, :] = product[:, low : low + half]
            if carries:
                for index in range(4):
                    at = (3 * len(kernel_rows) + index) * half
                    target[at : at + half, :] = (
                        more[0][index, rows, :].astype(F32) + more[1][index, rows, :].astype(F32)
                    ).astype(BF16)


def linear_halves(slot, place_ref, kept_ref, got_ref, sent_out, kept_out):
    bit = place_ref[slot]
    count, rows, half = kept_ref.shape
    rows //= 2
    for target, part in ((sent_out, 1 - bit), (kept_out, bit)):
        span = pl.ds(pl.multiple_of(part * rows, rows), rows)
        for index in range(count):
            target[index * rows : (index + 1) * rows, :] = (
                kept_ref[index, span, :].astype(F32) + got_ref[index, span, :].astype(F32)
            ).astype(BF16)


def input_grad_body(with_rest, stats_row, place_ref, *refs):
    grad_ref, weight_ref, source_ref, stats_ref, lines_ref, same_ref = refs[:6]
    if with_rest:
        rest_ref, small_two_ref, small_three_ref = refs[6:9]
    else:
        linear_kept_ref, linear_got_ref = refs[6:8]
    refs = refs[9:] if with_rest else refs[8:]
    if with_rest:
        sent_ref, kept_ref, small_ref, cat_ref, held_ref, out_ref, rows_ref = refs
    else:
        out_ref, d_sent_ref, small_ref, linear_sent_out, linear_kept_out, cat_ref, held_ref = refs
    core = place_ref[1]
    total, channels = grad_ref.shape
    centre = stats_ref[stats_row : stats_row + 1, :]
    factor = stats_ref[stats_row + 1 : stats_row + 2, :]
    gain, shift = line(lines_ref, stats_row), line(lines_ref, stats_row + 1)
    clear_border(cat_ref)

    def fill(at):
        fill_shifted(cat_ref, at, grad_ref[pl.ds(at, TILE), :].astype(F32))

    tiles(total, TILE, fill)

    zero = jnp.zeros((8, channels), F32)

    def product(at, held):
        rows = pl.ds(at, MM_TILE)
        normed = (source_ref[rows, :].astype(F32) - centre) * factor
        pre = normed * gain + shift
        logistic = jax.nn.sigmoid(pre)
        slope = logistic * (1.0 + pre * (1.0 - logistic))
        grad = window_product_turned(cat_ref, weight_ref, at, MM_TILE) * slope
        held_ref[rows, :] = grad
        return held[0] + fold_rows(grad), held[1] + fold_rows(grad * normed)

    shift_sum, gain_sum = fold_tiles(total, MM_TILE, product, (zero, zero))
    shift_grad, gain_grad = column(shift_sum), column(gain_sum)
    members = total * (channels // GROUPS)
    mean_grad, cross_grad = group_means(same_ref, [shift_grad * gain, gain_grad * gain], members)

    def finish(at, held):
        rows = pl.ds(at, TILE)
        normed = (source_ref[rows, :].astype(F32) - centre) * factor
        grad = factor * (held_ref[rows, :] * gain - mean_grad - normed * cross_grad)
        if with_rest:
            grad = grad + rest_ref[rows, :]
        rounded = grad.astype(BF16)
        out_ref[rows, :] = rounded
        if not with_rest:
            d_sent_ref[rows, :] = out_ref[rows, lane_half(1 - core, channels // 2)]
        return held + fold_rows(rounded.astype(F32))

    out_sum = column(fold_tiles(total, TILE, finish, zero))
    if not with_rest:
        linear_halves(
            ORDER_SLOTS[LINEAR_ORDER[0]], place_ref, linear_kept_ref, linear_got_ref, linear_sent_out,
            linear_kept_out,
        )
        small_ref[0:1, :] = gain_grad
        small_ref[1:2, :] = shift_grad
        small_ref[2:3, :] = out_sum
        small_ref[3:8, :] = jnp.zeros((5, channels), F32)
        return
    return_pieces(place_ref, out_ref, sent_ref, kept_ref)
    rows_ref[0:1, :] = gain_grad
    rows_ref[1:2, :] = shift_grad
    rows_ref[2:5, :] = small_two_ref[0:3, :]
    rows_ref[5:11, :] = small_three_ref[0:6, :]
    rows_ref[11:SMALL, :] = jnp.zeros((SMALL - 11, channels), F32)
    half = channels // 2
    small_ref[0:SMALL, :] = rows_ref[:, 0:half].astype(BF16)
    small_ref[SMALL:TAIL, :] = rows_ref[:, half:channels].astype(BF16)


def pack_by_core_body(place_ref, block_ref, sent_ref, kept_ref):
    me = place_ref[0]
    for target, side in ((kept_ref, 0), (sent_ref, 1)):
        for index in range(4):
            for row in range(block_ref.shape[0]):
                rows = pl.ds(row * ACROSS, ACROSS)
                target[index, rows, :] = block_ref[row, me ^ (2 * index + side)]


def pair_body(place_ref, kept_ref, got_ref, *refs):
    count = (len(refs) - 5) // 2
    staged, pair_refs, sems = refs[:count], refs[count : count + 4], refs[-1]
    targets = refs[count + 4 : 2 * count + 4]
    copies = [
        pltpu.make_async_copy(staged[index], targets[index], sems.at[index])
        for index in range(count)
    ]
    for copy in copies:
        copy.start()
    for index in range(4):
        pair_refs[index][0] = kept_ref[index]
        pair_refs[index][1] = got_ref[index]
    if count:
        same_ref = refs[2 * count + 4]
        one, two = (lax.broadcasted_iota(jnp.int32, same_ref.shape, dim) for dim in (0, 1))
        size = same_ref.shape[0] // GROUPS
        same_ref[...] = jnp.where(one // size == two // size, 1.0, 0.0).astype(BF16)
    for copy in copies:
        copy.wait()


def swap_by_core(place, block, staged=()):
    rows, _, across, channels = block.shape
    four = shape_of((4, rows * across, channels), BF16)
    sent, kept = kernel_call(
        pack_by_core_body, [four] * 2, [SMEM, VMEM], limit=8, moved=2 * MEGA, flops=BRIEF
    )(place, block)
    got = exchange(sent, "core")
    pair = shape_of((2, rows * across, channels), BF16)
    results = kernel_call(
        pair_body,
        [pair] * 4
        + [shape_of(array.shape, array.dtype) for array in staged]
        + [shape_of((channels, channels), BF16)] * bool(staged),
        [SMEM, VMEM, VMEM] + [HBM] * len(staged),
        [pltpu.SemaphoreType.DMA((max(len(staged), 1),))],
        limit=16 if staged else 8,
        moved=2 * MEGA,
        flops=BRIEF,
    )(place, kept, got, *staged)
    return results[:4], results[4:]


def swap_pieces(pieces, unit):
    count = len(pieces)
    return [pieces[0]] + [
        lax.ppermute(pieces[k], "rows", [(r, r ^ (unit * k)) for r in range(count * unit)])
        for k in range(1, count)
    ]


def partner_table(kind):
    table = []
    for row in range(8):
        for img in range(4):
            core = row & 1
            if kind == "core":
                other = (row ^ 1, img)
            elif kind == "near":
                other = (row ^ (4 if core else 2), img)
            elif kind == "far":
                other = (row ^ (2 if core else 4), img)
            elif kind == "plane_a":
                other = (row, img ^ (2 if core else 1))
            else:
                other = (row, img ^ (1 if core else 2))
            table.append((row * 4 + img, other[0] * 4 + other[1]))
    return table


def exchange(tensor, kind):
    return lax.ppermute(tensor, AXES, partner_table(kind))


def own_place():
    row, img = lax.axis_index("rows"), lax.axis_index("imgs")
    core, near, far = row & 1, (row >> 1) & 1, (row >> 2) & 1
    low, high = img & 1, (img >> 1) & 1
    plane_a = jnp.where(core == 1, high, low)
    plane_b = jnp.where(core == 1, low, high)
    first_z = jnp.where(core == 1, far, near)
    second_z = jnp.where(core == 1, near, far)
    return jnp.stack([row, core, plane_a, plane_b, first_z, second_z, row, row]).astype(jnp.int32)


def add_tails(target, target_at, kept_ref, got_ref, at):
    target[target_at : target_at + TAIL, :] = (
        kept_ref[at : at + TAIL, :].astype(F32) + got_ref[at : at + TAIL, :].astype(F32)
    ).astype(BF16)


def add_split(chain, slot, place_ref, ins, outs):
    kept_ref, got_ref = ins[:2]
    count, rows = chain.count, chain.rows
    half = rows // 2
    bit = place_ref[slot]

    def one(index, carry):
        for target, part in zip(outs, (1 - bit, bit)):
            span = pl.ds(pl.multiple_of(index * rows + part * half, half), half)
            target[pl.ds(pl.multiple_of(index * half, half), half), :] = (
                kept_ref[span, :].astype(F32) + got_ref[span, :].astype(F32)
            ).astype(BF16)
        return carry

    lax.fori_loop(0, count, one, 0)
    if chain.small is not None:
        for target in outs:
            if len(ins) > 2:
                target[count * half : count * half + TAIL, :] = ins[2][...]
            else:
                add_tails(target, count * half, kept_ref, got_ref, count * rows)


def add_last(chain, slot, place_ref, ins, outs):
    outs[0][...] = (ins[0][...].astype(F32) + ins[1][...].astype(F32)).astype(BF16)


def join(chain, slot, place_ref, ins, outs):
    count, rows = chain.count, chain.rows
    bit = place_ref[slot]

    def one(index, carry):
        for source, part in zip(ins, (bit, 1 - bit)):
            span = pl.ds(pl.multiple_of((2 * index + part) * rows, rows), rows)
            outs[0][span, :] = source[pl.ds(pl.multiple_of(index * rows, rows), rows), :]
        return carry

    lax.fori_loop(0, count, one, 0)
    if chain.small is not None:
        at = count * rows
        if slot == ORDER_SLOTS["X"]:
            add_tails(outs[0], 2 * at, ins[0], ins[1], at)
        else:
            outs[0][2 * at : 2 * at + TAIL, :] = ins[0][at : at + TAIL, :]


def turn_pairs(chain, slot, place_ref, ins, outs):
    kept_ref, got_ref = ins
    for target, part in zip(outs, (1, 0)):
        for index in range(2):
            if slot == 0:
                target[index] = kept_ref[2 * part + index]
                target[2 + index] = got_ref[2 * part + index]
            else:
                target[index] = kept_ref[2 * index + part]
                target[2 + index] = got_ref[2 * index + part]


def spread(chain, slot, place_ref, ins, outs):
    me, core = place_ref[0], place_ref[1]
    first, second = z_bits(core)
    out_ref = outs[0]
    for source, side in zip(ins, (0, 1)):
        for index in range(4):
            image = me ^ ((index % 2) + (index // 2) * first + side * second)
            for row in range(out_ref.shape[0]):
                rows = pl.ds(row * ACROSS, ACROSS)
                out_ref[row, image] = source[index, rows, :].astype(F32)


def join_last(place, sources, targets):
    half = sources[0][0].shape[1]
    rows = 2 * half
    sides = [side for _, side in sources]
    count = sum(target[4] for target in targets)
    wholes = [target[0] for target in targets if target[0] is not None]

    def body(place_ref, *refs):
        source_refs = refs[: len(sources)]
        out_refs = refs[len(sources) + len(wholes) : -2]
        held_ref, sems = refs[-2:]
        core = place_ref[1]
        copies = []
        for out_ref, (_, _, there, here, planes) in zip(out_refs, targets):
            for plane in range(planes):
                for number, side in enumerate(sides):
                    index = len(copies)
                    at = (here + plane) * rows
                    held_ref[index] = source_refs[number][at : at + rows, :].astype(F32)
                    part = 1 - core if side else core
                    copy = pltpu.make_async_copy(
                        held_ref.at[index],
                        out_ref.at[there + plane, :, lane_half(part, half)],
                        sems.at[index],
                    )
                    copy.start()
                    copies.append(copy)
        for copy in copies:
            copy.wait()

    anywhere = pl.BlockSpec(memory_space=pl.ANY)
    aliases, taken = {}, 0
    for number, target in enumerate(targets):
        if target[0] is not None:
            aliases[1 + len(sources) + taken] = number
            taken += 1
    slots = count * len(sources)
    return pl.pallas_call(
        body,
        out_shape=[shape_of((target[1], rows, rows), F32) for target in targets],
        in_specs=[SMEM] + [VMEM] * len(sources) + [anywhere] * len(wholes),
        out_specs=[anywhere] * len(targets),
        input_output_aliases=aliases,
        scratch_shapes=[pltpu.VMEM((slots, rows, half), F32), pltpu.SemaphoreType.DMA((slots,))],
        compiler_params=pltpu.CompilerParams(vmem_limit_bytes=(slots // 2 + 6) * MEGA),
        cost_estimate=pl.CostEstimate(
            flops=FLOPS, bytes_accessed=BYTES * 6 * slots * rows * half, transcendentals=0
        ),
    )(place, *[array for array, _ in sources], *wholes)


def small_last(place, mine, got):
    half = mine.shape[1]
    block = mine.shape[0] // TAIL - 1

    def body(place_ref, mine_ref, got_ref, out_ref):
        total = mine_ref[...].astype(F32) + got_ref[...].astype(F32)
        out_ref[:, 0:half] = total[0:SMALL]
        out_ref[:, half : 2 * half] = total[SMALL:TAIL]

    spec = pl.BlockSpec((TAIL, half), lambda i: (block, 0))
    return pl.pallas_call(
        body,
        grid=(1,),
        out_shape=shape_of((SMALL, 2 * half), F32),
        in_specs=[SMEM, spec, spec],
        out_specs=pl.BlockSpec((SMALL, 2 * half), lambda i: (0, 0)),
        cost_estimate=pl.CostEstimate(flops=FLOPS, bytes_accessed=MEGA, transcendentals=0),
    )(place, mine, got)


def tie(values, earlier):
    return lax.optimization_barrier(tuple(values) + tuple(earlier))[: len(values)]


def after(values, token):
    tied = lax.optimization_barrier(tuple(values) + (token,))
    return tied[:-1]


class SumChain:
    def __init__(self, sent, kept, order):
        self.kept, self.at, self.small = kept, 0, None
        self.rows = kept.shape[1]
        self.count = kept.shape[0] // self.rows
        self.slots = [ORDER_SLOTS[letter] for letter in order]
        self.got = exchange(sent, STEPS[self.slots[0] - 1])

    def inputs(self):
        with_small = self.small is not None and self.at == 0
        return [self.kept, self.got] + ([self.small] if with_small else [])

    def todo(self):
        tail = 0 if self.small is None else TAIL
        lanes = self.kept.shape[1]
        at, size = self.at, self.count * self.rows
        if at < 3:
            return add_split, self.slots[at + 1], [shape_of((size // 2 + tail, lanes), BF16)] * 2
        if at == 3:
            return add_last, 0, [shape_of((size + tail, lanes), BF16)]
        return join, self.slots[7 - at], [shape_of((2 * size + tail, lanes), BF16)]

    def take(self, outs):
        at = self.at
        self.at += 1
        self.kept = outs[-1]
        if at < 3:
            self.rows //= 2
            slot = self.slots[at + 1]
        elif at == 3:
            slot = self.slots[3]
        else:
            self.rows *= 2
            slot = self.slots[6 - at] if at < 7 else 1
        self.got = exchange(outs[0], STEPS[slot - 1])


class ReturnChain:
    def __init__(self, sent, kept, block_shape):
        self.kept, self.at, self.block_shape = kept, 0, block_shape
        self.got = exchange(sent, "core")

    def inputs(self):
        return [self.kept, self.got]

    def todo(self):
        if self.at < 2:
            return turn_pairs, self.at, [shape_of(self.kept.shape, BF16)] * 2
        return spread, 0, [shape_of(self.block_shape, F32)]

    def take(self, outs):
        self.kept = outs[-1]
        if self.at < 2:
            self.got = exchange(outs[0], ("near", "far")[self.at])
        self.at += 1


def step(place, chain, token):
    work, slot, shapes = chain.todo()
    arrays = after(chain.inputs(), token)

    def body(place_ref, *refs):
        work(chain, slot, place_ref, refs[: len(arrays)], refs[len(arrays) :])

    moved = 2 * sum(a.size * a.dtype.itemsize for a in arrays)
    results = kernel_call(
        body, shapes, [SMEM] + [VMEM] * len(arrays), limit=3 + moved // MEGA, moved=moved
    )(place, *arrays)
    chain.take(results)
    return results[0]


def per_device_by_images(
    features,
    cotangent,
    norm1_gain,
    norm1_shift,
    conv1_kernel,
    conv1_shift,
    norm2_gain,
    norm2_shift,
    conv2_kernel,
    conv2_shift,
    norm3_gain,
    norm3_shift,
    query_weight,
    query_shift,
    key_weight,
    value_weight,
    value_shift,
    out_weight,
    out_shift,
):
    rows, images, across, channels = features.shape
    total = rows * images * across
    place = own_place()
    lines = jnp.stack([
        norm1_gain, norm1_shift, norm2_gain, norm2_shift, norm3_gain, norm3_shift,
        conv1_shift, conv2_shift, query_shift, value_shift, out_shift, out_shift,
    ] + [out_shift] * 4)

    image = shape_of((total, channels), BF16)
    image_f32 = shape_of((total, channels), F32)
    piece = shape_of((total // 8, channels), BF16)
    stats_shape = shape_of((8, channels), F32)
    cat = pltpu.VMEM((total + 2 * across, 3 * channels), BF16)
    bf16_image = pltpu.VMEM((total, channels), BF16)
    f32_image = pltpu.VMEM((total, channels), F32)
    tall = (3, 3 * channels, channels)

    feature_pairs, _ = swap_by_core(place, features)
    feature_pieces = swap_pieces(feature_pairs, 2)
    cot_pairs, (weight1, weight2, q_weight, k_weight, v_weight, o_weight, same) = swap_by_core(
        place,
        after((cotangent,), feature_pairs[0])[0],
        (conv1_kernel.reshape(tall), conv2_kernel.reshape(tall), query_weight, key_weight,
         value_weight, out_weight),
    )
    cot_near = tie(cot_pairs, feature_pieces[1:2])
    cot_far = tie(cot_pairs, feature_pieces[1:])
    cot_pieces = swap_pieces([cot_pairs[0], cot_near[1], *cot_far[2:]], 2)

    (image_in, act_one, conv_one, act_two, residual, stats, normed, query, key, value) = kernel_call(
        forward_body,
        [image, image, image_f32, image, image_f32, stats_shape] + [image] * 4,
        [SMEM] + [VMEM] * 11,
        [cat, pltpu.VMEM((8, channels), F32)],
        limit=FORWARD_LIMIT,
        moved=24 * MEGA,
        flops=5 * 10**9,
    )(place, *feature_pieces, lines, same, weight1, weight2, q_weight, k_weight, v_weight)
    act_two_got = exchange(act_two, "core")
    half = channels // 2
    four = shape_of((4, total // 8, channels), BF16)
    halves = shape_of((4, channels, half), BF16)
    grad_half = shape_of((total, half), BF16)
    (out_sent, out_kept, linear_sent, linear_kept, small_three, d_resid, d_conv_two,
     d_sent_two) = kernel_call(
        attention_body,
        [four, four, halves, halves, stats_shape, image_f32, image, grad_half],
        [SMEM] + [VMEM] * 16,
        [bf16_image] * 7 + [pltpu.VMEM((total, total), BF16)] * 2,
        limit=ATTEND_LIMIT,
        moved=16 * MEGA,
    )(
        place, *cot_pieces, query, key, value, normed, residual, stats, lines, same,
        o_weight, q_weight, k_weight, v_weight,
    )
    d_got_two = exchange(d_sent_two, "core")
    linear_got = exchange(linear_sent, "core")
    half_cat = pltpu.VMEM((total + 2 * across, 3 * half), BF16)

    def kernel_grad(made, *arrays):
        parts = []
        for kernel_rows, carries, _ in made:
            planes = 3 * len(kernel_rows) + 4 * carries
            parts += [shape_of((planes * half, half), BF16)] * 2
        return kernel_call(
            lambda *refs: kernel_grad_body(made, *refs), parts, [SMEM] + [VMEM] * len(arrays),
            [half_cat] * 2 + [pltpu.VMEM((channels, total), BF16)] * 2,
            limit=14, moved=8 * MEGA,
        )(place, *arrays)

    linear_part = shape_of((4 * half, half), BF16)

    def second_input_grad(grad):
        return kernel_call(
            lambda *refs: input_grad_body(False, 2, *refs),
            [image, grad_half, stats_shape, linear_part, linear_part],
            [SMEM] + [VMEM] * 8, [cat, f32_image],
            limit=16, moved=10 * MEGA,
        )(place, grad, weight2, conv_one, stats, lines, same, linear_kept, linear_got)

    def first_input_grad(grad):
        return kernel_call(
            lambda *refs: input_grad_body(True, 0, *refs),
            [four, four, shape_of((TAIL, half), BF16)],
            [SMEM] + [VMEM] * 9,
            [cat, f32_image, bf16_image, pltpu.VMEM((SMALL, channels), F32)],
            limit=16, moved=10 * MEGA,
        )(place, grad, weight1, image_in, stats, lines, same, d_resid, small_two, small_three)

    chains, groups, sums = {}, {}, {}

    def begin(letter, parts, made):
        for number, group in enumerate(made):
            name = letter + str(number)
            chains[name] = SumChain(*parts[2 * number : 2 * number + 2], group[2])
            groups[name] = group

    def end(name, token, sides):
        chain = chains[name]
        arrays = after([(chain.kept, chain.got)[side] for side in sides], token)
        sources = list(zip(arrays, sides))
        kernel_rows, carries, _ = groups[name]
        taps = 3 * len(kernel_rows)
        targets = {}
        if taps:
            targets[name[0]] = (sums.get(name[0]), 9, 3 * kernel_rows[0], 0, taps)
        if carries:
            targets["linear"] = (None, 4, 0, taps, 4)
        made = join_last(place, sources, list(targets.values()))
        sums.update(zip(targets, made))
        if chain.small is not None and 1 in sides:
            sums["small"] = small_last(place, chain.kept, arrays[-1])
        return made[0]

    token = small_three
    for event in " ".join(PLAN).split():
        if event == "W2":
            parts = kernel_grad(
                SECOND_GROUPS, act_two, act_two_got, after((d_conv_two,), token)[0], d_got_two
            )
            begin("B", parts, SECOND_GROUPS)
            token = parts[0]
            act_one_got = exchange(after((act_one,), token)[0], "core")
        elif event == "D2":
            d_conv_one, d_sent_one, small_two, *parts = second_input_grad(
                after((d_conv_two,), token)[0]
            )
            begin("L", parts, (((), True, LINEAR_ORDER),))
            d_got_one = exchange(d_sent_one, "core")
            token = small_two
        elif event == "W1":
            parts = kernel_grad(
                FIRST_GROUPS, act_one, act_one_got, after((d_conv_one,), token)[0], d_got_one
            )
            begin("C", parts, FIRST_GROUPS)
            token = parts[0]
        elif event == "D1":
            sent, kept, small = first_input_grad(after((d_conv_one,), token)[0])
            token = small
            chains["G"] = ReturnChain(sent, kept, features.shape)
            chains[RIDE].small = small
        elif event == "O!":
            chains["O"] = ReturnChain(*after((out_sent, out_kept), token), features.shape)
        elif event.endswith("<"):
            token = end(event[:-1], token, (0,))
        elif event.endswith(">"):
            token = end(event[:-1], token, (1,))
        elif event in groups and chains[event].at == 8:
            token = end(event, token, (0, 1))
        else:
            token = step(place, chains[event], token)

    output, features_grad = chains["O"].kept, chains["G"].kept
    small = sums["small"]
    linear_sum, conv2_sum, conv1_sum = sums["linear"], sums["B"], sums["C"]
    return (
        output,
        features_grad,
        small[0],
        small[1],
        conv1_sum.reshape(conv1_kernel.shape),
        small[4],
        small[2],
        small[3],
        conv2_sum.reshape(conv2_kernel.shape),
        small[10],
        small[5],
        small[6],
        linear_sum[0],
        small[7],
        linear_sum[1],
        linear_sum[2],
        small[8],
        linear_sum[3],
        small[9],
    )


def per_device(features, *rest):
    rows, imgs = lax.axis_size("rows"), lax.axis_size("imgs")
    if (rows, imgs) == (8, 4) and features.shape[1] == rows and features.shape[2] == ACROSS:
        return per_device_by_images(features, *rest)
    return per_device_by_rows(features, *rest)


def solution(mesh):
    placed = (
        P("rows", "imgs", None, None),
        P("rows", "imgs", None, None),
        P(),
        P(),
        P(),
        P(),
        P(),
        P(),
        P(),
        P(),
        P(),
        P(),
        P(),
        P(),
        P(),
        P(),
        P(),
        P(),
        P(),
    )
    return jax.shard_map(
        per_device,
        mesh=mesh,
        in_specs=placed,
        out_specs=(
            P("rows", "imgs", None, None),
            P("rows", "imgs", None, None),
            P(),
            P(),
            P(),
            P(),
            P(),
            P(),
            P(),
            P(),
            P(),
            P(),
            P(),
            P(),
            P(),
            P(),
            P(),
            P(),
            P(),
        ),
        check_vma=False,
    )
```

```python
import math

import jax
import jax.numpy as jnp
from jax import lax
from jax.experimental import pallas as pl
from jax.experimental.pallas import tpu as pltpu
from jax.sharding import PartitionSpec as P

GROUPS = 32
H = 32


EPSILON = 1e-06


def padded_2(block, sides, width):
    for axis, dim in sides:
        count = lax.axis_size(axis)
        forward = [(i, i + 1) for i in range(count - 1)]
        backward = [(target, source) for source, target in forward]
        low = lax.ppermute(
            lax.slice_in_dim(block, block.shape[dim] - width, None, axis=dim), axis, forward
        )
        high = lax.ppermute(lax.slice_in_dim(block, 0, width, axis=dim), axis, backward)
        block = jnp.concatenate([low, block, high], axis=dim)
    return block


def sigmoid_pair(tensor):
    logistic = jax.nn.sigmoid(tensor)
    return (tensor * logistic, logistic * (1.0 + tensor * (1.0 - logistic)))


def group_view(tensor):
    height, images, across, channels = tensor.shape
    return tensor.reshape(height, images, across, GROUPS, channels // GROUPS)


def spread_back(statistic):
    return statistic[None, :, None, :, None]


def norm_forward(tensor, norm_gain, norm_offset):
    grouped = group_view(tensor)
    members = H * tensor.shape[2] * (tensor.shape[3] // GROUPS)
    centre = lax.psum(jnp.sum(grouped, axis=(0, 2, 4)), "rows") / members
    centered = grouped - spread_back(centre)
    spread = lax.psum(jnp.sum(jnp.square(centered), axis=(0, 2, 4)), "rows") / members
    factor = lax.rsqrt(spread + EPSILON)
    normed = (centered * spread_back(factor)).reshape(tensor.shape)
    return (normed * norm_gain + norm_offset, normed, factor)


def norm_backward(gradient, normed, factor, norm_gain):
    gain_grad = jnp.sum(gradient * normed, axis=(0, 1, 2))
    offset_grad = jnp.sum(gradient, axis=(0, 1, 2))
    scaled = group_view(gradient * norm_gain)
    flat_normed = group_view(normed)
    members = H * gradient.shape[2] * (gradient.shape[3] // GROUPS)
    mean_grad, cross_grad = lax.psum(
        (jnp.sum(scaled, axis=(0, 2, 4)), jnp.sum(scaled * flat_normed, axis=(0, 2, 4))), "rows"
    )
    input_grad = (
        scaled - spread_back(mean_grad / members) - flat_normed * spread_back(cross_grad / members)
    ) * spread_back(factor)
    return (input_grad.reshape(gradient.shape), gain_grad, offset_grad)


def widen(tensor):
    return jnp.pad(tensor, ((0, 0), (0, 0), (1, 1), (0, 0)))


def conv_forward(tensor, kernel, offset):
    height, across = (tensor.shape[0], tensor.shape[2])
    padded = widen(padded_2(tensor, (("rows", 0),), 1))
    summed = jnp.zeros(tensor.shape[:3] + (kernel.shape[3],), jnp.float32)
    for row_off in range(3):
        for col_off in range(3):
            window = padded[row_off : row_off + height, :, col_off : col_off + across, :]
            summed = summed + jnp.einsum(
                "rbwc,cd->rbwd",
                window,
                kernel[row_off, col_off],
                preferred_element_type=jnp.float32,
            )
    return (summed + offset, padded)


def conv_backward(gradient, padded, kernel):
    height, across = (gradient.shape[0], gradient.shape[2])
    beside_all = widen(padded_2(gradient, (("rows", 0),), 1))
    input_grad = jnp.zeros(gradient.shape[:3] + (kernel.shape[2],), jnp.float32)
    tap_grads = []
    for row_off in range(3):
        for col_off in range(3):
            window = beside_all[
                2 - row_off : 2 - row_off + height, :, 2 - col_off : 2 - col_off + across, :
            ]
            input_grad = input_grad + jnp.einsum(
                "rbwd,cd->rbwc",
                window,
                kernel[row_off, col_off],
                preferred_element_type=jnp.float32,
            )
            source = padded[row_off : row_off + height, :, col_off : col_off + across, :]
            tap_grads.append(
                jnp.einsum("rbwc,rbwd->cd", source, gradient, preferred_element_type=jnp.float32)
            )
    kernel_grad = jnp.stack(tap_grads).reshape(kernel.shape)
    offset_grad = jnp.sum(gradient.astype(jnp.float32), axis=(0, 1, 2))
    return (input_grad, kernel_grad, offset_grad)


def linear(tensor, weight):
    return jnp.einsum("rbwc,cd->rbwd", tensor, weight, preferred_element_type=jnp.float32)


def back_linear(gradient, weight):
    return jnp.einsum("rbwd,cd->rbwc", gradient, weight, preferred_element_type=jnp.float32)


def weight_product(tensor, gradient):
    return jnp.einsum("rbwc,rbwd->cd", tensor, gradient, preferred_element_type=jnp.float32)


def image_to_sequence(tensor):
    height, images, across, channels = tensor.shape
    return tensor.transpose(1, 0, 2, 3).reshape(images, height * across, channels)


def from_sequence(sequence, height, across):
    images, length, channels = sequence.shape
    return sequence.reshape(images, height, across, channels).transpose(1, 0, 2, 3)


def reduce_all(gradients):
    flattened = jnp.concatenate([gradient.reshape(-1) for gradient in gradients])
    length = flattened.shape[0]
    devices = lax.axis_size("rows") * lax.axis_size("imgs")
    per_share = -(-length // (devices * 128)) * 128
    padded_len = per_share * devices
    strided = jnp.pad(flattened, (0, padded_len - length)).reshape(per_share, devices).T
    packed = strided.reshape(padded_len // 128, 128)
    my_share = lax.psum_scatter(packed, ("rows", "imgs"), scatter_dimension=0, tiled=True)
    summed_all = lax.all_gather(
        my_share.astype(jnp.bfloat16), ("rows", "imgs"), axis=0, tiled=True
    ).astype(my_share.dtype)
    summed_all = summed_all.reshape(devices, per_share).T.reshape(-1)
    results = []
    offset_at = 0
    for gradient in gradients:
        results.append(summed_all[offset_at : offset_at + gradient.size].reshape(gradient.shape))
        offset_at = offset_at + gradient.size
    return results


def per_device_by_rows(
    features,
    cotangent,
    norm1_gain,
    norm1_shift,
    conv1_kernel,
    conv1_shift,
    norm2_gain,
    norm2_shift,
    conv2_kernel,
    conv2_shift,
    norm3_gain,
    norm3_shift,
    query_weight,
    query_shift,
    key_weight,
    value_weight,
    value_shift,
    out_weight,
    out_shift,
):
    height, images, across, channels = features.shape
    attention_score_scale = 1.0 / math.sqrt(channels)
    inputs = features.astype(jnp.float32)
    norm_one, normed_one, factor_one = norm_forward(inputs, norm1_gain, norm1_shift)
    act_one, slope_one = sigmoid_pair(norm_one)
    conv_one, padded_one = conv_forward(act_one.astype(jnp.bfloat16), conv1_kernel, conv1_shift)
    norm_two, normed_two, factor_two = norm_forward(conv_one, norm2_gain, norm2_shift)
    act_two, slope_two = sigmoid_pair(norm_two)
    conv_two, padded_two = conv_forward(act_two.astype(jnp.bfloat16), conv2_kernel, conv2_shift)
    residual = inputs + conv_two
    norm_three, normed_three, factor_three = norm_forward(residual, norm3_gain, norm3_shift)
    attend_input = norm_three.astype(jnp.bfloat16)
    query_rows = (linear(attend_input, query_weight) + query_shift).astype(jnp.bfloat16)
    key_state_rows = linear(attend_input, key_weight).astype(jnp.bfloat16)
    value_state_rows = (linear(attend_input, value_weight) + value_shift).astype(jnp.bfloat16)
    all_keys, all_values = (
        lax.all_gather(key_state_rows, "rows", axis=0, tiled=True),
        lax.all_gather(value_state_rows, "rows", axis=0, tiled=True),
    )
    query_sequence = image_to_sequence(query_rows)
    key_sequence = image_to_sequence(all_keys)
    value_sequence = image_to_sequence(all_values)
    attention_scores = (
        jnp.einsum("xao,xno->xan", query_sequence, key_sequence, preferred_element_type=jnp.float32)
        * attention_score_scale
    )
    row_peak = jnp.max(attention_scores, axis=-1, keepdims=True)
    log_total = row_peak + jnp.log(
        jnp.sum(jnp.exp(attention_scores - row_peak), axis=-1, keepdims=True)
    )
    weight_tensors = jnp.exp(attention_scores - log_total).astype(jnp.bfloat16)
    attended_seq = jnp.einsum(
        "afj,ajy->afy", weight_tensors, value_sequence, preferred_element_type=jnp.float32
    )
    attention_output = from_sequence(attended_seq.astype(jnp.bfloat16), height, across)
    output = residual + linear(attention_output, out_weight) + out_shift
    out_shift_grad = jnp.sum(cotangent.astype(jnp.float32), axis=(0, 1, 2))
    out_weight_grad = weight_product(attention_output, cotangent)
    mixed_grad = back_linear(cotangent, out_weight).astype(jnp.bfloat16)
    mixed_sequence = image_to_sequence(mixed_grad)
    scores_again = (
        jnp.einsum("xao,xno->xan", query_sequence, key_sequence, preferred_element_type=jnp.float32)
        * attention_score_scale
    )
    probabilities = jnp.exp(scores_again - log_total)
    probability_gradient = jnp.einsum(
        "xao,xno->xan", mixed_sequence, value_sequence, preferred_element_type=jnp.float32
    )
    delta = jnp.sum(probabilities * probability_gradient, axis=-1, keepdims=True)
    score_gradient = (probabilities * (probability_gradient - delta)).astype(jnp.bfloat16)
    query_local = (
        jnp.einsum("afj,ajy->afy", score_gradient, key_sequence, preferred_element_type=jnp.float32)
        * attention_score_scale
    )
    query_grad = from_sequence(query_local, height, across).astype(jnp.bfloat16)
    key_full = (
        jnp.einsum(
            "svt,svz->stz", score_gradient, query_sequence, preferred_element_type=jnp.float32
        )
        * attention_score_scale
    )
    value_full = jnp.einsum(
        "svt,svz->stz",
        probabilities.astype(jnp.bfloat16),
        mixed_sequence,
        preferred_element_type=jnp.float32,
    )
    stacked = from_sequence(jnp.concatenate([key_full, value_full], axis=-1), H, across)
    own_grads = lax.psum_scatter(
        stacked.astype(jnp.bfloat16), "rows", scatter_dimension=0, tiled=True
    ).astype(jnp.float32)
    key_grad = own_grads[..., :channels].astype(jnp.bfloat16)
    value_grad = own_grads[..., channels:].astype(jnp.bfloat16)
    query_weight_grad = weight_product(attend_input, query_grad)
    query_shift_grad = jnp.sum(query_grad.astype(jnp.float32), axis=(0, 1, 2))
    key_weight_grad = weight_product(attend_input, key_grad)
    value_weight_grad = weight_product(attend_input, value_grad)
    value_shift_grad = jnp.sum(value_grad.astype(jnp.float32), axis=(0, 1, 2))
    attend_grad = (
        back_linear(query_grad, query_weight)
        + back_linear(key_grad, key_weight)
        + back_linear(value_grad, value_weight)
    )
    resid_part, norm3_gain_grad, norm3_shift_grad = norm_backward(
        attend_grad, normed_three, factor_three, norm3_gain
    )
    resid_grad = cotangent.astype(jnp.float32) + resid_part
    conv_two_in, conv2_kernel_grad, conv2_shift_grad = conv_backward(
        resid_grad.astype(jnp.bfloat16), padded_two, conv2_kernel
    )
    conv_one_out, norm2_gain_grad, norm2_shift_grad = norm_backward(
        conv_two_in * slope_two, normed_two, factor_two, norm2_gain
    )
    conv_one_in, conv1_kernel_grad, conv1_shift_grad = conv_backward(
        conv_one_out.astype(jnp.bfloat16), padded_one, conv1_kernel
    )
    inputs_part, norm1_gain_grad, norm1_shift_grad = norm_backward(
        conv_one_in * slope_one, normed_one, factor_one, norm1_gain
    )
    features_grad = resid_grad + inputs_part
    reduced = reduce_all(
        [
            norm1_gain_grad,
            norm1_shift_grad,
            conv1_kernel_grad,
            conv1_shift_grad,
            norm2_gain_grad,
            norm2_shift_grad,
            conv2_kernel_grad,
            conv2_shift_grad,
            norm3_gain_grad,
            norm3_shift_grad,
            query_weight_grad,
            query_shift_grad,
            key_weight_grad,
            value_weight_grad,
            value_shift_grad,
            out_weight_grad,
            out_shift_grad,
        ]
    )
    return (output, features_grad) + tuple(reduced)


F32 = jnp.float32
BF16 = jnp.bfloat16
AXES = ("rows", "imgs")
MEGA = 1024 * 1024
TILE = 64
MM_TILE = 256
ACROSS = 32
UNROLLED = 4
FLOPS = 3 * 10**10
BYTES = 1
BRIEF = 10**7
FORWARD_LIMIT = 18
ATTEND_LIMIT = 22
SECOND_GROUPS = (((0, 1, 2), False, "XYNF"),)
FIRST_GROUPS = (((0, 1, 2), False, "XYNF"),)
LINEAR_ORDER = "XYNF"
ORDER_SLOTS = {"X": 2, "Y": 3, "N": 4, "F": 5}
RIDE = "C0"
TAIL = 32
SMALL = 16
PLAN = (
    "W2 O! D2 O", "B0 W1 B0 D1", "B0 C0 B0 L0", "C0 B0 C0 B0",
    "L0 C0 B0 C0", "L0 G L0 C0", "B0 L0 O C0", "B0 L0 G L0",
    "O C0 C0< L0", "G C0> L0",
)
STEPS = ("core", "plane_a", "plane_b", "near", "far")
VMEM = pl.BlockSpec(memory_space=pltpu.VMEM)
SMEM = pl.BlockSpec(memory_space=pltpu.SMEM)
HBM = pl.BlockSpec(memory_space=pltpu.HBM)


def shape_of(shape, dtype):
    return jax.ShapeDtypeStruct(shape, dtype)


def kernel_call(
    body, out_shape, in_specs, scratch=(), limit=24, moved=0, flops=FLOPS
):
    return pl.pallas_call(
        body,
        out_shape=out_shape,
        in_specs=in_specs,
        out_specs=jax.tree.map(lambda _: VMEM, out_shape),
        scratch_shapes=list(scratch),
        compiler_params=pltpu.CompilerParams(vmem_limit_bytes=limit * MEGA),
        cost_estimate=pl.CostEstimate(
            flops=flops, bytes_accessed=BYTES * moved, transcendentals=0
        ),
    )


def tiles(total, size, body):
    if total // size <= UNROLLED:
        for index in range(total // size):
            body(index * size)
        return

    def step(index, carry):
        body(pl.multiple_of(index * size, size))
        return carry

    lax.fori_loop(0, total // size, step, 0)


def fold_tiles(total, size, body, carry):
    if total // size <= UNROLLED:
        for index in range(total // size):
            carry = body(index * size, carry)
        return carry

    def step(index, held):
        return body(pl.multiple_of(index * size, size), held)

    return lax.fori_loop(0, total // size, step, carry)


def fold_rows(tensor):
    return jnp.sum(tensor.reshape(tensor.shape[0] // 8, 8, tensor.shape[1]), axis=0)


def column(partial):
    return jnp.sum(partial, axis=0, keepdims=True)


def group_means(same_ref, columns, members):
    channels = columns[0].shape[1]
    place = lax.broadcasted_iota(jnp.int32, (8, channels), 0)
    rows = jnp.zeros((8, channels), F32)
    for number, values in enumerate(columns):
        left = values
        for term in range(3):
            part = left.astype(BF16).astype(F32)
            left = left - part
            rows = jnp.where(place == 3 * number + term, part, rows)
    summed = dot(rows.astype(BF16), same_ref[...])
    return [
        (summed[3 * n : 3 * n + 1] + summed[3 * n + 1 : 3 * n + 2] + summed[3 * n + 2 : 3 * n + 3])
        * (1.0 / members)
        for n in range(len(columns))
    ]


def pivot_sums(values, pivot):
    moved = values - pivot
    return fold_rows(moved), fold_rows(moved * moved)


def norm_stats(same_ref, sums, squares, pivot, total):
    channels = pivot.shape[1]
    size = channels // GROUPS
    sums, squares = column(sums), column(squares)
    (centre,) = group_means(same_ref, [sums + total * pivot], total * size)
    offset = pivot - centre
    (spread,) = group_means(
        same_ref, [squares + offset * (2.0 * sums + total * offset)], total * size
    )
    return centre, lax.rsqrt(spread + EPSILON)


def fill_shifted(cat_ref, at, tile):
    size, channels = tile.shape
    place = lax.broadcasted_iota(jnp.int32, tile.shape, 0) % ACROSS
    before = jnp.where(place == 0, 0.0, pltpu.roll(tile, 1, 0))
    after = jnp.where(place == ACROSS - 1, 0.0, pltpu.roll(tile, size - 1, 0))
    rows = pl.ds(pl.multiple_of(ACROSS + at, ACROSS), size)
    cat_ref[rows, 0:channels] = before.astype(BF16)
    cat_ref[rows, channels : 2 * channels] = tile.astype(BF16)
    cat_ref[rows, 2 * channels : 3 * channels] = after.astype(BF16)


def clear_border(cat_ref):
    total, width = cat_ref.shape
    cat_ref[0:ACROSS, :] = jnp.zeros((ACROSS, width), BF16)
    cat_ref[total - ACROSS : total, :] = jnp.zeros((ACROSS, width), BF16)


def at_rows(at):
    return at if isinstance(at, int) else pl.multiple_of(at, ACROSS)


def window_product(cat_ref, weight_ref, at, size):
    total = None
    for row_off in range(3):
        rows = pl.ds(at_rows(at + row_off * ACROSS), size)
        part = jnp.dot(cat_ref[rows, :], weight_ref[row_off], preferred_element_type=F32)
        total = part if total is None else total + part
    return total


def window_product_turned(cat_ref, weight_ref, at, size):
    channels = weight_ref.shape[2]
    total = None
    for row_off in range(3):
        rows = pl.ds(at_rows(at + (2 - row_off) * ACROSS), size)
        for col_off in range(3):
            low = (2 - col_off) * channels
            tap = weight_ref[row_off, col_off * channels : (col_off + 1) * channels, :]
            part = dot_t(cat_ref[rows, low : low + channels], tap)
            total = part if total is None else total + part
    return total


def dot_t(left, right):
    return lax.dot_general(left, right, (((1,), (1,)), ((), ())), preferred_element_type=F32)


def t_dot(left, right):
    return lax.dot_general(left, right, (((0,), (0,)), ((), ())), preferred_element_type=F32)


def dot(left, right):
    return jnp.dot(left, right, preferred_element_type=F32)


def line(lines_ref, row):
    return lines_ref[row : row + 1, :]


def forward_body(place_ref, *refs):
    pairs = refs[:4]
    (lines_ref, same_ref, weight1_ref, weight2_ref, q_weight_ref, k_weight_ref, v_weight_ref,
     image_ref, act1_ref, conv_ref, act2_ref, resid_ref, stats_ref, norm_ref, q_ref, k_ref, v_ref,
     cat_ref, pivot_ref) = refs[4:]
    total, channels = image_ref.shape
    share = total // 8
    me = place_ref[0]
    for index in range(8):
        at = pl.multiple_of((me ^ index) * share, share)
        image_ref[pl.ds(at, share), :] = pairs[index // 2][index % 2]
    clear_border(cat_ref)
    zero = jnp.zeros((8, channels), F32)

    def activate_all(read, stats, stats_row, gain_row, act_ref):
        centre, factor = stats
        stats_ref[stats_row : stats_row + 1, :] = centre
        stats_ref[stats_row + 1 : stats_row + 2, :] = factor
        scale = factor * line(lines_ref, gain_row)
        shift = line(lines_ref, gain_row + 1) - centre * scale

        def activate(at):
            held = read(at) * scale + shift
            act = held * jax.nn.sigmoid(held)
            act_ref[pl.ds(at, TILE), :] = act.astype(BF16)
            fill_shifted(cat_ref, at, act)

        tiles(total, TILE, activate)

    def read_image(at):
        return image_ref[pl.ds(at, TILE), :].astype(F32)

    pivot1 = read_image(0)[0:1, :]

    def sum_image(at, held):
        sums, squares = pivot_sums(read_image(at), pivot1)
        return held[0] + sums, held[1] + squares

    sums, squares = fold_tiles(total, TILE, sum_image, (zero, zero))
    stats1 = norm_stats(same_ref, sums, squares, pivot1, total)
    activate_all(read_image, stats1, 0, 0, act1_ref)

    def convolve_all(weight_ref, bias, more, target_ref):
        def convolve(at, held):
            rows = pl.ds(at, MM_TILE)
            values = window_product(cat_ref, weight_ref, at, MM_TILE) + bias
            if more is not None:
                values = values + more[rows, :].astype(F32)

            if isinstance(at, int):
                if at == 0:
                    pivot_ref[0:1, :] = values[0:1, :]
            else:

                @pl.when(at == 0)
                def _():
                    pivot_ref[0:1, :] = values[0:1, :]

            target_ref[rows, :] = values
            sums, squares = pivot_sums(values, pivot_ref[0:1, :])
            return held[0] + sums, held[1] + squares

        sums, squares = fold_tiles(total, MM_TILE, convolve, (zero, zero))
        return norm_stats(same_ref, sums, squares, pivot_ref[0:1, :], total)

    stats2 = convolve_all(weight1_ref, line(lines_ref, 6), None, conv_ref)
    activate_all(lambda at: conv_ref[pl.ds(at, TILE), :], stats2, 2, 2, act2_ref)
    centre3, factor3 = convolve_all(weight2_ref, line(lines_ref, 7), image_ref, resid_ref)
    stats_ref[4:5, :] = centre3
    stats_ref[5:6, :] = factor3
    stats_ref[6:8, :] = jnp.zeros((2, channels), F32)
    scale3 = factor3 * line(lines_ref, 4)
    shift3 = line(lines_ref, 5) - centre3 * scale3
    q_shift, v_shift = line(lines_ref, 8), line(lines_ref, 9)

    def project(at):
        rows = pl.ds(at, MM_TILE)
        held = (resid_ref[rows, :] * scale3 + shift3).astype(BF16)
        norm_ref[rows, :] = held
        q_ref[rows, :] = (dot(held, q_weight_ref[...]) + q_shift).astype(BF16)
        k_ref[rows, :] = dot(held, k_weight_ref[...]).astype(BF16)
        v_ref[rows, :] = (dot(held, v_weight_ref[...]) + v_shift).astype(BF16)

    tiles(total, MM_TILE, project)


def lane_half(part, half):
    return pl.ds(pl.multiple_of(part * half, half), half)


def z_bits(core):
    return 2 << core, 4 >> core


def return_pieces(place_ref, out_ref, sent_ref, kept_ref):
    share = out_ref.shape[0] // 8
    me, core = place_ref[0], place_ref[1]
    for target, side in ((kept_ref, 0), (sent_ref, 1)):
        first, second = z_bits(core if side == 0 else 1 - core)
        for index in range(4):
            offset = side + (index // 2) * first + (index % 2) * second
            at = pl.multiple_of((me ^ offset) * share, share)
            target[index] = out_ref[pl.ds(at, share), :]


def attention_body(place_ref, *refs):
    cot_pieces = refs[:4]
    (q_ref, k_ref, v_ref, norm_ref, resid_ref, stats_ref, lines_ref, same_ref,
     o_weight_ref, q_weight_ref, k_weight_ref, v_weight_ref) = refs[4:16]
    (out_sent_ref, out_kept_ref, sent_ref, kept_ref, small_ref, d_resid_ref, d_conv_ref, d_sent_ref,
     cot_ref, out_ref, mixed_ref, d_mixed_ref, d_q_ref, d_k_ref, d_v_ref,
     weights_ref, d_scores_ref) = refs[16:]
    total, channels = q_ref.shape
    share = total // 8
    scale = 1.0 / math.sqrt(channels)
    me = place_ref[0]
    for index in range(8):
        at = pl.multiple_of((me ^ index) * share, share)
        cot_ref[pl.ds(at, share), :] = cot_pieces[index // 2][index % 2]
    o_shift = line(lines_ref, 10)
    zero = jnp.zeros((8, channels), F32)

    def attend(at, held):
        rows = pl.ds(at, MM_TILE)
        query = q_ref[rows, :]
        cot = cot_ref[rows, :]
        scores = dot_t(query, k_ref[...]) * scale
        d_mixed = dot_t(cot, o_weight_ref[...]).astype(BF16)
        d_mixed_ref[rows, :] = d_mixed
        d_prob = dot_t(d_mixed, v_ref[...])
        exps = jnp.exp(scores - jnp.max(scores, axis=-1, keepdims=True))
        probs = exps * (1.0 / jnp.sum(exps, axis=-1, keepdims=True))
        weights = probs.astype(BF16)
        weights_ref[rows, :] = weights
        mixed = dot(weights, v_ref[...]).astype(BF16)
        mixed_ref[rows, :] = mixed
        out_ref[rows, :] = (
            resid_ref[rows, :] + dot(mixed, o_weight_ref[...]) + o_shift
        ).astype(BF16)
        delta = jnp.sum(probs * d_prob, axis=-1, keepdims=True)
        d_scores = (probs * (d_prob - delta)).astype(BF16)
        d_scores_ref[rows, :] = d_scores
        d_query = (dot(d_scores, k_ref[...]) * scale).astype(BF16)
        d_q_ref[rows, :] = d_query
        return held[0] + fold_rows(cot.astype(F32)), held[1] + fold_rows(d_query.astype(F32))

    cot_sums, d_q_sums = fold_tiles(total, MM_TILE, attend, (zero, zero))
    return_pieces(place_ref, out_ref, out_sent_ref, out_kept_ref)

    def to_keys(at, held):
        rows = pl.ds(at, MM_TILE)
        d_k_ref[rows, :] = (t_dot(d_scores_ref[:, rows], q_ref[...]) * scale).astype(BF16)
        d_value = t_dot(weights_ref[:, rows], d_mixed_ref[...]).astype(BF16)
        d_v_ref[rows, :] = d_value
        return held + fold_rows(d_value.astype(F32))

    d_v_sums = fold_tiles(total, MM_TILE, to_keys, zero)
    half = channels // 2
    core = place_ref[1]
    for index, (left, right) in enumerate(
        ((norm_ref, d_q_ref), (norm_ref, d_k_ref), (norm_ref, d_v_ref), (mixed_ref, cot_ref))
    ):
        for target, part in ((sent_ref, 1 - core), (kept_ref, core)):
            target[index] = t_dot(left[...], right[:, lane_half(part, half)]).astype(BF16)

    centre, factor = stats_ref[4:5, :], stats_ref[5:6, :]
    gain = line(lines_ref, 4)

    def back(at, held):
        rows = pl.ds(at, MM_TILE)
        grad = (
            dot_t(d_q_ref[rows, :], q_weight_ref[...])
            + dot_t(d_k_ref[rows, :], k_weight_ref[...])
            + dot_t(d_v_ref[rows, :], v_weight_ref[...])
        )
        d_resid_ref[rows, :] = grad
        normed = (resid_ref[rows, :] - centre) * factor
        return held[0] + fold_rows(grad), held[1] + fold_rows(grad * normed)

    sums = fold_tiles(total, MM_TILE, back, (zero, zero))
    shift_grad, gain_grad, o_shift_grad, q_shift_grad, v_shift_grad = [
        column(part) for part in (*sums, cot_sums, d_q_sums, d_v_sums)
    ]
    members = total * (channels // GROUPS)
    mean_grad, cross_grad = group_means(same_ref, [shift_grad * gain, gain_grad * gain], members)

    def finish(at, held):
        rows = pl.ds(at, TILE)
        normed = (resid_ref[rows, :] - centre) * factor
        grad = cot_ref[rows, :].astype(F32) + factor * (
            d_resid_ref[rows, :] * gain - mean_grad - normed * cross_grad
        )
        d_resid_ref[rows, :] = grad
        rounded = grad.astype(BF16)
        d_conv_ref[rows, :] = rounded
        d_sent_ref[rows, :] = d_conv_ref[rows, lane_half(1 - core, half)]
        return held + fold_rows(rounded.astype(F32))

    conv_shift_grad = column(fold_tiles(total, TILE, finish, zero))
    small_ref[0:1, :] = gain_grad
    small_ref[1:2, :] = shift_grad
    small_ref[2:3, :] = q_shift_grad
    small_ref[3:4, :] = v_shift_grad
    small_ref[4:5, :] = o_shift_grad
    small_ref[5:6, :] = conv_shift_grad
    small_ref[6:8, :] = jnp.zeros((2, channels), F32)


def kernel_grad_body(groups, place_ref, act_ref, act_got_ref, grad_ref, grad_got_ref, *refs):
    linear = any(carries for _, carries, _ in groups)
    more, refs = (refs[:2], refs[2:]) if linear else ((), refs)
    parts, (cat_ref, cat_got_ref, turned_ref, turned_got_ref) = refs[: 2 * len(groups)], refs[2 * len(groups) :]
    total, channels = act_ref.shape
    half = channels // 2
    core = place_ref[1]
    clear_border(cat_ref)
    clear_border(cat_got_ref)

    def fill(at):
        rows = pl.ds(at, TILE)
        fill_shifted(cat_ref, at, grad_ref[rows, lane_half(core, half)].astype(F32))
        fill_shifted(cat_got_ref, at, grad_got_ref[rows, :].astype(F32))

    tiles(total, TILE, fill)
    turned_ref[...] = act_ref[...].T
    turned_got_ref[...] = act_got_ref[...].T
    for number, (kernel_rows, carries, order) in enumerate(groups):
        bit = place_ref[ORDER_SLOTS[order[0]]]
        for target, part in ((parts[2 * number], 1 - bit), (parts[2 * number + 1], bit)):
            rows = pl.ds(pl.multiple_of(part * half, half), half)
            for index, row_off in enumerate(kernel_rows):
                span = pl.ds((2 - row_off) * ACROSS, total)
                product = (
                    dot(turned_ref[rows, :], cat_ref[span, :])
                    + dot(turned_got_ref[rows, :], cat_got_ref[span, :])
                ).astype(BF16)
                for col_off in range(3):
                    at = (3 * index + col_off) * half
                    low = (2 - col_off) * half
                    target[at : at + half, :] = product[:, low : low + half]
            if carries:
                for index in range(4):
                    at = (3 * len(kernel_rows) + index) * half
                    target[at : at + half, :] = (
                        more[0][index, rows, :].astype(F32) + more[1][index, rows, :].astype(F32)
                    ).astype(BF16)


def linear_halves(slot, place_ref, kept_ref, got_ref, sent_out, kept_out):
    bit = place_ref[slot]
    count, rows, half = kept_ref.shape
    rows //= 2
    for target, part in ((sent_out, 1 - bit), (kept_out, bit)):
        span = pl.ds(pl.multiple_of(part * rows, rows), rows)
        for index in range(count):
            target[index * rows : (index + 1) * rows, :] = (
                kept_ref[index, span, :].astype(F32) + got_ref[index, span, :].astype(F32)
            ).astype(BF16)


def input_grad_body(with_rest, stats_row, place_ref, *refs):
    grad_ref, weight_ref, source_ref, stats_ref, lines_ref, same_ref = refs[:6]
    if with_rest:
        rest_ref, small_two_ref, small_three_ref = refs[6:9]
    else:
        linear_kept_ref, linear_got_ref = refs[6:8]
    refs = refs[9:] if with_rest else refs[8:]
    if with_rest:
        sent_ref, kept_ref, small_ref, cat_ref, held_ref, out_ref, rows_ref = refs
    else:
        out_ref, d_sent_ref, small_ref, linear_sent_out, linear_kept_out, cat_ref, held_ref = refs
    core = place_ref[1]
    total, channels = grad_ref.shape
    centre = stats_ref[stats_row : stats_row + 1, :]
    factor = stats_ref[stats_row + 1 : stats_row + 2, :]
    gain, shift = line(lines_ref, stats_row), line(lines_ref, stats_row + 1)
    clear_border(cat_ref)

    def fill(at):
        fill_shifted(cat_ref, at, grad_ref[pl.ds(at, TILE), :].astype(F32))

    tiles(total, TILE, fill)

    zero = jnp.zeros((8, channels), F32)

    def product(at, held):
        rows = pl.ds(at, MM_TILE)
        normed = (source_ref[rows, :].astype(F32) - centre) * factor
        pre = normed * gain + shift
        logistic = jax.nn.sigmoid(pre)
        slope = logistic * (1.0 + pre * (1.0 - logistic))
        grad = window_product_turned(cat_ref, weight_ref, at, MM_TILE) * slope
        held_ref[rows, :] = grad
        return held[0] + fold_rows(grad), held[1] + fold_rows(grad * normed)

    shift_sum, gain_sum = fold_tiles(total, MM_TILE, product, (zero, zero))
    shift_grad, gain_grad = column(shift_sum), column(gain_sum)
    members = total * (channels // GROUPS)
    mean_grad, cross_grad = group_means(same_ref, [shift_grad * gain, gain_grad * gain], members)

    def finish(at, held):
        rows = pl.ds(at, TILE)
        normed = (source_ref[rows, :].astype(F32) - centre) * factor
        grad = factor * (held_ref[rows, :] * gain - mean_grad - normed * cross_grad)
        if with_rest:
            grad = grad + rest_ref[rows, :]
        rounded = grad.astype(BF16)
        out_ref[rows, :] = rounded
        if not with_rest:
            d_sent_ref[rows, :] = out_ref[rows, lane_half(1 - core, channels // 2)]
        return held + fold_rows(rounded.astype(F32))

    out_sum = column(fold_tiles(total, TILE, finish, zero))
    if not with_rest:
        linear_halves(
            ORDER_SLOTS[LINEAR_ORDER[0]], place_ref, linear_kept_ref, linear_got_ref, linear_sent_out,
            linear_kept_out,
        )
        small_ref[0:1, :] = gain_grad
        small_ref[1:2, :] = shift_grad
        small_ref[2:3, :] = out_sum
        small_ref[3:8, :] = jnp.zeros((5, channels), F32)
        return
    return_pieces(place_ref, out_ref, sent_ref, kept_ref)
    rows_ref[0:1, :] = gain_grad
    rows_ref[1:2, :] = shift_grad
    rows_ref[2:5, :] = small_two_ref[0:3, :]
    rows_ref[5:11, :] = small_three_ref[0:6, :]
    rows_ref[11:SMALL, :] = jnp.zeros((SMALL - 11, channels), F32)
    half = channels // 2
    small_ref[0:SMALL, :] = rows_ref[:, 0:half].astype(BF16)
    small_ref[SMALL:TAIL, :] = rows_ref[:, half:channels].astype(BF16)


def pack_by_core_body(place_ref, block_ref, sent_ref, kept_ref):
    me = place_ref[0]
    for target, side in ((kept_ref, 0), (sent_ref, 1)):
        for index in range(4):
            for row in range(block_ref.shape[0]):
                rows = pl.ds(row * ACROSS, ACROSS)
                target[index, rows, :] = block_ref[row, me ^ (2 * index + side)]


def pair_body(place_ref, kept_ref, got_ref, *refs):
    count = (len(refs) - 5) // 2
    staged, pair_refs, sems = refs[:count], refs[count : count + 4], refs[-1]
    targets = refs[count + 4 : 2 * count + 4]
    copies = [
        pltpu.make_async_copy(staged[index], targets[index], sems.at[index])
        for index in range(count)
    ]
    for copy in copies:
        copy.start()
    for index in range(4):
        pair_refs[index][0] = kept_ref[index]
        pair_refs[index][1] = got_ref[index]
    if count:
        same_ref = refs[2 * count + 4]
        one, two = (lax.broadcasted_iota(jnp.int32, same_ref.shape, dim) for dim in (0, 1))
        size = same_ref.shape[0] // GROUPS
        same_ref[...] = jnp.where(one // size == two // size, 1.0, 0.0).astype(BF16)
    for copy in copies:
        copy.wait()


def pack_by_core(place, block):
    rows, _, across, channels = block.shape
    four = shape_of((4, rows * across, channels), BF16)
    return kernel_call(
        pack_by_core_body, [four] * 2, [SMEM, VMEM], limit=8, moved=2 * MEGA
    )(place, block)


def pair_up(place, kept, got, staged=()):
    channels = kept.shape[2]
    pair = shape_of((2,) + kept.shape[1:], BF16)
    results = kernel_call(
        pair_body,
        [pair] * 4
        + [shape_of(array.shape, array.dtype) for array in staged]
        + [shape_of((channels, channels), BF16)] * bool(staged),
        [SMEM, VMEM, VMEM] + [HBM] * len(staged),
        [pltpu.SemaphoreType.DMA((max(len(staged), 1),))],
        limit=16 if staged else 8,
        moved=2 * MEGA,
        flops=BRIEF if staged else FLOPS,
    )(place, kept, got, *staged)
    return results[:4], results[4:]


def swap_pieces(pieces, unit):
    count = len(pieces)
    return [pieces[0]] + [
        lax.ppermute(pieces[k], "rows", [(r, r ^ (unit * k)) for r in range(count * unit)])
        for k in range(1, count)
    ]


def partner_table(kind):
    table = []
    for row in range(8):
        for img in range(4):
            core = row & 1
            if kind == "core":
                other = (row ^ 1, img)
            elif kind == "near":
                other = (row ^ (4 if core else 2), img)
            elif kind == "far":
                other = (row ^ (2 if core else 4), img)
            elif kind == "plane_a":
                other = (row, img ^ (2 if core else 1))
            else:
                other = (row, img ^ (1 if core else 2))
            table.append((row * 4 + img, other[0] * 4 + other[1]))
    return table


def exchange(tensor, kind):
    return lax.ppermute(tensor, AXES, partner_table(kind))


def own_place():
    row, img = lax.axis_index("rows"), lax.axis_index("imgs")
    core, near, far = row & 1, (row >> 1) & 1, (row >> 2) & 1
    low, high = img & 1, (img >> 1) & 1
    plane_a = jnp.where(core == 1, high, low)
    plane_b = jnp.where(core == 1, low, high)
    first_z = jnp.where(core == 1, far, near)
    second_z = jnp.where(core == 1, near, far)
    return jnp.stack([row, core, plane_a, plane_b, first_z, second_z, row, row]).astype(jnp.int32)


def add_tails(target, target_at, kept_ref, got_ref, at):
    target[target_at : target_at + TAIL, :] = (
        kept_ref[at : at + TAIL, :].astype(F32) + got_ref[at : at + TAIL, :].astype(F32)
    ).astype(BF16)


def add_split(chain, slot, place_ref, ins, outs):
    kept_ref, got_ref = ins[:2]
    count, rows = chain.count, chain.rows
    half = rows // 2
    bit = place_ref[slot]

    def one(index, carry):
        for target, part in zip(outs, (1 - bit, bit)):
            span = pl.ds(pl.multiple_of(index * rows + part * half, half), half)
            target[pl.ds(pl.multiple_of(index * half, half), half), :] = (
                kept_ref[span, :].astype(F32) + got_ref[span, :].astype(F32)
            ).astype(BF16)
        return carry

    lax.fori_loop(0, count, one, 0)
    if chain.small is not None:
        for target in outs:
            if len(ins) > 2:
                target[count * half : count * half + TAIL, :] = ins[2][...]
            else:
                add_tails(target, count * half, kept_ref, got_ref, count * rows)


def add_last(chain, slot, place_ref, ins, outs):
    outs[0][...] = (ins[0][...].astype(F32) + ins[1][...].astype(F32)).astype(BF16)


def join(chain, slot, place_ref, ins, outs):
    count, rows = chain.count, chain.rows
    bit = place_ref[slot]

    def one(index, carry):
        for source, part in zip(ins, (bit, 1 - bit)):
            span = pl.ds(pl.multiple_of((2 * index + part) * rows, rows), rows)
            outs[0][span, :] = source[pl.ds(pl.multiple_of(index * rows, rows), rows), :]
        return carry

    lax.fori_loop(0, count, one, 0)
    if chain.small is not None:
        at = count * rows
        if slot == chain.slots[0]:
            add_tails(outs[0], 2 * at, ins[0], ins[1], at)
        else:
            outs[0][2 * at : 2 * at + TAIL, :] = ins[0][at : at + TAIL, :]


def turn_pairs(chain, slot, place_ref, ins, outs):
    kept_ref, got_ref = ins
    for target, part in zip(outs, (1, 0)):
        for index in range(2):
            if slot == 0:
                target[index] = kept_ref[2 * part + index]
                target[2 + index] = got_ref[2 * part + index]
            else:
                target[index] = kept_ref[2 * index + part]
                target[2 + index] = got_ref[2 * index + part]


def spread(chain, slot, place_ref, ins, outs):
    me, core = place_ref[0], place_ref[1]
    first, second = z_bits(core)
    out_ref = outs[0]
    for source, side in zip(ins, (0, 1)):
        for index in range(4):
            image = me ^ ((index % 2) + (index // 2) * first + side * second)
            for row in range(out_ref.shape[0]):
                rows = pl.ds(row * ACROSS, ACROSS)
                out_ref[row, image] = source[index, rows, :].astype(F32)


def join_last(place, sources, targets, tail=None, with_tail=False):
    half = sources[0][0].shape[1]
    rows = 2 * half
    sides = [side for _, side in sources]
    count = sum(target[4] for target in targets)
    wholes = [target[0] for target in targets if target[0] is not None]
    tails = [] if tail is None else [tail]
    at_tail = sources[0][0].shape[0] - TAIL

    def body(place_ref, *refs):
        source_refs = refs[: len(sources)]
        refs = refs[len(sources) :]
        tail_refs, refs = refs[: len(tails)], refs[len(tails) + len(wholes) :]
        out_refs = refs[: len(targets)]
        held_ref, sems = refs[-2:]
        core = place_ref[1]
        copies = []
        for out_ref, (_, _, there, here, planes) in zip(out_refs, targets):
            for plane in range(planes):
                for number, side in enumerate(sides):
                    index = len(copies)
                    at = (here + plane) * rows
                    held_ref[index] = source_refs[number][at : at + rows, :].astype(F32)
                    part = 1 - core if side else core
                    copy = pltpu.make_async_copy(
                        held_ref.at[index],
                        out_ref.at[there + plane, :, lane_half(part, half)],
                        sems.at[index],
                    )
                    copy.start()
                    copies.append(copy)
        if with_tail:
            mine = source_refs[0][at_tail : at_tail + TAIL, :]
            if tails:
                total = mine.astype(F32) + tail_refs[0][...].astype(F32)
                refs[len(targets)][:, 0:half] = total[0:SMALL]
                refs[len(targets)][:, half : 2 * half] = total[SMALL:TAIL]
            else:
                refs[len(targets)][...] = mine
        for copy in copies:
            copy.wait()

    anywhere = pl.BlockSpec(memory_space=pl.ANY)
    aliases, taken = {}, 0
    for number, target in enumerate(targets):
        if target[0] is not None:
            aliases[1 + len(sources) + len(tails) + taken] = number
            taken += 1
    slots = count * len(sources)
    out_shape = [shape_of((target[1], rows, rows), F32) for target in targets]
    if with_tail:
        out_shape.append(
            shape_of((SMALL, 2 * half), F32) if tails else shape_of((TAIL, half), BF16)
        )
    return pl.pallas_call(
        body,
        out_shape=out_shape,
        in_specs=[SMEM] + [VMEM] * (len(sources) + len(tails)) + [anywhere] * len(wholes),
        out_specs=[anywhere] * len(targets) + [VMEM] * with_tail,
        input_output_aliases=aliases,
        scratch_shapes=[pltpu.VMEM((slots, rows, half), F32), pltpu.SemaphoreType.DMA((slots,))],
        compiler_params=pltpu.CompilerParams(vmem_limit_bytes=(slots // 2 + 6) * MEGA),
        cost_estimate=pl.CostEstimate(
            flops=FLOPS, bytes_accessed=BYTES * 6 * slots * rows * half, transcendentals=0
        ),
    )(place, *[array for array, _ in sources], *tails, *wholes)


def tie(values, earlier):
    return lax.optimization_barrier(tuple(values) + tuple(earlier))[: len(values)]


def after(values, token):
    tied = lax.optimization_barrier(tuple(values) + (token,))
    return tied[:-1]


class SumChain:
    def __init__(self, sent, kept, order):
        self.kept, self.at, self.small = kept, 0, None
        self.rows = kept.shape[1]
        self.count = kept.shape[0] // self.rows
        self.slots = [ORDER_SLOTS[letter] for letter in order]
        self.got = exchange(sent, STEPS[self.slots[0] - 1])

    def inputs(self):
        with_small = self.small is not None and self.at == 0
        return [self.kept, self.got] + ([self.small] if with_small else [])

    def todo(self):
        tail = 0 if self.small is None else TAIL
        lanes = self.kept.shape[1]
        at, size = self.at, self.count * self.rows
        if at < 3:
            return add_split, self.slots[at + 1], [shape_of((size // 2 + tail, lanes), BF16)] * 2
        if at == 3:
            return add_last, 0, [shape_of((size + tail, lanes), BF16)]
        return join, self.slots[7 - at], [shape_of((2 * size + tail, lanes), BF16)]

    def take(self, outs):
        at = self.at
        self.at += 1
        self.kept = outs[-1]
        if at < 3:
            self.rows //= 2
            slot = self.slots[at + 1]
        elif at == 3:
            slot = self.slots[3]
        else:
            self.rows *= 2
            slot = self.slots[6 - at] if at < 7 else 1
        self.got = exchange(outs[0], STEPS[slot - 1])


class ReturnChain:
    def __init__(self, sent, kept, block_shape):
        self.kept, self.at, self.block_shape = kept, 0, block_shape
        self.got = exchange(sent, "core")

    def inputs(self):
        return [self.kept, self.got]

    def todo(self):
        if self.at < 2:
            return turn_pairs, self.at, [shape_of(self.kept.shape, BF16)] * 2
        return spread, 0, [shape_of(self.block_shape, F32)]

    def take(self, outs):
        self.kept = outs[-1]
        if self.at < 2:
            self.got = exchange(outs[0], ("near", "far")[self.at])
        self.at += 1


def step(place, chain, token):
    work, slot, shapes = chain.todo()
    arrays = after(chain.inputs(), token)

    def body(place_ref, *refs):
        work(chain, slot, place_ref, refs[: len(arrays)], refs[len(arrays) :])

    moved = 2 * sum(a.size * a.dtype.itemsize for a in arrays)
    results = kernel_call(
        body, shapes, [SMEM] + [VMEM] * len(arrays), limit=3 + moved // MEGA, moved=moved
    )(place, *arrays)
    chain.take(results)
    return results[0]


def per_device_by_images(
    features,
    cotangent,
    norm1_gain,
    norm1_shift,
    conv1_kernel,
    conv1_shift,
    norm2_gain,
    norm2_shift,
    conv2_kernel,
    conv2_shift,
    norm3_gain,
    norm3_shift,
    query_weight,
    query_shift,
    key_weight,
    value_weight,
    value_shift,
    out_weight,
    out_shift,
):
    rows, images, across, channels = features.shape
    total = rows * images * across
    place = own_place()
    lines = jnp.stack([
        norm1_gain, norm1_shift, norm2_gain, norm2_shift, norm3_gain, norm3_shift,
        conv1_shift, conv2_shift, query_shift, value_shift, out_shift, out_shift,
    ] + [out_shift] * 4)

    image = shape_of((total, channels), BF16)
    image_f32 = shape_of((total, channels), F32)
    piece = shape_of((total // 8, channels), BF16)
    stats_shape = shape_of((8, channels), F32)
    cat = pltpu.VMEM((total + 2 * across, 3 * channels), BF16)
    bf16_image = pltpu.VMEM((total, channels), BF16)
    f32_image = pltpu.VMEM((total, channels), F32)
    tall = (3, 3 * channels, channels)

    sent, kept = pack_by_core(place, features)
    got = exchange(sent, "core")
    cot_sent, cot_kept = pack_by_core(place, after((cotangent,), sent)[0])
    feature_pairs, _ = pair_up(place, kept, after((got,), cot_sent)[0])
    feature_pieces = swap_pieces(feature_pairs, 2)
    cot_got = exchange(after((cot_sent,), feature_pairs[0])[0], "core")
    cot_pairs, (weight1, weight2, q_weight, k_weight, v_weight, o_weight, same) = pair_up(
        place,
        cot_kept,
        cot_got,
        after(
            (conv1_kernel.reshape(tall), conv2_kernel.reshape(tall), query_weight, key_weight,
             value_weight, out_weight),
            feature_pairs[0],
        ),
    )
    cot_near = tie(cot_pairs, feature_pieces[1:2])
    cot_far = tie(cot_pairs, feature_pieces[1:])
    cot_pieces = swap_pieces([cot_pairs[0], cot_near[1], *cot_far[2:]], 2)

    (image_in, act_one, conv_one, act_two, residual, stats, normed, query, key, value) = kernel_call(
        forward_body,
        [image, image, image_f32, image, image_f32, stats_shape] + [image] * 4,
        [SMEM] + [VMEM] * 11,
        [cat, pltpu.VMEM((8, channels), F32)],
        limit=FORWARD_LIMIT,
        moved=24 * MEGA,
        flops=5 * 10**9,
    )(place, *feature_pieces, lines, same, weight1, weight2, q_weight, k_weight, v_weight)
    act_two_got = exchange(act_two, "core")
    half = channels // 2
    four = shape_of((4, total // 8, channels), BF16)
    halves = shape_of((4, channels, half), BF16)
    grad_half = shape_of((total, half), BF16)
    (out_sent, out_kept, linear_sent, linear_kept, small_three, d_resid, d_conv_two,
     d_sent_two) = kernel_call(
        attention_body,
        [four, four, halves, halves, stats_shape, image_f32, image, grad_half],
        [SMEM] + [VMEM] * 16,
        [bf16_image] * 7 + [pltpu.VMEM((total, total), BF16)] * 2,
        limit=ATTEND_LIMIT,
        moved=16 * MEGA,
    )(
        place, *cot_pieces, query, key, value, normed, residual, stats, lines, same,
        o_weight, q_weight, k_weight, v_weight,
    )
    d_got_two = exchange(d_sent_two, "core")
    linear_got = exchange(linear_sent, "core")
    half_cat = pltpu.VMEM((total + 2 * across, 3 * half), BF16)

    def kernel_grad(made, *arrays):
        parts = []
        for kernel_rows, carries, _ in made:
            planes = 3 * len(kernel_rows) + 4 * carries
            parts += [shape_of((planes * half, half), BF16)] * 2
        return kernel_call(
            lambda *refs: kernel_grad_body(made, *refs), parts, [SMEM] + [VMEM] * len(arrays),
            [half_cat] * 2 + [pltpu.VMEM((channels, total), BF16)] * 2,
            limit=14, moved=8 * MEGA,
        )(place, *arrays)

    linear_part = shape_of((4 * half, half), BF16)

    def second_input_grad(grad):
        return kernel_call(
            lambda *refs: input_grad_body(False, 2, *refs),
            [image, grad_half, stats_shape, linear_part, linear_part],
            [SMEM] + [VMEM] * 8, [cat, f32_image],
            limit=16, moved=10 * MEGA,
        )(place, grad, weight2, conv_one, stats, lines, same, linear_kept, linear_got)

    def first_input_grad(grad):
        return kernel_call(
            lambda *refs: input_grad_body(True, 0, *refs),
            [four, four, shape_of((TAIL, half), BF16)],
            [SMEM] + [VMEM] * 9,
            [cat, f32_image, bf16_image, pltpu.VMEM((SMALL, channels), F32)],
            limit=16, moved=10 * MEGA,
        )(place, grad, weight1, image_in, stats, lines, same, d_resid, small_two, small_three)

    chains, groups, sums = {}, {}, {}

    def begin(letter, parts, made):
        for number, group in enumerate(made):
            name = letter + str(number)
            chains[name] = SumChain(*parts[2 * number : 2 * number + 2], group[2])
            groups[name] = group

    def end(name, token, sides):
        chain = chains[name]
        arrays = after([(chain.kept, chain.got)[side] for side in sides], token)
        sources = list(zip(arrays, sides))
        kernel_rows, carries, _ = groups[name]
        taps = 3 * len(kernel_rows)
        targets = {}
        if taps:
            targets[name[0]] = (sums.get(name[0]), 9, 3 * kernel_rows[0], 0, taps)
        for index in range(4 * carries):
            targets["linear" + str(index)] = (None, 1, 0, taps + index, 1)
        with_tail = chain.small is not None
        made = join_last(
            place, sources, list(targets.values()), sums.get(name + "tail"), with_tail
        )
        sums.update(zip(targets, made))
        if with_tail:
            sums["small" if name + "tail" in sums else name + "tail"] = made[-1]
        return made[0]

    token = small_three
    for event in " ".join(PLAN).split():
        if event == "W2":
            parts = kernel_grad(
                SECOND_GROUPS, act_two, act_two_got, after((d_conv_two,), token)[0], d_got_two
            )
            begin("B", parts, SECOND_GROUPS)
            token = parts[0]
            act_one_got = exchange(after((act_one,), token)[0], "core")
        elif event == "D2":
            d_conv_one, d_sent_one, small_two, *parts = second_input_grad(
                after((d_conv_two,), token)[0]
            )
            begin("L", parts, (((), True, LINEAR_ORDER),))
            d_got_one = exchange(d_sent_one, "core")
            token = small_two
        elif event == "W1":
            parts = kernel_grad(
                FIRST_GROUPS, act_one, act_one_got, after((d_conv_one,), token)[0], d_got_one
            )
            begin("C", parts, FIRST_GROUPS)
            token = parts[0]
        elif event == "D1":
            sent, kept, small = first_input_grad(after((d_conv_one,), token)[0])
            token = small
            chains["G"] = ReturnChain(sent, kept, features.shape)
            chains[RIDE].small = small
        elif event == "O!":
            chains["O"] = ReturnChain(*after((out_sent, out_kept), token), features.shape)
        elif event.endswith("<"):
            token = end(event[:-1], token, (0,))
        elif event.endswith(">"):
            token = end(event[:-1], token, (1,))
        elif event in groups and chains[event].at == 8:
            token = end(event, token, (0, 1))
        else:
            token = step(place, chains[event], token)

    output, features_grad = chains["O"].kept, chains["G"].kept
    small = sums["small"]
    linear_sum = [sums["linear" + str(index)].reshape(channels, channels) for index in range(4)]
    conv2_sum, conv1_sum = sums["B"], sums["C"]
    return (
        output,
        features_grad,
        small[0],
        small[1],
        conv1_sum.reshape(conv1_kernel.shape),
        small[4],
        small[2],
        small[3],
        conv2_sum.reshape(conv2_kernel.shape),
        small[10],
        small[5],
        small[6],
        linear_sum[0],
        small[7],
        linear_sum[1],
        linear_sum[2],
        small[8],
        linear_sum[3],
        small[9],
    )


def per_device(features, *rest):
    rows, imgs = lax.axis_size("rows"), lax.axis_size("imgs")
    if (rows, imgs) == (8, 4) and features.shape[1] == rows and features.shape[2] == ACROSS:
        return per_device_by_images(features, *rest)
    return per_device_by_rows(features, *rest)


def solution(mesh):
    placed = (
        P("rows", "imgs", None, None),
        P("rows", "imgs", None, None),
        P(),
        P(),
        P(),
        P(),
        P(),
        P(),
        P(),
        P(),
        P(),
        P(),
        P(),
        P(),
        P(),
        P(),
        P(),
        P(),
        P(),
    )
    return jax.shard_map(
        per_device,
        mesh=mesh,
        in_specs=placed,
        out_specs=(
            P("rows", "imgs", None, None),
            P("rows", "imgs", None, None),
            P(),
            P(),
            P(),
            P(),
            P(),
            P(),
            P(),
            P(),
            P(),
            P(),
            P(),
            P(),
            P(),
            P(),
            P(),
            P(),
            P(),
        ),
        check_vma=False,
    )
```

```python
import math

import jax
import jax.numpy as jnp
from jax import lax
from jax.experimental import pallas as pl
from jax.experimental.pallas import tpu as pltpu
from jax.sharding import PartitionSpec as P

GROUPS = 32
H = 32


EPSILON = 1e-06


def padded_2(block, sides, width):
    for axis, dim in sides:
        count = lax.axis_size(axis)
        forward = [(i, i + 1) for i in range(count - 1)]
        backward = [(target, source) for source, target in forward]
        low = lax.ppermute(
            lax.slice_in_dim(block, block.shape[dim] - width, None, axis=dim), axis, forward
        )
        high = lax.ppermute(lax.slice_in_dim(block, 0, width, axis=dim), axis, backward)
        block = jnp.concatenate([low, block, high], axis=dim)
    return block


def sigmoid_pair(tensor):
    logistic = jax.nn.sigmoid(tensor)
    return (tensor * logistic, logistic * (1.0 + tensor * (1.0 - logistic)))


def group_view(tensor):
    height, images, across, channels = tensor.shape
    return tensor.reshape(height, images, across, GROUPS, channels // GROUPS)


def spread_back(statistic):
    return statistic[None, :, None, :, None]


def norm_forward(tensor, norm_gain, norm_offset):
    grouped = group_view(tensor)
    members = H * tensor.shape[2] * (tensor.shape[3] // GROUPS)
    centre = lax.psum(jnp.sum(grouped, axis=(0, 2, 4)), "rows") / members
    centered = grouped - spread_back(centre)
    spread = lax.psum(jnp.sum(jnp.square(centered), axis=(0, 2, 4)), "rows") / members
    factor = lax.rsqrt(spread + EPSILON)
    normed = (centered * spread_back(factor)).reshape(tensor.shape)
    return (normed * norm_gain + norm_offset, normed, factor)


def norm_backward(gradient, normed, factor, norm_gain):
    gain_grad = jnp.sum(gradient * normed, axis=(0, 1, 2))
    offset_grad = jnp.sum(gradient, axis=(0, 1, 2))
    scaled = group_view(gradient * norm_gain)
    flat_normed = group_view(normed)
    members = H * gradient.shape[2] * (gradient.shape[3] // GROUPS)
    mean_grad, cross_grad = lax.psum(
        (jnp.sum(scaled, axis=(0, 2, 4)), jnp.sum(scaled * flat_normed, axis=(0, 2, 4))), "rows"
    )
    input_grad = (
        scaled - spread_back(mean_grad / members) - flat_normed * spread_back(cross_grad / members)
    ) * spread_back(factor)
    return (input_grad.reshape(gradient.shape), gain_grad, offset_grad)


def widen(tensor):
    return jnp.pad(tensor, ((0, 0), (0, 0), (1, 1), (0, 0)))


def conv_forward(tensor, kernel, offset):
    height, across = (tensor.shape[0], tensor.shape[2])
    padded = widen(padded_2(tensor, (("rows", 0),), 1))
    summed = jnp.zeros(tensor.shape[:3] + (kernel.shape[3],), jnp.float32)
    for row_off in range(3):
        for col_off in range(3):
            window = padded[row_off : row_off + height, :, col_off : col_off + across, :]
            summed = summed + jnp.einsum(
                "rbwc,cd->rbwd",
                window,
                kernel[row_off, col_off],
                preferred_element_type=jnp.float32,
            )
    return (summed + offset, padded)


def conv_backward(gradient, padded, kernel):
    height, across = (gradient.shape[0], gradient.shape[2])
    beside_all = widen(padded_2(gradient, (("rows", 0),), 1))
    input_grad = jnp.zeros(gradient.shape[:3] + (kernel.shape[2],), jnp.float32)
    tap_grads = []
    for row_off in range(3):
        for col_off in range(3):
            window = beside_all[
                2 - row_off : 2 - row_off + height, :, 2 - col_off : 2 - col_off + across, :
            ]
            input_grad = input_grad + jnp.einsum(
                "rbwd,cd->rbwc",
                window,
                kernel[row_off, col_off],
                preferred_element_type=jnp.float32,
            )
            source = padded[row_off : row_off + height, :, col_off : col_off + across, :]
            tap_grads.append(
                jnp.einsum("rbwc,rbwd->cd", source, gradient, preferred_element_type=jnp.float32)
            )
    kernel_grad = jnp.stack(tap_grads).reshape(kernel.shape)
    offset_grad = jnp.sum(gradient.astype(jnp.float32), axis=(0, 1, 2))
    return (input_grad, kernel_grad, offset_grad)


def linear(tensor, weight):
    return jnp.einsum("rbwc,cd->rbwd", tensor, weight, preferred_element_type=jnp.float32)


def back_linear(gradient, weight):
    return jnp.einsum("rbwd,cd->rbwc", gradient, weight, preferred_element_type=jnp.float32)


def weight_product(tensor, gradient):
    return jnp.einsum("rbwc,rbwd->cd", tensor, gradient, preferred_element_type=jnp.float32)


def image_to_sequence(tensor):
    height, images, across, channels = tensor.shape
    return tensor.transpose(1, 0, 2, 3).reshape(images, height * across, channels)


def from_sequence(sequence, height, across):
    images, length, channels = sequence.shape
    return sequence.reshape(images, height, across, channels).transpose(1, 0, 2, 3)


def reduce_all(gradients):
    flattened = jnp.concatenate([gradient.reshape(-1) for gradient in gradients])
    length = flattened.shape[0]
    devices = lax.axis_size("rows") * lax.axis_size("imgs")
    per_share = -(-length // (devices * 128)) * 128
    padded_len = per_share * devices
    strided = jnp.pad(flattened, (0, padded_len - length)).reshape(per_share, devices).T
    packed = strided.reshape(padded_len // 128, 128)
    my_share = lax.psum_scatter(packed, ("rows", "imgs"), scatter_dimension=0, tiled=True)
    summed_all = lax.all_gather(
        my_share.astype(jnp.bfloat16), ("rows", "imgs"), axis=0, tiled=True
    ).astype(my_share.dtype)
    summed_all = summed_all.reshape(devices, per_share).T.reshape(-1)
    results = []
    offset_at = 0
    for gradient in gradients:
        results.append(summed_all[offset_at : offset_at + gradient.size].reshape(gradient.shape))
        offset_at = offset_at + gradient.size
    return results


def per_device_by_rows(
    features,
    cotangent,
    norm1_gain,
    norm1_shift,
    conv1_kernel,
    conv1_shift,
    norm2_gain,
    norm2_shift,
    conv2_kernel,
    conv2_shift,
    norm3_gain,
    norm3_shift,
    query_weight,
    query_shift,
    key_weight,
    value_weight,
    value_shift,
    out_weight,
    out_shift,
):
    height, images, across, channels = features.shape
    attention_score_scale = 1.0 / math.sqrt(channels)
    inputs = features.astype(jnp.float32)
    norm_one, normed_one, factor_one = norm_forward(inputs, norm1_gain, norm1_shift)
    act_one, slope_one = sigmoid_pair(norm_one)
    conv_one, padded_one = conv_forward(act_one.astype(jnp.bfloat16), conv1_kernel, conv1_shift)
    norm_two, normed_two, factor_two = norm_forward(conv_one, norm2_gain, norm2_shift)
    act_two, slope_two = sigmoid_pair(norm_two)
    conv_two, padded_two = conv_forward(act_two.astype(jnp.bfloat16), conv2_kernel, conv2_shift)
    residual = inputs + conv_two
    norm_three, normed_three, factor_three = norm_forward(residual, norm3_gain, norm3_shift)
    attend_input = norm_three.astype(jnp.bfloat16)
    query_rows = (linear(attend_input, query_weight) + query_shift).astype(jnp.bfloat16)
    key_state_rows = linear(attend_input, key_weight).astype(jnp.bfloat16)
    value_state_rows = (linear(attend_input, value_weight) + value_shift).astype(jnp.bfloat16)
    all_keys, all_values = (
        lax.all_gather(key_state_rows, "rows", axis=0, tiled=True),
        lax.all_gather(value_state_rows, "rows", axis=0, tiled=True),
    )
    query_sequence = image_to_sequence(query_rows)
    key_sequence = image_to_sequence(all_keys)
    value_sequence = image_to_sequence(all_values)
    attention_scores = (
        jnp.einsum("xao,xno->xan", query_sequence, key_sequence, preferred_element_type=jnp.float32)
        * attention_score_scale
    )
    row_peak = jnp.max(attention_scores, axis=-1, keepdims=True)
    log_total = row_peak + jnp.log(
        jnp.sum(jnp.exp(attention_scores - row_peak), axis=-1, keepdims=True)
    )
    weight_tensors = jnp.exp(attention_scores - log_total).astype(jnp.bfloat16)
    attended_seq = jnp.einsum(
        "afj,ajy->afy", weight_tensors, value_sequence, preferred_element_type=jnp.float32
    )
    attention_output = from_sequence(attended_seq.astype(jnp.bfloat16), height, across)
    output = residual + linear(attention_output, out_weight) + out_shift
    out_shift_grad = jnp.sum(cotangent.astype(jnp.float32), axis=(0, 1, 2))
    out_weight_grad = weight_product(attention_output, cotangent)
    mixed_grad = back_linear(cotangent, out_weight).astype(jnp.bfloat16)
    mixed_sequence = image_to_sequence(mixed_grad)
    scores_again = (
        jnp.einsum("xao,xno->xan", query_sequence, key_sequence, preferred_element_type=jnp.float32)
        * attention_score_scale
    )
    probabilities = jnp.exp(scores_again - log_total)
    probability_gradient = jnp.einsum(
        "xao,xno->xan", mixed_sequence, value_sequence, preferred_element_type=jnp.float32
    )
    delta = jnp.sum(probabilities * probability_gradient, axis=-1, keepdims=True)
    score_gradient = (probabilities * (probability_gradient - delta)).astype(jnp.bfloat16)
    query_local = (
        jnp.einsum("afj,ajy->afy", score_gradient, key_sequence, preferred_element_type=jnp.float32)
        * attention_score_scale
    )
    query_grad = from_sequence(query_local, height, across).astype(jnp.bfloat16)
    key_full = (
        jnp.einsum(
            "svt,svz->stz", score_gradient, query_sequence, preferred_element_type=jnp.float32
        )
        * attention_score_scale
    )
    value_full = jnp.einsum(
        "svt,svz->stz",
        probabilities.astype(jnp.bfloat16),
        mixed_sequence,
        preferred_element_type=jnp.float32,
    )
    stacked = from_sequence(jnp.concatenate([key_full, value_full], axis=-1), H, across)
    own_grads = lax.psum_scatter(
        stacked.astype(jnp.bfloat16), "rows", scatter_dimension=0, tiled=True
    ).astype(jnp.float32)
    key_grad = own_grads[..., :channels].astype(jnp.bfloat16)
    value_grad = own_grads[..., channels:].astype(jnp.bfloat16)
    query_weight_grad = weight_product(attend_input, query_grad)
    query_shift_grad = jnp.sum(query_grad.astype(jnp.float32), axis=(0, 1, 2))
    key_weight_grad = weight_product(attend_input, key_grad)
    value_weight_grad = weight_product(attend_input, value_grad)
    value_shift_grad = jnp.sum(value_grad.astype(jnp.float32), axis=(0, 1, 2))
    attend_grad = (
        back_linear(query_grad, query_weight)
        + back_linear(key_grad, key_weight)
        + back_linear(value_grad, value_weight)
    )
    resid_part, norm3_gain_grad, norm3_shift_grad = norm_backward(
        attend_grad, normed_three, factor_three, norm3_gain
    )
    resid_grad = cotangent.astype(jnp.float32) + resid_part
    conv_two_in, conv2_kernel_grad, conv2_shift_grad = conv_backward(
        resid_grad.astype(jnp.bfloat16), padded_two, conv2_kernel
    )
    conv_one_out, norm2_gain_grad, norm2_shift_grad = norm_backward(
        conv_two_in * slope_two, normed_two, factor_two, norm2_gain
    )
    conv_one_in, conv1_kernel_grad, conv1_shift_grad = conv_backward(
        conv_one_out.astype(jnp.bfloat16), padded_one, conv1_kernel
    )
    inputs_part, norm1_gain_grad, norm1_shift_grad = norm_backward(
        conv_one_in * slope_one, normed_one, factor_one, norm1_gain
    )
    features_grad = resid_grad + inputs_part
    reduced = reduce_all(
        [
            norm1_gain_grad,
            norm1_shift_grad,
            conv1_kernel_grad,
            conv1_shift_grad,
            norm2_gain_grad,
            norm2_shift_grad,
            conv2_kernel_grad,
            conv2_shift_grad,
            norm3_gain_grad,
            norm3_shift_grad,
            query_weight_grad,
            query_shift_grad,
            key_weight_grad,
            value_weight_grad,
            value_shift_grad,
            out_weight_grad,
            out_shift_grad,
        ]
    )
    return (output, features_grad) + tuple(reduced)


F32 = jnp.float32
BF16 = jnp.bfloat16
AXES = ("rows", "imgs")
MEGA = 1024 * 1024
TILE = 64
MM_TILE = 256
ACROSS = 32
UNROLLED = 4
FLOPS = 3 * 10**10
BYTES = 1
BRIEF = 10**7
FORWARD_LIMIT = 18
ATTEND_LIMIT = 18
SECOND_GROUPS = (((0, 1, 2), False, "XYNF"),)
FIRST_GROUPS = (((0, 1, 2), False, "XYNF"),)
LINEAR_ORDER = "XYNF"
ORDER_SLOTS = {"X": 2, "Y": 3, "N": 4, "F": 5}
RIDE = "C0"
TAIL = 32
SMALL = 16
PLAN = (
    "W2 O! D2 O", "B0 W1 B0 D1", "B0 C0 B0 L0", "C0 B0 C0 B0",
    "L0 C0 B0 C0", "L0 G L0 C0", "B0 L0 O C0", "B0 L0 G L0",
    "O C0 C0< L0", "G C0> L0",
)
STEPS = ("core", "plane_a", "plane_b", "near", "far")
VMEM = pl.BlockSpec(memory_space=pltpu.VMEM)
SMEM = pl.BlockSpec(memory_space=pltpu.SMEM)
HBM = pl.BlockSpec(memory_space=pltpu.HBM)


def shape_of(shape, dtype):
    return jax.ShapeDtypeStruct(shape, dtype)


def kernel_call(
    body, out_shape, in_specs, scratch=(), limit=24, moved=0, flops=FLOPS
):
    return pl.pallas_call(
        body,
        out_shape=out_shape,
        in_specs=in_specs,
        out_specs=jax.tree.map(lambda _: VMEM, out_shape),
        scratch_shapes=list(scratch),
        compiler_params=pltpu.CompilerParams(vmem_limit_bytes=limit * MEGA),
        cost_estimate=pl.CostEstimate(
            flops=flops, bytes_accessed=BYTES * moved, transcendentals=0
        ),
    )


def tiles(total, size, body):
    if total // size <= UNROLLED:
        for index in range(total // size):
            body(index * size)
        return

    def step(index, carry):
        body(pl.multiple_of(index * size, size))
        return carry

    lax.fori_loop(0, total // size, step, 0)


def fold_tiles(total, size, body, carry):
    if total // size <= UNROLLED:
        for index in range(total // size):
            carry = body(index * size, carry)
        return carry

    def step(index, held):
        return body(pl.multiple_of(index * size, size), held)

    return lax.fori_loop(0, total // size, step, carry)


def fold_rows(tensor):
    return jnp.sum(tensor.reshape(tensor.shape[0] // 8, 8, tensor.shape[1]), axis=0)


def column(partial):
    return jnp.sum(partial, axis=0, keepdims=True)


def group_means(same_ref, columns, members):
    channels = columns[0].shape[1]
    place = lax.broadcasted_iota(jnp.int32, (8, channels), 0)
    rows = jnp.zeros((8, channels), F32)
    for number, values in enumerate(columns):
        left = values
        for term in range(3):
            part = left.astype(BF16).astype(F32)
            left = left - part
            rows = jnp.where(place == 3 * number + term, part, rows)
    summed = dot(rows.astype(BF16), same_ref[...])
    return [
        (summed[3 * n : 3 * n + 1] + summed[3 * n + 1 : 3 * n + 2] + summed[3 * n + 2 : 3 * n + 3])
        * (1.0 / members)
        for n in range(len(columns))
    ]


def pivot_sums(values, pivot):
    moved = values - pivot
    return fold_rows(moved), fold_rows(moved * moved)


def norm_stats(same_ref, sums, squares, pivot, total):
    channels = pivot.shape[1]
    size = channels // GROUPS
    sums, squares = column(sums), column(squares)
    (centre,) = group_means(same_ref, [sums + total * pivot], total * size)
    offset = pivot - centre
    (spread,) = group_means(
        same_ref, [squares + offset * (2.0 * sums + total * offset)], total * size
    )
    return centre, lax.rsqrt(spread + EPSILON)


def fill_shifted(cat_ref, at, tile):
    size, channels = tile.shape
    place = lax.broadcasted_iota(jnp.int32, tile.shape, 0) % ACROSS
    before = jnp.where(place == 0, 0.0, pltpu.roll(tile, 1, 0))
    after = jnp.where(place == ACROSS - 1, 0.0, pltpu.roll(tile, size - 1, 0))
    rows = pl.ds(pl.multiple_of(ACROSS + at, ACROSS), size)
    cat_ref[rows, 0:channels] = before.astype(BF16)
    cat_ref[rows, channels : 2 * channels] = tile.astype(BF16)
    cat_ref[rows, 2 * channels : 3 * channels] = after.astype(BF16)


def clear_border(cat_ref):
    total, width = cat_ref.shape
    cat_ref[0:ACROSS, :] = jnp.zeros((ACROSS, width), BF16)
    cat_ref[total - ACROSS : total, :] = jnp.zeros((ACROSS, width), BF16)


def at_rows(at):
    return at if isinstance(at, int) else pl.multiple_of(at, ACROSS)


def window_product(cat_ref, weight_ref, at, size):
    total = None
    for row_off in range(3):
        rows = pl.ds(at_rows(at + row_off * ACROSS), size)
        part = jnp.dot(cat_ref[rows, :], weight_ref[row_off], preferred_element_type=F32)
        total = part if total is None else total + part
    return total


def window_product_turned(cat_ref, weight_ref, at, size):
    channels = weight_ref.shape[2]
    total = None
    for row_off in range(3):
        rows = pl.ds(at_rows(at + (2 - row_off) * ACROSS), size)
        for col_off in range(3):
            low = (2 - col_off) * channels
            tap = weight_ref[row_off, col_off * channels : (col_off + 1) * channels, :]
            part = dot_t(cat_ref[rows, low : low + channels], tap)
            total = part if total is None else total + part
    return total


def dot_t(left, right):
    return lax.dot_general(left, right, (((1,), (1,)), ((), ())), preferred_element_type=F32)


def t_dot(left, right):
    return lax.dot_general(left, right, (((0,), (0,)), ((), ())), preferred_element_type=F32)


def dot(left, right):
    return jnp.dot(left, right, preferred_element_type=F32)


def line(lines_ref, row):
    return lines_ref[row : row + 1, :]


def forward_body(place_ref, *refs):
    pairs = refs[:4]
    (lines_ref, same_ref, weight1_ref, weight2_ref, q_weight_ref, k_weight_ref, v_weight_ref,
     o_weight_ref, image_ref, act1_ref, conv_ref, act2_ref, resid_ref, stats_ref, norm_ref, q_ref, k_ref, v_ref,
     weights_ref, mixed_ref, out_sent_ref, out_kept_ref, cat_ref, pivot_ref, out_ref) = refs[4:]
    total, channels = image_ref.shape
    share = total // 8
    me = place_ref[0]
    for index in range(8):
        at = pl.multiple_of((me ^ index) * share, share)
        image_ref[pl.ds(at, share), :] = pairs[index // 2][index % 2]
    clear_border(cat_ref)
    zero = jnp.zeros((8, channels), F32)

    def activate_all(read, stats, stats_row, gain_row, act_ref):
        centre, factor = stats
        stats_ref[stats_row : stats_row + 1, :] = centre
        stats_ref[stats_row + 1 : stats_row + 2, :] = factor
        scale = factor * line(lines_ref, gain_row)
        shift = line(lines_ref, gain_row + 1) - centre * scale

        def activate(at):
            held = read(at) * scale + shift
            act = held * jax.nn.sigmoid(held)
            act_ref[pl.ds(at, TILE), :] = act.astype(BF16)
            fill_shifted(cat_ref, at, act)

        tiles(total, TILE, activate)

    def read_image(at):
        return image_ref[pl.ds(at, TILE), :].astype(F32)

    pivot1 = read_image(0)[0:1, :]

    def sum_image(at, held):
        sums, squares = pivot_sums(read_image(at), pivot1)
        return held[0] + sums, held[1] + squares

    sums, squares = fold_tiles(total, TILE, sum_image, (zero, zero))
    stats1 = norm_stats(same_ref, sums, squares, pivot1, total)
    activate_all(read_image, stats1, 0, 0, act1_ref)

    def convolve_all(weight_ref, bias, more, target_ref):
        def convolve(at, held):
            rows = pl.ds(at, MM_TILE)
            values = window_product(cat_ref, weight_ref, at, MM_TILE) + bias
            if more is not None:
                values = values + more[rows, :].astype(F32)

            if isinstance(at, int):
                if at == 0:
                    pivot_ref[0:1, :] = values[0:1, :]
            else:

                @pl.when(at == 0)
                def _():
                    pivot_ref[0:1, :] = values[0:1, :]

            target_ref[rows, :] = values
            sums, squares = pivot_sums(values, pivot_ref[0:1, :])
            return held[0] + sums, held[1] + squares

        sums, squares = fold_tiles(total, MM_TILE, convolve, (zero, zero))
        return norm_stats(same_ref, sums, squares, pivot_ref[0:1, :], total)

    stats2 = convolve_all(weight1_ref, line(lines_ref, 6), None, conv_ref)
    activate_all(lambda at: conv_ref[pl.ds(at, TILE), :], stats2, 2, 2, act2_ref)
    centre3, factor3 = convolve_all(weight2_ref, line(lines_ref, 7), image_ref, resid_ref)
    stats_ref[4:5, :] = centre3
    stats_ref[5:6, :] = factor3
    stats_ref[6:8, :] = jnp.zeros((2, channels), F32)
    scale3 = factor3 * line(lines_ref, 4)
    shift3 = line(lines_ref, 5) - centre3 * scale3
    q_shift, v_shift = line(lines_ref, 8), line(lines_ref, 9)

    def project(at):
        rows = pl.ds(at, MM_TILE)
        held = (resid_ref[rows, :] * scale3 + shift3).astype(BF16)
        norm_ref[rows, :] = held
        q_ref[rows, :] = (dot(held, q_weight_ref[...]) + q_shift).astype(BF16)
        k_ref[rows, :] = dot(held, k_weight_ref[...]).astype(BF16)
        v_ref[rows, :] = (dot(held, v_weight_ref[...]) + v_shift).astype(BF16)

    tiles(total, MM_TILE, project)
    o_shift = line(lines_ref, 10)
    root = 1.0 / math.sqrt(channels)

    def attend(at):
        rows = pl.ds(at, MM_TILE)
        scores = dot_t(q_ref[rows, :], k_ref[...]) * root
        exps = jnp.exp(scores - jnp.max(scores, axis=-1, keepdims=True))
        weights = (exps * (1.0 / jnp.sum(exps, axis=-1, keepdims=True))).astype(BF16)
        weights_ref[rows, :] = weights
        mixed = dot(weights, v_ref[...]).astype(BF16)
        mixed_ref[rows, :] = mixed
        out_ref[rows, :] = (
            resid_ref[rows, :] + dot(mixed, o_weight_ref[...]) + o_shift
        ).astype(BF16)

    tiles(total, MM_TILE, attend)
    return_pieces(place_ref, out_ref, out_sent_ref, out_kept_ref)


def lane_half(part, half):
    return pl.ds(pl.multiple_of(part * half, half), half)


def z_bits(core):
    return 2 << core, 4 >> core


def return_pieces(place_ref, out_ref, sent_ref, kept_ref):
    share = out_ref.shape[0] // 8
    me, core = place_ref[0], place_ref[1]
    for target, side in ((kept_ref, 0), (sent_ref, 1)):
        first, second = z_bits(core if side == 0 else 1 - core)
        for index in range(4):
            offset = side + (index // 2) * first + (index % 2) * second
            at = pl.multiple_of((me ^ offset) * share, share)
            target[index] = out_ref[pl.ds(at, share), :]


def attention_body(place_ref, *refs):
    cot_pieces = refs[:4]
    (q_ref, k_ref, v_ref, norm_ref, resid_ref, stats_ref, weights_ref, mixed_ref, lines_ref, same_ref,
     o_weight_ref, q_weight_ref, k_weight_ref, v_weight_ref) = refs[4:18]
    (sent_ref, kept_ref, small_ref, d_resid_ref, d_conv_ref, d_sent_ref,
     cot_ref, d_mixed_ref, d_q_ref, d_k_ref, d_v_ref, d_scores_ref) = refs[18:]
    total, channels = q_ref.shape
    share = total // 8
    scale = 1.0 / math.sqrt(channels)
    me = place_ref[0]
    for index in range(8):
        at = pl.multiple_of((me ^ index) * share, share)
        cot_ref[pl.ds(at, share), :] = cot_pieces[index // 2][index % 2]
    zero = jnp.zeros((8, channels), F32)

    def attend(at, held):
        rows = pl.ds(at, MM_TILE)
        cot = cot_ref[rows, :]
        d_mixed = dot_t(cot, o_weight_ref[...]).astype(BF16)
        d_mixed_ref[rows, :] = d_mixed
        d_prob = dot_t(d_mixed, v_ref[...])
        probs = weights_ref[rows, :].astype(F32)
        delta = jnp.sum(probs * d_prob, axis=-1, keepdims=True)
        d_scores = (probs * (d_prob - delta)).astype(BF16)
        d_scores_ref[rows, :] = d_scores
        d_query = (dot(d_scores, k_ref[...]) * scale).astype(BF16)
        d_q_ref[rows, :] = d_query
        return held[0] + fold_rows(cot.astype(F32)), held[1] + fold_rows(d_query.astype(F32))

    cot_sums, d_q_sums = fold_tiles(total, MM_TILE, attend, (zero, zero))

    def to_keys(at, held):
        rows = pl.ds(at, MM_TILE)
        d_k_ref[rows, :] = (t_dot(d_scores_ref[:, rows], q_ref[...]) * scale).astype(BF16)
        d_value = t_dot(weights_ref[:, rows], d_mixed_ref[...]).astype(BF16)
        d_v_ref[rows, :] = d_value
        return held + fold_rows(d_value.astype(F32))

    d_v_sums = fold_tiles(total, MM_TILE, to_keys, zero)
    half = channels // 2
    core = place_ref[1]
    for index, (left, right) in enumerate(
        ((norm_ref, d_q_ref), (norm_ref, d_k_ref), (norm_ref, d_v_ref), (mixed_ref, cot_ref))
    ):
        for target, part in ((sent_ref, 1 - core), (kept_ref, core)):
            target[index] = t_dot(left[...], right[:, lane_half(part, half)]).astype(BF16)

    centre, factor = stats_ref[4:5, :], stats_ref[5:6, :]
    gain = line(lines_ref, 4)

    def back(at, held):
        rows = pl.ds(at, MM_TILE)
        grad = (
            dot_t(d_q_ref[rows, :], q_weight_ref[...])
            + dot_t(d_k_ref[rows, :], k_weight_ref[...])
            + dot_t(d_v_ref[rows, :], v_weight_ref[...])
        )
        d_resid_ref[rows, :] = grad
        normed = (resid_ref[rows, :] - centre) * factor
        return held[0] + fold_rows(grad), held[1] + fold_rows(grad * normed)

    sums = fold_tiles(total, MM_TILE, back, (zero, zero))
    shift_grad, gain_grad, o_shift_grad, q_shift_grad, v_shift_grad = [
        column(part) for part in (*sums, cot_sums, d_q_sums, d_v_sums)
    ]
    members = total * (channels // GROUPS)
    mean_grad, cross_grad = group_means(same_ref, [shift_grad * gain, gain_grad * gain], members)

    def finish(at, held):
        rows = pl.ds(at, TILE)
        normed = (resid_ref[rows, :] - centre) * factor
        grad = cot_ref[rows, :].astype(F32) + factor * (
            d_resid_ref[rows, :] * gain - mean_grad - normed * cross_grad
        )
        d_resid_ref[rows, :] = grad
        rounded = grad.astype(BF16)
        d_conv_ref[rows, :] = rounded
        d_sent_ref[rows, :] = d_conv_ref[rows, lane_half(1 - core, half)]
        return held + fold_rows(rounded.astype(F32))

    conv_shift_grad = column(fold_tiles(total, TILE, finish, zero))
    small_ref[0:1, :] = gain_grad
    small_ref[1:2, :] = shift_grad
    small_ref[2:3, :] = q_shift_grad
    small_ref[3:4, :] = v_shift_grad
    small_ref[4:5, :] = o_shift_grad
    small_ref[5:6, :] = conv_shift_grad
    small_ref[6:8, :] = jnp.zeros((2, channels), F32)


def kernel_grad_body(groups, place_ref, act_ref, act_got_ref, grad_ref, grad_got_ref, *refs):
    linear = any(carries for _, carries, _ in groups)
    more, refs = (refs[:2], refs[2:]) if linear else ((), refs)
    parts, (cat_ref, cat_got_ref, turned_ref, turned_got_ref) = refs[: 2 * len(groups)], refs[2 * len(groups) :]
    total, channels = act_ref.shape
    half = channels // 2
    core = place_ref[1]
    clear_border(cat_ref)
    clear_border(cat_got_ref)

    def fill(at):
        rows = pl.ds(at, TILE)
        fill_shifted(cat_ref, at, grad_ref[rows, lane_half(core, half)].astype(F32))
        fill_shifted(cat_got_ref, at, grad_got_ref[rows, :].astype(F32))

    tiles(total, TILE, fill)
    turned_ref[...] = act_ref[...].T
    turned_got_ref[...] = act_got_ref[...].T
    for number, (kernel_rows, carries, order) in enumerate(groups):
        bit = place_ref[ORDER_SLOTS[order[0]]]
        for target, part in ((parts[2 * number], 1 - bit), (parts[2 * number + 1], bit)):
            rows = pl.ds(pl.multiple_of(part * half, half), half)
            for index, row_off in enumerate(kernel_rows):
                span = pl.ds((2 - row_off) * ACROSS, total)
                product = (
                    dot(turned_ref[rows, :], cat_ref[span, :])
                    + dot(turned_got_ref[rows, :], cat_got_ref[span, :])
                ).astype(BF16)
                for col_off in range(3):
                    at = (3 * index + col_off) * half
                    low = (2 - col_off) * half
                    target[at : at + half, :] = product[:, low : low + half]
            if carries:
                for index in range(4):
                    at = (3 * len(kernel_rows) + index) * half
                    target[at : at + half, :] = (
                        more[0][index, rows, :].astype(F32) + more[1][index, rows, :].astype(F32)
                    ).astype(BF16)


def linear_halves(slot, place_ref, kept_ref, got_ref, sent_out, kept_out):
    bit = place_ref[slot]
    count, rows, half = kept_ref.shape
    rows //= 2
    for target, part in ((sent_out, 1 - bit), (kept_out, bit)):
        span = pl.ds(pl.multiple_of(part * rows, rows), rows)
        for index in range(count):
            target[index * rows : (index + 1) * rows, :] = (
                kept_ref[index, span, :].astype(F32) + got_ref[index, span, :].astype(F32)
            ).astype(BF16)


def input_grad_body(with_rest, stats_row, place_ref, *refs):
    grad_ref, weight_ref, source_ref, stats_ref, lines_ref, same_ref = refs[:6]
    if with_rest:
        rest_ref, small_two_ref, small_three_ref = refs[6:9]
    else:
        linear_kept_ref, linear_got_ref = refs[6:8]
    refs = refs[9:] if with_rest else refs[8:]
    if with_rest:
        sent_ref, kept_ref, small_ref, cat_ref, held_ref, out_ref, rows_ref = refs
    else:
        out_ref, d_sent_ref, small_ref, linear_sent_out, linear_kept_out, cat_ref, held_ref = refs
    core = place_ref[1]
    total, channels = grad_ref.shape
    centre = stats_ref[stats_row : stats_row + 1, :]
    factor = stats_ref[stats_row + 1 : stats_row + 2, :]
    gain, shift = line(lines_ref, stats_row), line(lines_ref, stats_row + 1)
    clear_border(cat_ref)

    def fill(at):
        fill_shifted(cat_ref, at, grad_ref[pl.ds(at, TILE), :].astype(F32))

    tiles(total, TILE, fill)

    zero = jnp.zeros((8, channels), F32)

    def product(at, held):
        rows = pl.ds(at, MM_TILE)
        normed = (source_ref[rows, :].astype(F32) - centre) * factor
        pre = normed * gain + shift
        logistic = jax.nn.sigmoid(pre)
        slope = logistic * (1.0 + pre * (1.0 - logistic))
        grad = window_product_turned(cat_ref, weight_ref, at, MM_TILE) * slope
        held_ref[rows, :] = grad
        return held[0] + fold_rows(grad), held[1] + fold_rows(grad * normed)

    shift_sum, gain_sum = fold_tiles(total, MM_TILE, product, (zero, zero))
    shift_grad, gain_grad = column(shift_sum), column(gain_sum)
    members = total * (channels // GROUPS)
    mean_grad, cross_grad = group_means(same_ref, [shift_grad * gain, gain_grad * gain], members)

    def finish(at, held):
        rows = pl.ds(at, TILE)
        normed = (source_ref[rows, :].astype(F32) - centre) * factor
        grad = factor * (held_ref[rows, :] * gain - mean_grad - normed * cross_grad)
        if with_rest:
            grad = grad + rest_ref[rows, :]
        rounded = grad.astype(BF16)
        out_ref[rows, :] = rounded
        if not with_rest:
            d_sent_ref[rows, :] = out_ref[rows, lane_half(1 - core, channels // 2)]
        return held + fold_rows(rounded.astype(F32))

    out_sum = column(fold_tiles(total, TILE, finish, zero))
    if not with_rest:
        linear_halves(
            ORDER_SLOTS[LINEAR_ORDER[0]], place_ref, linear_kept_ref, linear_got_ref, linear_sent_out,
            linear_kept_out,
        )
        small_ref[0:1, :] = gain_grad
        small_ref[1:2, :] = shift_grad
        small_ref[2:3, :] = out_sum
        small_ref[3:8, :] = jnp.zeros((5, channels), F32)
        return
    return_pieces(place_ref, out_ref, sent_ref, kept_ref)
    rows_ref[0:1, :] = gain_grad
    rows_ref[1:2, :] = shift_grad
    rows_ref[2:5, :] = small_two_ref[0:3, :]
    rows_ref[5:11, :] = small_three_ref[0:6, :]
    rows_ref[11:SMALL, :] = jnp.zeros((SMALL - 11, channels), F32)
    half = channels // 2
    small_ref[0:SMALL, :] = rows_ref[:, 0:half].astype(BF16)
    small_ref[SMALL:TAIL, :] = rows_ref[:, half:channels].astype(BF16)


def pack_by_core_body(place_ref, block_ref, sent_ref, kept_ref):
    me = place_ref[0]
    for target, side in ((kept_ref, 0), (sent_ref, 1)):
        for index in range(4):
            for row in range(block_ref.shape[0]):
                rows = pl.ds(row * ACROSS, ACROSS)
                target[index, rows, :] = block_ref[row, me ^ (2 * index + side)]


def pair_body(place_ref, kept_ref, got_ref, *refs):
    count = (len(refs) - 5) // 2
    staged, pair_refs, sems = refs[:count], refs[count : count + 4], refs[-1]
    targets = refs[count + 4 : 2 * count + 4]
    copies = [
        pltpu.make_async_copy(staged[index], targets[index], sems.at[index])
        for index in range(count)
    ]
    for copy in copies:
        copy.start()
    for index in range(4):
        pair_refs[index][0] = kept_ref[index]
        pair_refs[index][1] = got_ref[index]
    if count:
        same_ref = refs[2 * count + 4]
        one, two = (lax.broadcasted_iota(jnp.int32, same_ref.shape, dim) for dim in (0, 1))
        size = same_ref.shape[0] // GROUPS
        same_ref[...] = jnp.where(one // size == two // size, 1.0, 0.0).astype(BF16)
    for copy in copies:
        copy.wait()


def pack_by_core(place, block):
    rows, _, across, channels = block.shape
    four = shape_of((4, rows * across, channels), BF16)
    return kernel_call(
        pack_by_core_body, [four] * 2, [SMEM, VMEM], limit=8, moved=2 * MEGA
    )(place, block)


def pair_up(place, kept, got, staged=()):
    channels = kept.shape[2]
    pair = shape_of((2,) + kept.shape[1:], BF16)
    results = kernel_call(
        pair_body,
        [pair] * 4
        + [shape_of(array.shape, array.dtype) for array in staged]
        + [shape_of((channels, channels), BF16)] * bool(staged),
        [SMEM, VMEM, VMEM] + [HBM] * len(staged),
        [pltpu.SemaphoreType.DMA((max(len(staged), 1),))],
        limit=16 if staged else 8,
        moved=2 * MEGA,
        flops=BRIEF if staged else FLOPS,
    )(place, kept, got, *staged)
    return results[:4], results[4:]


def swap_pieces(pieces, unit):
    count = len(pieces)
    return [pieces[0]] + [
        lax.ppermute(pieces[k], "rows", [(r, r ^ (unit * k)) for r in range(count * unit)])
        for k in range(1, count)
    ]


def partner_table(kind):
    table = []
    for row in range(8):
        for img in range(4):
            core = row & 1
            if kind == "core":
                other = (row ^ 1, img)
            elif kind == "near":
                other = (row ^ (4 if core else 2), img)
            elif kind == "far":
                other = (row ^ (2 if core else 4), img)
            elif kind == "plane_a":
                other = (row, img ^ (2 if core else 1))
            else:
                other = (row, img ^ (1 if core else 2))
            table.append((row * 4 + img, other[0] * 4 + other[1]))
    return table


def exchange(tensor, kind):
    return lax.ppermute(tensor, AXES, partner_table(kind))


def own_place():
    row, img = lax.axis_index("rows"), lax.axis_index("imgs")
    core, near, far = row & 1, (row >> 1) & 1, (row >> 2) & 1
    low, high = img & 1, (img >> 1) & 1
    plane_a = jnp.where(core == 1, high, low)
    plane_b = jnp.where(core == 1, low, high)
    first_z = jnp.where(core == 1, far, near)
    second_z = jnp.where(core == 1, near, far)
    return jnp.stack([row, core, plane_a, plane_b, first_z, second_z, row, row]).astype(jnp.int32)


def add_tails(target, target_at, kept_ref, got_ref, at):
    target[target_at : target_at + TAIL, :] = (
        kept_ref[at : at + TAIL, :].astype(F32) + got_ref[at : at + TAIL, :].astype(F32)
    ).astype(BF16)


def add_split(chain, slot, place_ref, ins, outs):
    kept_ref, got_ref = ins[:2]
    count, rows = chain.count, chain.rows
    half = rows // 2
    bit = place_ref[slot]

    def one(index, carry):
        for target, part in zip(outs, (1 - bit, bit)):
            span = pl.ds(pl.multiple_of(index * rows + part * half, half), half)
            target[pl.ds(pl.multiple_of(index * half, half), half), :] = (
                kept_ref[span, :].astype(F32) + got_ref[span, :].astype(F32)
            ).astype(BF16)
        return carry

    lax.fori_loop(0, count, one, 0)
    if chain.small is not None:
        for target in outs:
            if len(ins) > 2:
                target[count * half : count * half + TAIL, :] = ins[2][...]
            else:
                add_tails(target, count * half, kept_ref, got_ref, count * rows)


def add_last(chain, slot, place_ref, ins, outs):
    outs[0][...] = (ins[0][...].astype(F32) + ins[1][...].astype(F32)).astype(BF16)


def join(chain, slot, place_ref, ins, outs):
    count, rows = chain.count, chain.rows
    bit = place_ref[slot]

    def one(index, carry):
        for source, part in zip(ins, (bit, 1 - bit)):
            span = pl.ds(pl.multiple_of((2 * index + part) * rows, rows), rows)
            outs[0][span, :] = source[pl.ds(pl.multiple_of(index * rows, rows), rows), :]
        return carry

    lax.fori_loop(0, count, one, 0)
    if chain.small is not None:
        at = count * rows
        if slot == chain.slots[0]:
            add_tails(outs[0], 2 * at, ins[0], ins[1], at)
        else:
            outs[0][2 * at : 2 * at + TAIL, :] = ins[0][at : at + TAIL, :]


def turn_pairs(chain, slot, place_ref, ins, outs):
    kept_ref, got_ref = ins
    for target, part in zip(outs, (1, 0)):
        for index in range(2):
            if slot == 0:
                target[index] = kept_ref[2 * part + index]
                target[2 + index] = got_ref[2 * part + index]
            else:
                target[index] = kept_ref[2 * index + part]
                target[2 + index] = got_ref[2 * index + part]


def spread(chain, slot, place_ref, ins, outs):
    me, core = place_ref[0], place_ref[1]
    first, second = z_bits(core)
    out_ref = outs[0]
    for source, side in zip(ins, (0, 1)):
        for index in range(4):
            image = me ^ ((index % 2) + (index // 2) * first + side * second)
            for row in range(out_ref.shape[0]):
                rows = pl.ds(row * ACROSS, ACROSS)
                out_ref[row, image] = source[index, rows, :].astype(F32)


def join_last(place, sources, targets, tail=None, with_tail=False):
    half = sources[0][0].shape[1]
    rows = 2 * half
    sides = [side for _, side in sources]
    count = sum(target[4] for target in targets)
    wholes = [target[0] for target in targets if target[0] is not None]
    tails = [] if tail is None else [tail]
    at_tail = sources[0][0].shape[0] - TAIL

    def body(place_ref, *refs):
        source_refs = refs[: len(sources)]
        refs = refs[len(sources) :]
        tail_refs, refs = refs[: len(tails)], refs[len(tails) + len(wholes) :]
        out_refs = refs[: len(targets)]
        held_ref, sems = refs[-2:]
        core = place_ref[1]
        copies = []
        for out_ref, (_, _, there, here, planes) in zip(out_refs, targets):
            for plane in range(planes):
                for number, side in enumerate(sides):
                    index = len(copies)
                    at = (here + plane) * rows
                    held_ref[index] = source_refs[number][at : at + rows, :].astype(F32)
                    part = 1 - core if side else core
                    copy = pltpu.make_async_copy(
                        held_ref.at[index],
                        out_ref.at[there + plane, :, lane_half(part, half)],
                        sems.at[index],
                    )
                    copy.start()
                    copies.append(copy)
        if with_tail:
            mine = source_refs[0][at_tail : at_tail + TAIL, :]
            if tails:
                total = mine.astype(F32) + tail_refs[0][...].astype(F32)
                refs[len(targets)][:, 0:half] = total[0:SMALL]
                refs[len(targets)][:, half : 2 * half] = total[SMALL:TAIL]
            else:
                refs[len(targets)][...] = mine
        for copy in copies:
            copy.wait()

    anywhere = pl.BlockSpec(memory_space=pl.ANY)
    aliases, taken = {}, 0
    for number, target in enumerate(targets):
        if target[0] is not None:
            aliases[1 + len(sources) + len(tails) + taken] = number
            taken += 1
    slots = count * len(sources)
    out_shape = [shape_of((target[1], rows, rows), F32) for target in targets]
    if with_tail:
        out_shape.append(
            shape_of((SMALL, 2 * half), F32) if tails else shape_of((TAIL, half), BF16)
        )
    return pl.pallas_call(
        body,
        out_shape=out_shape,
        in_specs=[SMEM] + [VMEM] * (len(sources) + len(tails)) + [anywhere] * len(wholes),
        out_specs=[anywhere] * len(targets) + [VMEM] * with_tail,
        input_output_aliases=aliases,
        scratch_shapes=[pltpu.VMEM((slots, rows, half), F32), pltpu.SemaphoreType.DMA((slots,))],
        compiler_params=pltpu.CompilerParams(vmem_limit_bytes=(slots // 2 + 6) * MEGA),
        cost_estimate=pl.CostEstimate(
            flops=FLOPS, bytes_accessed=BYTES * 6 * slots * rows * half, transcendentals=0
        ),
    )(place, *[array for array, _ in sources], *tails, *wholes)


def tie(values, earlier):
    return lax.optimization_barrier(tuple(values) + tuple(earlier))[: len(values)]


def after(values, token):
    tied = lax.optimization_barrier(tuple(values) + (token,))
    return tied[:-1]


class SumChain:
    def __init__(self, sent, kept, order):
        self.kept, self.at, self.small = kept, 0, None
        self.rows = kept.shape[1]
        self.count = kept.shape[0] // self.rows
        self.slots = [ORDER_SLOTS[letter] for letter in order]
        self.got = exchange(sent, STEPS[self.slots[0] - 1])

    def inputs(self):
        with_small = self.small is not None and self.at == 0
        return [self.kept, self.got] + ([self.small] if with_small else [])

    def todo(self):
        tail = 0 if self.small is None else TAIL
        lanes = self.kept.shape[1]
        at, size = self.at, self.count * self.rows
        if at < 3:
            return add_split, self.slots[at + 1], [shape_of((size // 2 + tail, lanes), BF16)] * 2
        if at == 3:
            return add_last, 0, [shape_of((size + tail, lanes), BF16)]
        return join, self.slots[7 - at], [shape_of((2 * size + tail, lanes), BF16)]

    def take(self, outs):
        at = self.at
        self.at += 1
        self.kept = outs[-1]
        if at < 3:
            self.rows //= 2
            slot = self.slots[at + 1]
        elif at == 3:
            slot = self.slots[3]
        else:
            self.rows *= 2
            slot = self.slots[6 - at] if at < 7 else 1
        self.got = exchange(outs[0], STEPS[slot - 1])


class ReturnChain:
    def __init__(self, sent, kept, block_shape):
        self.kept, self.at, self.block_shape = kept, 0, block_shape
        self.got = exchange(sent, "core")

    def inputs(self):
        return [self.kept, self.got]

    def todo(self):
        if self.at < 2:
            return turn_pairs, self.at, [shape_of(self.kept.shape, BF16)] * 2
        return spread, 0, [shape_of(self.block_shape, F32)]

    def take(self, outs):
        self.kept = outs[-1]
        if self.at < 2:
            self.got = exchange(outs[0], ("near", "far")[self.at])
        self.at += 1


def step(place, chain, token):
    work, slot, shapes = chain.todo()
    arrays = after(chain.inputs(), token)

    def body(place_ref, *refs):
        work(chain, slot, place_ref, refs[: len(arrays)], refs[len(arrays) :])

    moved = 2 * sum(a.size * a.dtype.itemsize for a in arrays)
    results = kernel_call(
        body, shapes, [SMEM] + [VMEM] * len(arrays), limit=3 + moved // MEGA, moved=moved
    )(place, *arrays)
    chain.take(results)
    return results[0]


def per_device_by_images(
    features,
    cotangent,
    norm1_gain,
    norm1_shift,
    conv1_kernel,
    conv1_shift,
    norm2_gain,
    norm2_shift,
    conv2_kernel,
    conv2_shift,
    norm3_gain,
    norm3_shift,
    query_weight,
    query_shift,
    key_weight,
    value_weight,
    value_shift,
    out_weight,
    out_shift,
):
    rows, images, across, channels = features.shape
    total = rows * images * across
    place = own_place()
    lines = jnp.stack([
        norm1_gain, norm1_shift, norm2_gain, norm2_shift, norm3_gain, norm3_shift,
        conv1_shift, conv2_shift, query_shift, value_shift, out_shift, out_shift,
    ] + [out_shift] * 4)

    image = shape_of((total, channels), BF16)
    image_f32 = shape_of((total, channels), F32)
    piece = shape_of((total // 8, channels), BF16)
    stats_shape = shape_of((8, channels), F32)
    cat = pltpu.VMEM((total + 2 * across, 3 * channels), BF16)
    bf16_image = pltpu.VMEM((total, channels), BF16)
    f32_image = pltpu.VMEM((total, channels), F32)
    tall = (3, 3 * channels, channels)

    sent, kept = pack_by_core(place, features)
    got = exchange(sent, "core")
    cot_sent, cot_kept = pack_by_core(place, after((cotangent,), sent)[0])
    feature_pairs, _ = pair_up(place, kept, after((got,), cot_sent)[0])
    feature_pieces = swap_pieces(feature_pairs, 2)
    cot_got = exchange(after((cot_sent,), feature_pairs[0])[0], "core")
    cot_pairs, (weight1, weight2, q_weight, k_weight, v_weight, o_weight, same) = pair_up(
        place,
        cot_kept,
        cot_got,
        after(
            (conv1_kernel.reshape(tall), conv2_kernel.reshape(tall), query_weight, key_weight,
             value_weight, out_weight),
            feature_pairs[0],
        ),
    )
    cot_near = tie(cot_pairs, feature_pieces[1:2])
    cot_far = tie(cot_pairs, feature_pieces[1:])
    cot_pieces = swap_pieces([cot_pairs[0], cot_near[1], *cot_far[2:]], 2)

    four = shape_of((4, total // 8, channels), BF16)
    square = shape_of((total, total), BF16)
    (image_in, act_one, conv_one, act_two, residual, stats, normed, query, key, value, weights, mixed,
     out_sent, out_kept) = kernel_call(
        forward_body,
        [image, image, image_f32, image, image_f32, stats_shape] + [image] * 4
        + [square, image, four, four],
        [SMEM] + [VMEM] * 12,
        [cat, pltpu.VMEM((8, channels), F32), bf16_image],
        limit=FORWARD_LIMIT,
        moved=24 * MEGA,
    )(
        place, *feature_pieces, lines, same, weight1, weight2, q_weight, k_weight, v_weight,
        o_weight,
    )
    act_two_got = exchange(act_two, "core")
    half = channels // 2
    halves = shape_of((4, channels, half), BF16)
    grad_half = shape_of((total, half), BF16)
    (linear_sent, linear_kept, small_three, d_resid, d_conv_two, d_sent_two) = kernel_call(
        attention_body,
        [halves, halves, stats_shape, image_f32, image, grad_half],
        [SMEM] + [VMEM] * 18,
        [bf16_image] * 5 + [pltpu.VMEM((total, total), BF16)],
        limit=ATTEND_LIMIT,
        moved=16 * MEGA,
    )(
        place, *cot_pieces, query, key, value, normed, residual, stats, weights, mixed, lines, same,
        o_weight, q_weight, k_weight, v_weight,
    )
    d_got_two = exchange(d_sent_two, "core")
    linear_got = exchange(linear_sent, "core")
    half_cat = pltpu.VMEM((total + 2 * across, 3 * half), BF16)

    def kernel_grad(made, *arrays):
        parts = []
        for kernel_rows, carries, _ in made:
            planes = 3 * len(kernel_rows) + 4 * carries
            parts += [shape_of((planes * half, half), BF16)] * 2
        return kernel_call(
            lambda *refs: kernel_grad_body(made, *refs), parts, [SMEM] + [VMEM] * len(arrays),
            [half_cat] * 2 + [pltpu.VMEM((channels, total), BF16)] * 2,
            limit=14, moved=8 * MEGA,
        )(place, *arrays)

    linear_part = shape_of((4 * half, half), BF16)

    def second_input_grad(grad):
        return kernel_call(
            lambda *refs: input_grad_body(False, 2, *refs),
            [image, grad_half, stats_shape, linear_part, linear_part],
            [SMEM] + [VMEM] * 8, [cat, f32_image],
            limit=16, moved=10 * MEGA,
        )(place, grad, weight2, conv_one, stats, lines, same, linear_kept, linear_got)

    def first_input_grad(grad):
        return kernel_call(
            lambda *refs: input_grad_body(True, 0, *refs),
            [four, four, shape_of((TAIL, half), BF16)],
            [SMEM] + [VMEM] * 9,
            [cat, f32_image, bf16_image, pltpu.VMEM((SMALL, channels), F32)],
            limit=16, moved=10 * MEGA,
        )(place, grad, weight1, image_in, stats, lines, same, d_resid, small_two, small_three)

    chains, groups, sums = {}, {}, {}

    def begin(letter, parts, made):
        for number, group in enumerate(made):
            name = letter + str(number)
            chains[name] = SumChain(*parts[2 * number : 2 * number + 2], group[2])
            groups[name] = group

    def end(name, token, sides):
        chain = chains[name]
        arrays = after([(chain.kept, chain.got)[side] for side in sides], token)
        sources = list(zip(arrays, sides))
        kernel_rows, carries, _ = groups[name]
        taps = 3 * len(kernel_rows)
        targets = {}
        if taps:
            targets[name[0]] = (sums.get(name[0]), 9, 3 * kernel_rows[0], 0, taps)
        for index in range(4 * carries):
            targets["linear" + str(index)] = (None, 1, 0, taps + index, 1)
        with_tail = chain.small is not None
        made = join_last(
            place, sources, list(targets.values()), sums.get(name + "tail"), with_tail
        )
        sums.update(zip(targets, made))
        if with_tail:
            sums["small" if name + "tail" in sums else name + "tail"] = made[-1]
        return made[0]

    token = small_three
    for event in " ".join(PLAN).split():
        if event == "W2":
            parts = kernel_grad(
                SECOND_GROUPS, act_two, act_two_got, after((d_conv_two,), token)[0], d_got_two
            )
            begin("B", parts, SECOND_GROUPS)
            token = parts[0]
            act_one_got = exchange(after((act_one,), token)[0], "core")
        elif event == "D2":
            d_conv_one, d_sent_one, small_two, *parts = second_input_grad(
                after((d_conv_two,), token)[0]
            )
            begin("L", parts, (((), True, LINEAR_ORDER),))
            d_got_one = exchange(d_sent_one, "core")
            token = small_two
        elif event == "W1":
            parts = kernel_grad(
                FIRST_GROUPS, act_one, act_one_got, after((d_conv_one,), token)[0], d_got_one
            )
            begin("C", parts, FIRST_GROUPS)
            token = parts[0]
        elif event == "D1":
            sent, kept, small = first_input_grad(after((d_conv_one,), token)[0])
            token = small
            chains["G"] = ReturnChain(sent, kept, features.shape)
            chains[RIDE].small = small
        elif event == "O!":
            chains["O"] = ReturnChain(*after((out_sent, out_kept), token), features.shape)
        elif event.endswith("<"):
            token = end(event[:-1], token, (0,))
        elif event.endswith(">"):
            token = end(event[:-1], token, (1,))
        elif event in groups and chains[event].at == 8:
            token = end(event, token, (0, 1))
        else:
            token = step(place, chains[event], token)

    output, features_grad = chains["O"].kept, chains["G"].kept
    small = sums["small"]
    linear_sum = [sums["linear" + str(index)].reshape(channels, channels) for index in range(4)]
    conv2_sum, conv1_sum = sums["B"], sums["C"]
    return (
        output,
        features_grad,
        small[0],
        small[1],
        conv1_sum.reshape(conv1_kernel.shape),
        small[4],
        small[2],
        small[3],
        conv2_sum.reshape(conv2_kernel.shape),
        small[10],
        small[5],
        small[6],
        linear_sum[0],
        small[7],
        linear_sum[1],
        linear_sum[2],
        small[8],
        linear_sum[3],
        small[9],
    )


def per_device(features, *rest):
    rows, imgs = lax.axis_size("rows"), lax.axis_size("imgs")
    if (rows, imgs) == (8, 4) and features.shape[1] == rows and features.shape[2] == ACROSS:
        return per_device_by_images(features, *rest)
    return per_device_by_rows(features, *rest)


def solution(mesh):
    placed = (
        P("rows", "imgs", None, None),
        P("rows", "imgs", None, None),
        P(),
        P(),
        P(),
        P(),
        P(),
        P(),
        P(),
        P(),
        P(),
        P(),
        P(),
        P(),
        P(),
        P(),
        P(),
        P(),
        P(),
    )
    return jax.shard_map(
        per_device,
        mesh=mesh,
        in_specs=placed,
        out_specs=(
            P("rows", "imgs", None, None),
            P("rows", "imgs", None, None),
            P(),
            P(),
            P(),
            P(),
            P(),
            P(),
            P(),
            P(),
            P(),
            P(),
            P(),
            P(),
            P(),
            P(),
            P(),
            P(),
            P(),
        ),
        check_vma=False,
    )
```
